32 devices in a mesh: dp: 2 (over x), row: 4 (over y, core), col: 4 (over z).
Axes of the slice: x: 2, y: 2, z: 4, core: 2. Of those that a mesh axis runs over, the one named last changes fastest.
Arguments:
- residual_in: float32 [12288, 1280], P(('dp', 'row'), 'col'), may hold values from -6 to 6
- seq_ids: int32 [12288], P('dp'), may hold values from 0 to 3, as said below
- norm1_gain: float32 [1280], P('col'), may hold values from 0.1 to 1.9
- w_qkv: float32 [1280, 3, 1280], P('row', None, 'col'), may hold values from -0.15625 to 0.15625
- per_dim: float32 [80], replicated, may hold values from 0 to 1.5
- w_out: float32 [1280, 1280], P('col', 'row'), may hold values from -1.25 to 1.25
- norm2_gain: float32 [1280], P('col'), may hold values from 0.1 to 1.9
- w_up: float32 [1280, 1280], P('row', 'col'), may hold values from -0.15625 to 0.15625
- w_down: float32 [1280, 1280], P('col', 'row'), may hold values from -0.15625 to 0.15625
- out_grad: float32 [12288, 1280], P(('dp', 'row'), 'col'), may hold values from -6 to 6
Outputs:
- output: float32 [12288, 1280], P(('dp', 'row'), 'col')
- input_grad: float32 [12288, 1280], P(('dp', 'row'), 'col')
- norm1_gain_grad: float32 [1280], P('col')
- w_qkv_grad: float32 [1280, 3, 1280], P('row', None, 'col')
- per_dim_grad: float32 [80], replicated
- w_out_grad: float32 [1280, 1280], P('col', 'row')
- norm2_gain_grad: float32 [1280], P('col')
- w_up_grad: float32 [1280, 1280], P('row', 'col')
- w_down_grad: float32 [1280, 1280], P('col', 'row')
The draws below stay inside these ranges and needn't reach their ends.
Inputs may be any that keep to these rules, and one draw needn't show every extreme that they name: seq_ids never fall; the 6144 tokens of one index g of dp hold exactly 2 sequences, numbered g * 2 to g * 2 + 1; each sequence starts at a multiple of 256 tokens within the group and has at least 768 tokens.
All inputs are finite; a program needn't handle non-finite values.
Results may differ from the reference program's by a relative error of at most 0.017.
The reference program's roundings to bfloat16 on the way count: a program that leaves them out, or rounds other values in their place, can miss the bound.
Values may be sent and summed in bfloat16 or wider, within the bound.
No kernel may reach another device: no remote copies, remote signals or barrier semaphores. Data moves between devices by JAX's collectives and lax.ppermute only.
A program may use at most 320 MiB of HBM per device.

```python
import math
import jax
import jax.numpy as jnp
from jax import lax

D = 1280
HEADS = 16
HD = 80
FF = 1280
SEQ_DP = 2
LEN = 3072
BLK = 256
TOKENS = 12288


def draw_seq_ids(key, part):
    group_size = SEQ_DP * LEN
    groups = TOKENS // group_size
    blocks = group_size // BLK
    least_blocks = LEN // (4 * BLK)
    spare_blocks = blocks - SEQ_DP * least_blocks
    cut_points = jnp.sort(jax.random.randint(key, (groups, SEQ_DP - 1), 0, spare_blocks + 1), axis=1).astype(jnp.int32)
    edge_points = jnp.concatenate([jnp.zeros((groups, 1), jnp.int32), cut_points], axis=1)
    starts = edge_points + least_blocks * jnp.arange(SEQ_DP, dtype=jnp.int32)[None, :]
    numbers = jnp.arange(blocks, dtype=jnp.int32)
    within = jnp.sum((numbers[None, :, None] >= starts[:, None, 1:]).astype(jnp.int32), axis=2)
    seq_numbers = within + SEQ_DP * jnp.arange(groups, dtype=jnp.int32)[:, None]
    return jnp.repeat(seq_numbers, BLK, axis=1).reshape(TOKENS).astype(jnp.int32)


def level_of(key, shape, split, low, high):
    level = 1.0
    for axis_at, blocks in split:
        heights = jax.random.uniform(jax.random.fold_in(jax.random.fold_in(key, 6), axis_at), (blocks,), jnp.float32, low / len(split), high / len(split))
        level = level * jnp.repeat(jnp.exp(heights), shape[axis_at] // blocks).reshape((-1,) + (1,) * (len(shape) - 1 - axis_at))
    return level


def scatter_about(stream_key, extent, width, most, pieces=(), kind=jnp.bfloat16):
    factor_of = level_of(stream_key, extent, pieces, -0.22, 0.18) if pieces else 1.0
    values = jax.random.normal(stream_key, extent, jnp.float32) * width * factor_of
    return jnp.minimum(jnp.maximum(values, -most), most).astype(kind)


def setup_inputs(seed: int = 0) -> dict:
    splits = jax.random.split(jax.random.key(seed), 11)
    return {
        "residual_in": scatter_about(splits[0], (TOKENS, D), 1.0, 6.0, ((0, 8), (1, 4)), jnp.float32),
        "seq_ids": draw_seq_ids(jax.random.fold_in(splits[10], 71), 0),
        "norm1_gain": jnp.clip(1.0 + 0.18 * jax.random.normal(splits[2], (D,), jnp.float32), 0.1, 1.9),
        "w_qkv": scatter_about(splits[3], (D, 3, D), D ** -0.5, 0.15625, ((0, 4), (2, 4)), jnp.float32),
        "per_dim": jnp.clip(jax.random.uniform(splits[4], (HD,), jnp.float32, 0.0, 1.5), 0.0, 1.5),
        "w_out": scatter_about(splits[5], (D, D), (D // 64) ** -0.5, 1.25, ((0, 4), (1, 4)), jnp.float32),
        "norm2_gain": jnp.clip(1.0 + 0.18 * jax.random.normal(splits[6], (D,), jnp.float32), 0.1, 1.9),
        "w_up": scatter_about(splits[7], (D, FF), D ** -0.5, 0.15625, ((0, 4), (1, 4)), jnp.float32),
        "w_down": scatter_about(splits[8], (FF, D), FF ** -0.5, 0.15625, ((0, 4), (1, 4)), jnp.float32),
        "out_grad": scatter_about(splits[9], (TOKENS, D), 1.0, 6.0, ((0, 8), (1, 4)), jnp.float32),
    }


@jax.custom_vjp
def low(v):
    return lax.optimization_barrier(v.astype(jnp.bfloat16)).astype(jnp.float32)

@jax.custom_vjp
def low_back(v):
    return v

def low_keep(v):
    return (low(v), None)

def low_pass(kept, grad):
    return (grad,)

def back_keep(v):
    return (v, None)

def back_low(kept, grad):
    return (low(grad),)
low.defvjp(low_keep, low_pass)
low_back.defvjp(back_keep, back_low)
epsilon = 1e-06
scale_base = 1.442695041
masked = -1e+30
highest = lax.Precision.HIGHEST

def matmul(left, right):
    return jnp.dot(left, right, precision=highest)

def normalize(values, norm_gain):
    inverse = lax.rsqrt(lax.optimization_barrier(jnp.mean(values * values, axis=1, keepdims=True)) + epsilon)
    return values * inverse * norm_gain

def split_heads(array_in, group_size):
    return array_in.reshape(group_size, HEADS, HD).transpose(1, 0, 2)

def attend(queries, keys, values, seq_ids):
    group_size = SEQ_DP * LEN
    groups = queries.shape[0] // group_size

    def one_group(operands):
        group_q, group_k, group_v, group_ids = operands
        blocks = jnp.arange(group_size) // BLK
        allowed = (group_ids[:, None] == group_ids[None, :]) & (blocks[None, :] <= blocks[:, None])

        def one_head(head_ops):
            head_q, head_k, head_v = head_ops
            scores = low_back(jnp.dot(head_q, head_k.T, precision=highest))
            scores = jnp.where(allowed, scores, masked)
            weights = jax.nn.softmax(scores, axis=-1)
            return jnp.dot(low(weights), head_v, precision=highest)
        outputs = lax.map(jax.checkpoint(one_head), (split_heads(group_q, group_size), split_heads(group_k, group_size), split_heads(group_v, group_size)))
        return outputs.transpose(1, 0, 2).reshape(group_size, HEADS * HD)

    def by_group(array_in):
        return array_in.reshape(groups, group_size, array_in.shape[-1])
    outputs = lax.map(jax.checkpoint(one_group), (by_group(queries), by_group(keys), by_group(values), seq_ids.reshape(groups, group_size)))
    return outputs.reshape(queries.shape[0], HEADS * HD)

def layer(residual_in, norm1_gain, w_qkv, per_dim, w_out, norm2_gain, w_up, w_down, seq_ids):
    normed_one = low(normalize(residual_in, norm1_gain))
    projected = jnp.einsum('rd,dtc->rtc', normed_one, low(w_qkv), precision=highest)
    scale = jax.nn.softplus(per_dim) * scale_base / math.sqrt(HD)
    queries = low(low_back(projected[:, 0]) * jnp.tile(scale, HEADS))
    keys = low(low_back(projected[:, 1]))
    values = low(low_back(projected[:, 2]))
    attended = low(low_back(attend(queries, keys, values, seq_ids)))
    middle = residual_in + low_back(matmul(attended, low(w_out)))
    normed_two = low(normalize(middle, norm2_gain))
    up_proj = low_back(matmul(normed_two, low(w_up)))
    activated = low(jax.nn.silu(up_proj))
    return middle + low_back(matmul(activated, low(w_down)))

def reference(residual_in, seq_ids, norm1_gain, w_qkv, per_dim, w_out, norm2_gain, w_up, w_down, out_grad):

    def forward(res, gain_one, qkv_weight, scale_param, out_weight, gain_two, up_weight, down_weight):
        return layer(res, gain_one, qkv_weight, scale_param, out_weight, gain_two, up_weight, down_weight, seq_ids)
    output, pull = jax.vjp(forward, residual_in, norm1_gain, w_qkv, per_dim, w_out, norm2_gain, w_up, w_down)
    grads = pull(out_grad)
    return (output, grads[0], grads[1], grads[2], grads[3], grads[4], grads[5], grads[6], grads[7])
```

```python
import functools
import math

import jax
import jax.numpy as jnp
from jax import lax
from jax.experimental import pallas as pl
from jax.experimental.pallas import tpu as pltpu
from jax.sharding import PartitionSpec as P

D = 1280
HD = 80
BLK = 256
LANES = 128

epsilon = 1e-06
scale_base = 1.442695041
excluded = -1e30

bf16 = jnp.bfloat16
f32 = jnp.float32


def dot(left, right):
    return jnp.dot(left, right, preferred_element_type=f32)


def product(form, left, right):
    return jnp.einsum(form, left, right, preferred_element_type=f32)


def three_terms(values):
    high = values.astype(bf16)
    rest = values - high.astype(f32)
    middle = rest.astype(bf16)
    return [high, middle, (rest - middle.astype(f32)).astype(bf16)]


def block_bias(starts_ref, first_block, width, block_count):
    shape = (block_count, width)
    block = lax.broadcasted_iota(jnp.int32, shape, 0)
    own = lax.broadcasted_iota(jnp.int32, shape, 1) // BLK
    start = jnp.zeros(shape, jnp.int32)
    for number in range(width // BLK):
        start = jnp.where(own == number, starts_ref[first_block + number], start)
    return jnp.where((block >= start) & (block <= first_block + own), 0.0, excluded).astype(bf16)


def extended(top, width, block_count, first_block, extra):
    row = lax.broadcasted_iota(jnp.int32, (LANES - HD, width), 0)
    block = first_block + lax.broadcasted_iota(jnp.int32, (LANES - HD, width), 1) // BLK
    marks = (row >= block_count) & (row < block_count + extra)
    if block_count:
        marks = marks | (row == block)
    return jnp.concatenate([top, jnp.where(marks, 1.0, 0.0).astype(bf16)], axis=0).T


def padded(parts, width):
    used = sum(part.shape[0] for part in parts)
    return jnp.concatenate(list(parts) + [jnp.zeros((LANES - used, width), bf16)], axis=0)


def forward_kernel(starts_ref, qkv_ref, out_ref, lse_ref, key_scr, *, tokens, part, tile):
    block_count = tokens // BLK
    per_part = part // tile
    per_tile = tile // BLK
    for number in range(tokens // tile):
        source, at = divmod(number, per_part)
        key_scr[number * tile : (number + 1) * tile, :] = extended(
            qkv_ref[source, HD : 2 * HD, at * tile : (at + 1) * tile],
            tile,
            block_count,
            number * per_tile,
            0,
        )

    def query_tile(number, carried):
        source = number // per_part
        at = pl.multiple_of((number % per_part) * tile, tile)
        bias = block_bias(starts_ref, number * per_tile, tile, block_count)
        query = padded([qkv_ref[source, 0:HD, pl.ds(at, tile)], bias], tile)

        def key_tile(key_number, state):
            largest, total, result = state
            keys = key_scr[pl.ds(pl.multiple_of(key_number * tile, tile), tile), :]
            scores = dot(keys, query)
            key_at = pl.multiple_of((key_number % per_part) * tile, tile)
            values = qkv_ref[key_number // per_part, 2 * HD : 3 * HD, pl.ds(key_at, tile)]
            newest = jnp.maximum(largest, jnp.max(scores, axis=0, keepdims=True))
            factor = jnp.exp(largest - newest)
            weights = jnp.exp(scores - newest)
            total = total * factor + jnp.sum(weights, axis=0, keepdims=True)
            result = result * factor + dot(values, weights.astype(bf16))
            return newest, total, result

        largest, total, result = lax.fori_loop(
            starts_ref[number * per_tile] // per_tile,
            number + 1,
            key_tile,
            (
                jnp.full((1, tile), -jnp.inf, f32),
                jnp.zeros((1, tile), f32),
                jnp.zeros((HD, tile), f32),
            ),
        )
        out_ref[source, :, pl.ds(at, tile)] = result / total
        lse_ref[source, :, pl.ds(at, tile)] = largest + jnp.log(total)
        return carried

    lax.fori_loop(0, tokens // tile, query_tile, 0)


def backward_kernel(
    starts_ref,
    scale_ref,
    qkv_ref,
    go_ref,
    out_ref,
    lse_ref,
    grad_ref,
    dim_ref,
    key_scr,
    value_scr,
    key_grad,
    value_grad,
    *,
    tokens,
    part,
    tile,
):
    block_count = tokens // BLK
    per_part = part // tile
    per_tile = tile // BLK
    for number in range(tokens // tile):
        source, at = divmod(number, per_part)
        columns = slice(at * tile, (at + 1) * tile)
        rows = slice(number * tile, (number + 1) * tile)
        key_scr[rows, :] = extended(
            qkv_ref[source, HD : 2 * HD, columns], tile, block_count, number * per_tile, 3
        )
        value_scr[rows, :] = extended(qkv_ref[source, 2 * HD : 3 * HD, columns], tile, 0, 0, 3)
    key_grad[...] = jnp.zeros_like(key_grad)
    value_grad[...] = jnp.zeros_like(value_grad)

    def query_tile(number, dim_total):
        source = number // per_part
        at = pl.multiple_of((number % per_part) * tile, tile)
        query_t = qkv_ref[source, 0:HD, pl.ds(at, tile)]
        go_t = go_ref[source, :, pl.ds(at, tile)]
        delta = jnp.sum(
            go_t.astype(f32) * out_ref[source, :, pl.ds(at, tile)], axis=0, keepdims=True
        )
        lse = lse_ref[source, :, pl.ds(at, tile)]
        bias = block_bias(starts_ref, number * per_tile, tile, block_count)
        query_ext = padded([query_t, bias] + three_terms(-lse), tile)
        go_ext = padded([go_t] + three_terms(-delta), tile)
        query = padded([query_t], tile).T
        go = padded([go_t], tile).T

        def key_tile(key_number, total):
            rows = pl.ds(pl.multiple_of(key_number * tile, tile), tile)
            key_at = pl.multiple_of((key_number % per_part) * tile, tile)
            keys_t = qkv_ref[key_number // per_part, HD : 2 * HD, pl.ds(key_at, tile)]
            weights = jnp.exp(dot(key_scr[rows, :], query_ext))
            slopes = (weights * dot(value_scr[rows, :], go_ext)).astype(bf16)
            value_grad[rows, :] += dot(weights.astype(bf16), go)
            key_grad[rows, :] += dot(slopes, query)
            return total + dot(keys_t, slopes)

        grad = lax.fori_loop(
            starts_ref[number * per_tile] // per_tile,
            number + 1,
            key_tile,
            jnp.zeros((HD, tile), f32),
        )
        grad_ref[source, 0:HD, pl.ds(at, tile)] = (grad * scale_ref[...]).astype(bf16)
        return dim_total + jnp.sum(grad * query_t.astype(f32), axis=1, keepdims=True)

    dim_ref[...] = lax.fori_loop(0, tokens // tile, query_tile, jnp.zeros((HD, 1), f32))
    for number in range(tokens // tile):
        source, at = divmod(number, per_part)
        columns = slice(at * tile, (at + 1) * tile)
        rows = slice(number * tile, (number + 1) * tile)
        grad_ref[source, HD : 2 * HD, columns] = key_grad[rows, :].T[:HD].astype(bf16)
        grad_ref[source, 2 * HD : 3 * HD, columns] = value_grad[rows, :].T[:HD].astype(bf16)


in_vmem = pl.BlockSpec(memory_space=pltpu.VMEM)
in_smem = pl.BlockSpec(memory_space=pltpu.SMEM)


def attend(starts, qkv, tile):
    parts, _, part = qkv.shape
    tokens = parts * part
    return pl.pallas_call(
        functools.partial(forward_kernel, tokens=tokens, part=part, tile=tile),
        out_shape=(
            jax.ShapeDtypeStruct((parts, HD, part), f32),
            jax.ShapeDtypeStruct((parts, 1, part), f32),
        ),
        in_specs=[in_smem, in_vmem],
        out_specs=(in_vmem, in_vmem),
        scratch_shapes=[pltpu.VMEM((tokens, LANES), bf16)],
        compiler_params=pltpu.CompilerParams(vmem_limit_bytes=50 << 20),
    )(starts, qkv)


def attend_back(starts, scale, qkv, go, out, lse, tile):
    parts, _, part = qkv.shape
    tokens = parts * part
    return pl.pallas_call(
        functools.partial(backward_kernel, tokens=tokens, part=part, tile=tile),
        out_shape=(
            jax.ShapeDtypeStruct((parts, 3 * HD, part), bf16),
            jax.ShapeDtypeStruct((HD, 1), f32),
        ),
        in_specs=[in_smem] + [in_vmem] * 5,
        out_specs=(in_vmem, in_vmem),
        scratch_shapes=[pltpu.VMEM((tokens, LANES), bf16)] * 2
        + [pltpu.VMEM((tokens, LANES), f32)] * 2,
        compiler_params=pltpu.CompilerParams(vmem_limit_bytes=58 << 20),
    )(starts, scale.reshape(HD, 1), qkv, go, out, lse)


def on_device(
    rows, cols, residual_in, seq_ids, norm1_gain, w_qkv, per_dim, w_out, norm2_gain, w_up, w_down, out_grad
):
    count, width = residual_in.shape
    heads = width // HD
    twins = rows // heads
    sub = count // cols
    share = w_qkv.shape[0]
    tile = 768 if count % 768 == 0 else BLK
    here = lax.axis_index("col")

    block_seq = seq_ids[::BLK]
    starts = jnp.sum((block_seq[None, :] < block_seq[:, None]).astype(jnp.int32), axis=1)

    qkv_local = w_qkv.astype(bf16).reshape(share, 3, heads, HD).transpose(0, 2, 1, 3)
    qkv_copy = lax.all_gather(
        qkv_local.reshape(share, heads * 3 * HD), "row", axis=0, tiled=True
    )
    stacked = jnp.stack([w_out.T, w_up, w_down.T], axis=0).astype(bf16)
    gathered = lax.all_gather(stacked, ("row", "col"), axis=0)
    gathered = (
        gathered.reshape(rows, cols, 3, share, width)
        .transpose(2, 0, 3, 1, 4)
        .reshape(3, rows * share, cols * width)
    )
    out_copy, up_copy, down_copy = gathered[0], gathered[1], gathered[2]
    gains = lax.all_gather(jnp.stack([norm1_gain, norm2_gain]), "col", axis=1, tiled=True)
    gain_one, gain_two = gains[0][:, None], gains[1][:, None]

    residual = residual_in.T
    totals = lax.psum(jnp.sum(residual * residual, axis=0), "col")
    inverse_one = lax.rsqrt(totals / D + epsilon)[None, :]
    normed = (residual * inverse_one * norm1_gain[:, None]).astype(bf16)
    normed_all = lax.all_gather(normed, "col", axis=0, tiled=True)
    projected = product("dj,dn->jn", qkv_copy, normed_all).reshape(heads, 3, HD, count)
    scale = jax.nn.softplus(per_dim) * scale_base / math.sqrt(HD)
    factors = jnp.stack([scale, jnp.ones_like(scale), jnp.ones_like(scale)])
    qkv = (projected * factors[None, :, :, None]).astype(bf16).reshape(heads, 3 * HD, count)
    qkv_heads = lax.all_to_all(jnp.repeat(qkv, twins, axis=0), "row", 0, 0, tiled=True)

    result, lse = attend(starts, qkv_heads, tile)
    leaving = result.astype(bf16).reshape(rows, HD, cols, sub).transpose(0, 2, 1, 3)
    arrived = lax.all_to_all(leaving.reshape(rows * cols, HD, sub), ("row", "col"), 0, 0, tiled=True)
    attended = (
        arrived.reshape(rows, cols, HD, sub)[::twins].transpose(1, 0, 2, 3).reshape(D, sub)
    )

    def spread(values):
        pieces = values.reshape(width, cols, sub).transpose(1, 0, 2)
        return lax.all_to_all(pieces, "col", 0, 0, tiled=True).reshape(cols * width, sub)

    def collect(values):
        pieces = lax.all_to_all(values.reshape(cols, width, sub), "col", 0, 0, tiled=True)
        return pieces.transpose(1, 0, 2).reshape(width, count)

    grad_mlp = spread(out_grad.T.astype(bf16))
    own_inverse = lax.dynamic_slice_in_dim(inverse_one, here * sub, sub, 1)
    own_normed = lax.dynamic_slice_in_dim(normed_all, here * sub, sub, 1)
    branch = product("dc,cn->dn", out_copy, attended)
    middle = own_normed.astype(f32) / (own_inverse * gain_one) + branch
    inverse_two = lax.rsqrt(jnp.sum(middle * middle, axis=0, keepdims=True) / D + epsilon)
    normed_two = (middle * inverse_two * gain_two).astype(bf16)
    up_proj = product("df,dn->fn", up_copy, normed_two)
    sigmoid_up = jax.nn.sigmoid(up_proj)
    activated = (up_proj * sigmoid_up).astype(bf16)
    change = branch + product("df,fn->dn", down_copy, activated)
    grad_act = product("df,dn->fn", down_copy, grad_mlp)
    grad_up = (grad_act * sigmoid_up * (1.0 + up_proj * (1.0 - sigmoid_up))).astype(bf16)
    grad_two = product("df,fn->dn", up_copy, grad_up)
    along = jnp.sum(gain_two * grad_two * middle, axis=0, keepdims=True)
    back_two = inverse_two * gain_two * grad_two - middle * inverse_two**3 * along / D
    gain_two_part = jnp.sum(grad_two * middle * inverse_two, axis=1)
    grad_branch = (grad_mlp.astype(f32) + back_two).astype(bf16)
    grad_attended = product("dc,dn->cn", out_copy, grad_branch).astype(bf16)

    leaving = grad_attended.reshape(cols, heads, HD, sub).transpose(1, 0, 2, 3)
    leaving = jnp.repeat(leaving, twins, axis=0).reshape(rows * cols, HD, sub)
    arrived = lax.all_to_all(leaving, ("row", "col"), 0, 0, tiled=True)
    go = arrived.reshape(rows, cols, HD, sub).transpose(0, 2, 1, 3).reshape(rows, HD, count)

    output = residual_in + collect(change.astype(bf16)).astype(f32).T
    back_two_here = collect(back_two.astype(bf16)).astype(f32)

    parts = jnp.stack(
        [
            product("dn,cn->dc", grad_branch, attended),
            product("dn,fn->df", normed_two, grad_up),
            product("dn,fn->df", grad_mlp, activated),
        ]
    ).astype(bf16)
    parts = parts.reshape(3, rows, share, cols, width).transpose(1, 3, 0, 2, 4)
    parts = parts.reshape(rows * cols * 3, share, width)
    shard = lax.psum_scatter(parts, ("row", "col"), scatter_dimension=0, tiled=True)
    shard = lax.psum(shard, "dp").astype(f32)

    grad_heads, dim_part = attend_back(starts, scale, qkv_heads, go, result, lse, tile)
    grad_projected = lax.all_to_all(grad_heads, "row", 0, 0, tiled=True)[::twins]

    grad_flat = grad_projected.reshape(heads * 3 * HD, count)
    grad_one_part = product("dj,jn->dn", qkv_copy, grad_flat)
    grad_one = lax.psum_scatter(
        grad_one_part.astype(bf16), "col", scatter_dimension=0, tiled=True
    ).astype(f32)
    qkv_part = product("dn,jn->dj", normed_all, grad_flat)
    own_head = (lax.axis_index("row") % twins == 0).astype(f32)
    gain_one_part = jnp.sum(qkv_part * qkv_copy.astype(f32), axis=1)
    small = jnp.concatenate([gain_one_part, gain_two_part, dim_part[:, 0] * own_head])
    small = lax.psum(small, ("dp", "row", "col"))
    gain_one_grad = lax.dynamic_slice_in_dim(small[:D], here * width, width) / norm1_gain
    gain_two_grad = lax.dynamic_slice_in_dim(small[D : 2 * D], here * width, width)
    scale_grad = small[2 * D :] / scale * (scale_base / math.sqrt(HD)) * jax.nn.sigmoid(per_dim)
    qkv_shard = lax.psum_scatter(qkv_part.astype(bf16), "row", scatter_dimension=0, tiled=True)
    qkv_grad = lax.psum(qkv_shard, "dp").astype(f32)
    qkv_grad = qkv_grad.reshape(share, heads, 3, HD).transpose(0, 2, 1, 3).reshape(share, 3, width)

    along_one = lax.psum(jnp.sum(normed_all.astype(f32) * grad_one_part, axis=0), "col")
    back_one = inverse_one * norm1_gain[:, None] * grad_one - residual * inverse_one**2 * (
        along_one / D
    )
    input_grad = out_grad + (back_two_here + back_one).T
    return (
        output,
        input_grad,
        gain_one_grad,
        qkv_grad,
        scale_grad,
        shard[0].T,
        gain_two_grad,
        shard[1],
        shard[2].T,
    )


def solution(mesh):
    in_specs = (
        P(("dp", "row"), "col"),
        P("dp"),
        P("col"),
        P("row", None, "col"),
        P(),
        P("col", "row"),
        P("col"),
        P("row", "col"),
        P("col", "row"),
        P(("dp", "row"), "col"),
    )
    out_specs = (
        P(("dp", "row"), "col"),
        P(("dp", "row"), "col"),
        P("col"),
        P("row", None, "col"),
        P(),
        P("col", "row"),
        P("col"),
        P("row", "col"),
        P("col", "row"),
    )
    return jax.shard_map(
        functools.partial(on_device, mesh.shape["row"], mesh.shape["col"]),
        mesh=mesh,
        in_specs=in_specs,
        out_specs=out_specs,
        check_vma=False,
    )
```

```python
import functools
import math

import jax
import jax.numpy as jnp
from jax import lax
from jax.experimental import pallas as pl
from jax.experimental.pallas import tpu as pltpu
from jax.sharding import PartitionSpec as P

D = 1280
HD = 80
BLK = 256
LANES = 128

epsilon = 1e-06
scale_base = 1.442695041
excluded = -1e30

bf16 = jnp.bfloat16
f32 = jnp.float32


def dot(left, right):
    return jnp.dot(left, right, preferred_element_type=f32)


def product(form, left, right):
    return jnp.einsum(form, left, right, preferred_element_type=f32)


def three_terms(values):
    high = values.astype(bf16)
    rest = values - high.astype(f32)
    middle = rest.astype(bf16)
    return [high, middle, (rest - middle.astype(f32)).astype(bf16)]


def block_bias(starts_ref, first_block, width, block_count):
    shape = (block_count, width)
    block = lax.broadcasted_iota(jnp.int32, shape, 0)
    own = lax.broadcasted_iota(jnp.int32, shape, 1) // BLK
    start = jnp.zeros(shape, jnp.int32)
    for number in range(width // BLK):
        start = jnp.where(own == number, starts_ref[first_block + number], start)
    return jnp.where((block >= start) & (block <= first_block + own), 0.0, excluded).astype(bf16)


def extended(top, width, block_count, first_block, extra):
    row = lax.broadcasted_iota(jnp.int32, (LANES - HD, width), 0)
    block = first_block + lax.broadcasted_iota(jnp.int32, (LANES - HD, width), 1) // BLK
    marks = (row >= block_count) & (row < block_count + extra)
    if block_count:
        marks = marks | (row == block)
    return jnp.concatenate([top, jnp.where(marks, 1.0, 0.0).astype(bf16)], axis=0).T


def padded(parts, width):
    used = sum(part.shape[0] for part in parts)
    return jnp.concatenate(list(parts) + [jnp.zeros((LANES - used, width), bf16)], axis=0)


def forward_kernel(starts_ref, place_ref, *refs, tokens, part, tile, rows):
    pieces = refs[: -4]
    out_ref, lse_ref, qkv_ref, key_scr = refs[-4:]
    half = pieces[0].shape[1]
    for number, piece in enumerate(pieces):
        flip, at = number % rows, number // rows
        qkv_ref[jnp.bitwise_xor(place_ref[0], flip), :, at * half : (at + 1) * half] = piece[...]
    block_count = tokens // BLK
    per_part = part // tile
    per_tile = tile // BLK
    for number in range(tokens // tile):
        source, at = divmod(number, per_part)
        key_scr[number * tile : (number + 1) * tile, :] = extended(
            qkv_ref[source, HD : 2 * HD, at * tile : (at + 1) * tile],
            tile,
            block_count,
            number * per_tile,
            0,
        )

    def query_tile(number, carried):
        source = number // per_part
        at = pl.multiple_of((number % per_part) * tile, tile)
        bias = block_bias(starts_ref, number * per_tile, tile, block_count)
        query = padded([qkv_ref[source, 0:HD, pl.ds(at, tile)], bias], tile)

        def key_tile(key_number, state):
            largest, total, result = state
            keys = key_scr[pl.ds(pl.multiple_of(key_number * tile, tile), tile), :]
            scores = dot(keys, query)
            key_at = pl.multiple_of((key_number % per_part) * tile, tile)
            values = qkv_ref[key_number // per_part, 2 * HD : 3 * HD, pl.ds(key_at, tile)]
            newest = jnp.maximum(largest, jnp.max(scores, axis=0, keepdims=True))
            factor = jnp.exp(largest - newest)
            weights = jnp.exp(scores - newest)
            total = total * factor + jnp.sum(weights, axis=0, keepdims=True)
            result = result * factor + dot(values, weights.astype(bf16))
            return newest, total, result

        largest, total, result = lax.fori_loop(
            starts_ref[number * per_tile] // per_tile,
            number + 1,
            key_tile,
            (
                jnp.full((1, tile), -jnp.inf, f32),
                jnp.zeros((1, tile), f32),
                jnp.zeros((HD, tile), f32),
            ),
        )
        out_ref[source, :, pl.ds(at, tile)] = result / total
        lse_ref[source, :, pl.ds(at, tile)] = largest + jnp.log(total)
        return carried

    lax.fori_loop(0, tokens // tile, query_tile, 0)


def backward_kernel(
    starts_ref,
    place_ref,
    scale_ref,
    qkv_ref,
    go_ref,
    out_ref,
    lse_ref,
    *refs,
    tokens,
    part,
    tile,
    rows,
):
    pieces = refs[: -6]
    dim_ref, grad_ref, key_scr, value_scr, key_grad, value_grad = refs[-6:]
    block_count = tokens // BLK
    per_part = part // tile
    per_tile = tile // BLK
    for number in range(tokens // tile):
        source, at = divmod(number, per_part)
        columns = slice(at * tile, (at + 1) * tile)
        band = slice(number * tile, (number + 1) * tile)
        key_scr[band, :] = extended(
            qkv_ref[source, HD : 2 * HD, columns], tile, block_count, number * per_tile, 3
        )
        value_scr[band, :] = extended(qkv_ref[source, 2 * HD : 3 * HD, columns], tile, 0, 0, 3)
    key_grad[...] = jnp.zeros_like(key_grad)
    value_grad[...] = jnp.zeros_like(value_grad)

    def query_tile(number, dim_total):
        source = number // per_part
        at = pl.multiple_of((number % per_part) * tile, tile)
        query_t = qkv_ref[source, 0:HD, pl.ds(at, tile)]
        go_t = go_ref[source, :, pl.ds(at, tile)]
        delta = jnp.sum(
            go_t.astype(f32) * out_ref[source, :, pl.ds(at, tile)], axis=0, keepdims=True
        )
        lse = lse_ref[source, :, pl.ds(at, tile)]
        bias = block_bias(starts_ref, number * per_tile, tile, block_count)
        query_ext = padded([query_t, bias] + three_terms(-lse), tile)
        go_ext = padded([go_t] + three_terms(-delta), tile)
        query = padded([query_t], tile).T
        go = padded([go_t], tile).T

        def key_tile(key_number, total):
            band = pl.ds(pl.multiple_of(key_number * tile, tile), tile)
            key_at = pl.multiple_of((key_number % per_part) * tile, tile)
            keys_t = qkv_ref[key_number // per_part, HD : 2 * HD, pl.ds(key_at, tile)]
            weights = jnp.exp(dot(key_scr[band, :], query_ext))
            slopes = (weights * dot(value_scr[band, :], go_ext)).astype(bf16)
            value_grad[band, :] += dot(weights.astype(bf16), go)
            key_grad[band, :] += dot(slopes, query)
            return total + dot(keys_t, slopes)

        grad = lax.fori_loop(
            starts_ref[number * per_tile] // per_tile,
            number + 1,
            key_tile,
            jnp.zeros((HD, tile), f32),
        )
        grad_ref[source, 0:HD, pl.ds(at, tile)] = (grad * scale_ref[...]).astype(bf16)
        return dim_total + jnp.sum(grad * query_t.astype(f32), axis=1, keepdims=True)

    dim_ref[...] = lax.fori_loop(0, tokens // tile, query_tile, jnp.zeros((HD, 1), f32))
    for number in range(tokens // tile):
        source, at = divmod(number, per_part)
        columns = slice(at * tile, (at + 1) * tile)
        band = slice(number * tile, (number + 1) * tile)
        grad_ref[source, HD : 2 * HD, columns] = key_grad[band, :].T[:HD].astype(bf16)
        grad_ref[source, 2 * HD : 3 * HD, columns] = value_grad[band, :].T[:HD].astype(bf16)
    half = pieces[0].shape[1]
    for number, piece in enumerate(pieces):
        flip, at = number % rows, number // rows
        piece[...] = grad_ref[
            jnp.bitwise_xor(place_ref[0], flip), :, at * half : (at + 1) * half
        ]


in_vmem = pl.BlockSpec(memory_space=pltpu.VMEM)
in_smem = pl.BlockSpec(memory_space=pltpu.SMEM)


def attend(starts, place, pieces, rows, part, tile):
    tokens = rows * part
    return pl.pallas_call(
        functools.partial(forward_kernel, tokens=tokens, part=part, tile=tile, rows=rows),
        out_shape=(
            jax.ShapeDtypeStruct((rows, HD, part), f32),
            jax.ShapeDtypeStruct((rows, 1, part), f32),
            jax.ShapeDtypeStruct((rows, 3 * HD, part), bf16),
        ),
        in_specs=[in_smem] * 2 + [in_vmem] * len(pieces),
        out_specs=(in_vmem,) * 3,
        scratch_shapes=[pltpu.VMEM((tokens, LANES), bf16)],
        compiler_params=pltpu.CompilerParams(vmem_limit_bytes=60 << 20),
        cost_estimate=pl.CostEstimate(
            flops=3 * LANES * tokens * tokens,
            bytes_accessed=12 << 20,
            transcendentals=tokens * tokens // 3,
        ),
    )(starts, place, *pieces)


def attend_back(starts, place, scale, qkv, go, out, lse, tile, half):
    rows, _, part = qkv.shape
    tokens = rows * part
    count = rows * (part // half)
    results = pl.pallas_call(
        functools.partial(backward_kernel, tokens=tokens, part=part, tile=tile, rows=rows),
        out_shape=(jax.ShapeDtypeStruct((3 * HD, half), bf16),) * count
        + (jax.ShapeDtypeStruct((HD, 1), f32),),
        in_specs=[in_smem] * 2 + [in_vmem] * 5,
        out_specs=(in_vmem,) * (count + 1),
        scratch_shapes=[pltpu.VMEM((rows, 3 * HD, part), bf16)]
        + [pltpu.VMEM((tokens, LANES), bf16)] * 2
        + [pltpu.VMEM((tokens, LANES), f32)] * 2,
        compiler_params=pltpu.CompilerParams(vmem_limit_bytes=60 << 20),
        cost_estimate=pl.CostEstimate(
            flops=8 * LANES * tokens * tokens,
            bytes_accessed=16 << 20,
            transcendentals=tokens * tokens // 3,
        ),
    )(starts, place, scale.reshape(HD, 1), qkv, go, out, lse)
    return results[:-1], results[-1]


def assemble_kernel(place_ref, group_ref, *refs, cols, splits):
    blocks, out_ref = refs[:-1], refs[-1]
    part = out_ref.shape[1] // len(blocks)
    width = out_ref.shape[2] // cols
    for number, block in enumerate(blocks):
        row = jnp.bitwise_xor(place_ref[0], number // splits)
        piece = jnp.bitwise_xor(group_ref[0], number % splits)
        band = pl.ds(pl.multiple_of((row * splits + piece) * part, 16), part)
        for col in range(cols):
            value = block[col, 0:part, :]
            for matrix in range(3):
                out_ref[matrix, band, col * width : (col + 1) * width] = value[
                    :, matrix * width : (matrix + 1) * width
                ]


def feed_kernel(
    here_ref,
    att_ref,
    normed_ref,
    inverse_ref,
    gains_ref,
    w_ref,
    *refs,
    rows,
    cols,
    heads,
    twins,
):
    go_pieces, change_pieces = refs[:cols], refs[cols : 2 * cols]
    (
        back_ref,
        gain_ref,
        leave_ref,
        go_ref,
        attended,
        normed_two,
        act_ref,
        grad_up_ref,
        branch_grad,
        branch,
        middle,
        grad_two,
        flipped,
        flipped_go,
        grad_att,
        change_ref,
    ) = refs[2 * cols :]
    width, sub = go_pieces[0].shape

    def ring(shift):
        return pl.ds(pl.multiple_of(lax.rem(here_ref[0] + shift, cols) * width, 16), width)

    for number, piece in enumerate(go_pieces):
        go_ref[ring(cols - number), :] = piece[...]
    step = 256
    for col in range(cols):
        for head in range(heads):
            at = (col * heads + head) * HD
            attended[at : at + HD, :] = att_ref[head * twins * cols + col]
    inverse = inverse_ref[...]

    def part(number):
        return pl.ds(pl.multiple_of(number * step, step), step)

    def first(number, total):
        at = part(number)
        here = dot(w_ref[0, at, :], attended[...])
        branch[at, :] = here
        mid = normed_ref[at, :].astype(f32) / (inverse * gains_ref[at, 0:1]) + here
        middle[at, :] = mid
        flipped_go[:, at] = go_ref[at, :].T
        return total + jnp.sum(mid * mid, axis=0, keepdims=True)

    steps = D // step
    total = lax.fori_loop(0, steps, first, jnp.zeros((1, sub), f32))
    inverse_two = lax.rsqrt(total / D + epsilon)

    def second(number, carried):
        at = part(number)
        value = (middle[at, :] * inverse_two * gains_ref[at, 1:2]).astype(bf16)
        normed_two[at, :] = value
        flipped[:, at] = value.T
        return carried

    lax.fori_loop(0, steps, second, 0)

    def third(number, carried):
        at = part(number)
        up_proj = dot(flipped[...], w_ref[1, :, at])
        sigmoid_up = jax.nn.sigmoid(up_proj)
        act_ref[:, at] = (up_proj * sigmoid_up).astype(bf16)
        grad_act = dot(flipped_go[...], w_ref[2, :, at])
        grad_up_ref[:, at] = (
            grad_act * sigmoid_up * (1.0 + up_proj * (1.0 - sigmoid_up))
        ).astype(bf16)
        return carried

    lax.fori_loop(0, steps, third, 0)

    def fourth(number, along):
        at = part(number)
        change_ref[at, :] = (branch[at, :] + dot_last(w_ref[2, at, :], act_ref[...])).astype(bf16)
        grad = dot_last(w_ref[1, at, :], grad_up_ref[...])
        grad_two[at, :] = grad
        return along + jnp.sum(gains_ref[at, 1:2] * grad * middle[at, :], axis=0, keepdims=True)

    along = lax.fori_loop(0, steps, fourth, jnp.zeros((1, sub), f32))
    shrink = inverse_two * inverse_two * inverse_two * along / D

    def fifth(number, carried):
        at = part(number)
        grad = grad_two[at, :]
        mid = middle[at, :]
        back = inverse_two * gains_ref[at, 1:2] * grad - mid * shrink
        back_ref[at, :] = back / (inverse * gains_ref[at, 0:1])
        gain_ref[at, :] = jnp.sum(grad * mid * inverse_two, axis=1, keepdims=True)
        value = (go_ref[at, :].astype(f32) + back).astype(bf16)
        branch_grad[at, :] = value
        flipped[:, at] = value.T
        return carried

    lax.fori_loop(0, steps, fifth, 0)

    def sixth(number, carried):
        at = part(number)
        grad_att[at, :] = dot(flipped[...], w_ref[0, :, at]).T.astype(bf16)
        return carried

    lax.fori_loop(0, steps, sixth, 0)
    for number, piece in enumerate(change_pieces):
        piece[...] = change_ref[ring(number), :]
    for row in range(rows):
        for col in range(cols):
            at = (col * heads + row // twins) * HD
            leave_ref[row * cols + col] = grad_att[at : at + HD, :]


def dot_last(left, right):
    return lax.dot_general(left, right, (((1,), (1,)), ((), ())), preferred_element_type=f32)


def weights_kernel(
    place_ref, branch_grad, attended, normed_two, grad_up, go, act, *outs, cols, order
):
    share, wide = outs[0].shape[-2:]
    width = wide // 3
    for slot, (out, at) in enumerate(order):
        row = jnp.bitwise_xor(place_ref[0], slot)
        band = pl.ds(pl.multiple_of(row * share, 16), share)
        for number, value in enumerate(
            (
                dot_last(branch_grad[band, :], attended[...]),
                dot(normed_two[band, :], grad_up[...]),
                dot(go[band, :], act[...]),
            )
        ):
            value = value.astype(bf16)
            for col in range(cols):
                outs[out][col, at, :, number * width : (number + 1) * width] = value[
                    :, col * width : (col + 1) * width
                ]


def assemble(place, group, blocks, splits):
    cols = blocks[0].shape[0]
    return pl.pallas_call(
        functools.partial(assemble_kernel, cols=cols, splits=splits),
        out_shape=jax.ShapeDtypeStruct((3, D, D), bf16),
        in_specs=[in_smem] * 2 + [in_vmem] * len(blocks),
        out_specs=in_vmem,
        compiler_params=pltpu.CompilerParams(vmem_limit_bytes=60 << 20),
        cost_estimate=pl.CostEstimate(flops=0, bytes_accessed=20 << 20, transcendentals=0),
    )(place, group, *blocks)


def feed_forward(here, attended, pieces, normed, inverse, gains, weights, rows, cols, heads, twins):
    width, sub = pieces[0].shape
    flat = jax.ShapeDtypeStruct((D, sub), bf16)
    turned = jax.ShapeDtypeStruct((sub, D), bf16)
    results = pl.pallas_call(
        functools.partial(feed_kernel, rows=rows, cols=cols, heads=heads, twins=twins),
        out_shape=(jax.ShapeDtypeStruct((width, sub), bf16),) * cols
        + (
            jax.ShapeDtypeStruct((D, sub), f32),
            jax.ShapeDtypeStruct((D, 1), f32),
            jax.ShapeDtypeStruct((rows * cols, HD, sub), bf16),
            flat,
            flat,
            flat,
            turned,
            turned,
            flat,
        ),
        in_specs=[in_smem] + [in_vmem] * (5 + cols),
        out_specs=(in_vmem,) * (cols + 9),
        scratch_shapes=[pltpu.VMEM((D, sub), f32)] * 3
        + [pltpu.VMEM((sub, D), bf16)] * 2
        + [pltpu.VMEM((D, sub), bf16)] * 2,
        compiler_params=pltpu.CompilerParams(vmem_limit_bytes=60 << 20),
        cost_estimate=pl.CostEstimate(
            flops=12 * D * D * sub, bytes_accessed=20 << 20, transcendentals=D * sub
        ),
    )(here, attended, normed, inverse, gains, weights, *pieces)
    return results[:cols], results[cols:]


def weight_grads(place, branch_grad, attended, normed_two, grad_up, go, act, shapes, order):
    cols = shapes[0][0]
    sub = go.shape[1]
    return pl.pallas_call(
        functools.partial(weights_kernel, cols=cols, order=order),
        out_shape=tuple(jax.ShapeDtypeStruct(shape, bf16) for shape in shapes),
        in_specs=[in_smem] + [in_vmem] * 6,
        out_specs=(in_vmem,) * len(shapes),
        compiler_params=pltpu.CompilerParams(vmem_limit_bytes=60 << 20),
        cost_estimate=pl.CostEstimate(
            flops=6 * D * D * sub, bytes_accessed=16 << 20, transcendentals=0
        ),
    )(place, branch_grad, attended, normed_two, grad_up, go, act)


def copies_kernel(place_ref, *refs):
    blocks, (whole, turned) = refs[:-2], refs[-2:]
    share = blocks[0].shape[0]
    for flip, block in enumerate(blocks):
        row = jnp.bitwise_xor(place_ref[0], flip)
        whole[pl.ds(pl.multiple_of(row * share, 16), share), :] = block[...]
    for number in range(D // LANES):
        at = slice(number * LANES, (number + 1) * LANES)
        turned[:, at] = whole[at, :].T


def projection_copies(place, blocks):
    share, wide = blocks[0].shape
    return pl.pallas_call(
        copies_kernel,
        out_shape=(
            jax.ShapeDtypeStruct((D, wide), bf16),
            jax.ShapeDtypeStruct((wide, D), bf16),
        ),
        in_specs=[in_smem] + [in_vmem] * len(blocks),
        out_specs=(in_vmem,) * 2,
        compiler_params=pltpu.CompilerParams(vmem_limit_bytes=60 << 20),
        cost_estimate=pl.CostEstimate(flops=0, bytes_accessed=8 << 20, transcendentals=0),
    )(place, *blocks)


def project_kernel(here_ref, place_ref, turned_ref, factor_ref, *refs, rows, cols, heads):
    own, right, left = refs[0], refs[1:cols], refs[cols : 2 * cols - 1]
    outs, normed, result = refs[2 * cols - 1 : -2], refs[-2], refs[-1]
    width = own.shape[0]
    here = here_ref[0]

    def block(number):
        return pl.ds(pl.multiple_of(number * width, 16), width)

    normed[block(here), :] = own[...]
    for step in range(1, cols):

        @pl.when(here >= step)
        def _():
            normed[block(here - step), :] = right[step - 1][...]

        @pl.when(here + step < cols)
        def _():
            normed[block(here + step), :] = left[step - 1][...]

    for head in range(heads):
        at = slice(head * 3 * HD, (head + 1) * 3 * HD)
        value = dot(turned_ref[at, :], normed[...]) * factor_ref[at, :]
        result[head] = value.astype(bf16)
    for flip, out in enumerate(outs):
        out[...] = result[jnp.bitwise_xor(place_ref[0], flip) // (rows // heads)]


def project(here, place, turned, factors, pieces, rows, cols, heads):
    width, half = pieces[0].shape
    results = pl.pallas_call(
        functools.partial(project_kernel, rows=rows, cols=cols, heads=heads),
        out_shape=(jax.ShapeDtypeStruct((3 * HD, half), bf16),) * rows
        + (jax.ShapeDtypeStruct((D, half), bf16),),
        in_specs=[in_smem] * 2 + [in_vmem] * (2 + len(pieces)),
        out_specs=(in_vmem,) * (rows + 1),
        scratch_shapes=[pltpu.VMEM((heads, 3 * HD, half), bf16)],
        compiler_params=pltpu.CompilerParams(vmem_limit_bytes=60 << 20),
        cost_estimate=pl.CostEstimate(
            flops=2 * D * 3 * width * half, bytes_accessed=10 << 20, transcendentals=0
        ),
    )(here, place, turned, factors, *pieces)
    return results[:-1], results[-1]


def back_kernel(
    here_ref, place_ref, whole_ref, normed_ref, back_ref, *refs, rows, cols, heads, first
):
    pieces, (own, right, left) = refs[:rows], (refs[rows], refs[rows + 1 : rows + cols], refs[rows + cols : -2])
    grads, payload = refs[-2], refs[-1]
    half = normed_ref.shape[1]
    width = D // cols
    sub = back_ref.shape[1]
    here = here_ref[0]
    for flip, piece in enumerate(pieces):
        head = jnp.bitwise_xor(place_ref[0], flip) // (rows // heads)
        grads[pl.ds(pl.multiple_of(head * 3 * HD, 16), 3 * HD), :] = piece[...]
    along = jnp.zeros((1, half), f32)
    for col in range(cols):
        at = slice(col * width, (col + 1) * width)
        value = dot(whole_ref[at, :], grads[...])
        along += jnp.sum(value * normed_ref[at, :].astype(f32), axis=0, keepdims=True)
        payload[col, 0:width, :] = value.astype(bf16)
        for number in range(half // sub):

            @pl.when(here == first + number)
            def _():
                columns = slice(number * sub, (number + 1) * sub)
                payload[col, 0:width, columns] = (value[:, columns] + back_ref[at, :]).astype(bf16)

    tail = jnp.concatenate([along, jnp.zeros((15, half), f32)], axis=0).astype(bf16)
    for col in range(cols):
        payload[col, width : width + 16, :] = tail
    own[...] = payload[here]
    for step in range(1, cols):

        @pl.when(here + step < cols)
        def _():
            right[step - 1][...] = payload[here + step]

        @pl.when(here >= step)
        def _():
            left[step - 1][...] = payload[here - step]


def project_back(here, place, whole, normed, back, pieces, rows, cols, heads, first):
    half = normed.shape[1]
    width = D // cols
    block = jax.ShapeDtypeStruct((width + 16, half), bf16)
    results = pl.pallas_call(
        functools.partial(
            back_kernel, rows=rows, cols=cols, heads=heads, first=first
        ),
        out_shape=(block,) * (2 * cols - 1) + (jax.ShapeDtypeStruct((3 * width, half), bf16),),
        in_specs=[in_smem] * 2 + [in_vmem] * (3 + rows),
        out_specs=(in_vmem,) * (2 * cols),
        scratch_shapes=[pltpu.VMEM((cols, width + 16, half), bf16)],
        compiler_params=pltpu.CompilerParams(vmem_limit_bytes=60 << 20),
        cost_estimate=pl.CostEstimate(
            flops=2 * D * 3 * width * half, bytes_accessed=12 << 20, transcendentals=0
        ),
    )(here, place, whole, normed, back, *pieces)
    return results[0], results[1:cols], results[cols:-1], results[-1]


def projection_grads_kernel(place_ref, whole_ref, *refs, order):
    outs, gain_ref = refs[-1 - (max(out for out, _ in order) + 1) : -1], refs[-1]
    pairs = refs[: len(refs) - 1 - len(outs)]
    share = outs[0].shape[1]
    for slot, (out, at) in enumerate(order):
        row = jnp.bitwise_xor(place_ref[0], slot)
        band = pl.ds(pl.multiple_of(row * share, 16), share)
        value = sum(
            dot_last(pairs[2 * number][band, :], pairs[2 * number + 1][...])
            for number in range(len(pairs) // 2)
        )
        gain_ref[band, :] = jnp.sum(value * whole_ref[band, :].astype(f32), axis=1, keepdims=True)
        outs[out][at] = value.astype(bf16)


def projection_grads(place, whole, pairs, shapes, order):
    flops = 2 * D * whole.shape[1] * sum(pair.shape[1] for pair in pairs[::2])
    return pl.pallas_call(
        functools.partial(projection_grads_kernel, order=order),
        out_shape=tuple(jax.ShapeDtypeStruct(shape, bf16) for shape in shapes)
        + (jax.ShapeDtypeStruct((D, 1), f32),),
        in_specs=[in_smem] + [in_vmem] * (1 + len(pairs)),
        out_specs=(in_vmem,) * (len(shapes) + 1),
        compiler_params=pltpu.CompilerParams(vmem_limit_bytes=60 << 20),
        cost_estimate=pl.CostEstimate(flops=flops, bytes_accessed=12 << 20, transcendentals=0),
    )(place, whole, *pairs)


def after(values, *others):
    return lax.optimization_barrier((values,) + others)[0]


def partner(values, flip, size, axis="row"):
    return lax.ppermute(values, axis, [(at, at ^ flip) for at in range(size)])


def swapped(pieces, rows):
    return [pieces[0]] + [partner(pieces[flip], flip, rows) for flip in range(1, rows)]


def spread_rows(values, rows):
    if rows != 4:
        return swapped([values] * rows, rows)
    far = partner(values, 2, rows)
    return [values, partner(values, 1, rows), far, partner(far, 1, rows)]


class LineScatter:
    def __init__(self, own, right, left, cols):
        self.own, self.right, self.left, self.cols = own, right, left, cols
        self.moving = [right[-1], left[-1]]
        self.left_steps = cols - 1

    def step(self, *ties):
        step, cols = self.left_steps, self.cols
        to_right, to_left = (after(value, *ties) if ties else value for value in self.moving)
        from_left = lax.ppermute(to_right, "col", [(at, at + 1) for at in range(cols - step)])
        from_right = lax.ppermute(to_left, "col", [(at, at - 1) for at in range(step, cols)])
        if step > 1:
            self.moving = [
                add(self.right[step - 2], from_left).astype(bf16),
                add(self.left[step - 2], from_right).astype(bf16),
            ]
        else:
            self.total = self.own.astype(f32) + add(from_left, from_right)
        self.left_steps -= 1
        return from_left


def add(left, right):
    return left.astype(f32) + right.astype(f32)


def total(values, axes):
    for axis, size in axes:
        flip = 1
        while flip < size:
            values = values + partner(values, flip, size, axis)
            flip *= 2
    return values


def sum_groups(values, groups):
    if groups == 2:
        return add(values, partner(values, 1, 2, "dp"))
    return lax.psum(values, "dp").astype(f32)


def line_gather(piece, cols):
    right, left = [], []
    to_right = to_left = piece
    for step in range(1, cols):
        to_right = lax.ppermute(to_right, "col", [(at, at + 1) for at in range(step - 1, cols - 1)])
        to_left = lax.ppermute(to_left, "col", [(at, at - 1) for at in range(1, cols - step + 1)])
        right.append(to_right)
        left.append(to_left)
    return [piece] + right + left


def ring_swap(pieces, cols):
    return [pieces[0]] + [
        lax.ppermute(pieces[shift], "col", [(at, (at + shift) % cols) for at in range(cols)])
        for shift in range(1, cols)
    ]


def on_device(
    groups, rows, cols, residual_in, seq_ids, norm1_gain, w_qkv, per_dim, w_out, norm2_gain, w_up, w_down, out_grad
):
    count, width = residual_in.shape
    heads = width // HD
    twins = rows // heads
    sub = count // cols
    half = count // 2
    share = w_qkv.shape[0]
    tile = 768 if count % 768 == 0 else BLK
    here = lax.axis_index("col")
    place = lax.axis_index("row")
    here_of, place_of = here[None].astype(jnp.int32), place[None].astype(jnp.int32)

    block_seq = seq_ids[::BLK]
    starts = jnp.sum((block_seq[None, :] < block_seq[:, None]).astype(jnp.int32), axis=1)

    residual = residual_in.T
    squares = jnp.sum(residual * residual, axis=0)
    squares = squares + partner(squares, 1, cols, "col")
    inverse_one = lax.rsqrt((squares + partner(squares, 2, cols, "col")) / D + epsilon)[None, :]
    normed = (residual * inverse_one * norm1_gain[:, None]).astype(bf16)

    stacked = jnp.concatenate(
        [w_out.T, w_up, w_down.T], axis=1
    ).astype(bf16)
    gains = [jnp.concatenate(three_terms(gain))[None] for gain in (norm1_gain, norm2_gain)]
    splits = 2 if groups == 2 and rows == 4 else 1
    part = share // splits
    group_of = jnp.zeros((1,), jnp.int32)
    if splits == 2:
        group = lax.axis_index("dp")
        group_of = group[None].astype(jnp.int32)
        stacked = lax.dynamic_slice_in_dim(stacked, group * part, part, 0)
    stacked = jnp.concatenate([stacked] + gains + [jnp.zeros((14, 3 * width), bf16)], axis=0)
    gathered = lax.all_gather(stacked, "col", axis=0)
    gains = gathered[:, part : part + 2].astype(f32).reshape(cols, 2, 3, width).sum(axis=2)
    gains = gains.transpose(0, 2, 1).reshape(D, 2)

    qkv_local = w_qkv.astype(bf16).reshape(share, 3, heads, HD).transpose(0, 2, 1, 3)
    qkv_local = qkv_local.reshape(share, heads * 3 * HD)
    whole, turned = projection_copies(place_of, spread_rows(qkv_local, rows))
    scale = jax.nn.softplus(per_dim) * scale_base / math.sqrt(HD)
    factors = jnp.tile(jnp.concatenate([scale, jnp.ones((2 * HD,), f32)]), heads)[:, None]
    pieces, normed_parts = [], []
    for at in range(2):
        blocks = line_gather(normed[:, at * half : (at + 1) * half], cols)
        outs, normed_part = project(here_of, place_of, turned, factors, blocks, rows, cols, heads)
        pieces += swapped(outs, rows)
        normed_parts.append(normed_part)

    if splits == 2:
        far = partner(gathered, 2, rows)
        near = [gathered, partner(gathered, 1, 2, "dp"), far, partner(far, 1, 2, "dp")]

    result, lse, qkv_heads = attend(starts, place_of, pieces, rows, count, tile)
    if splits == 2:
        other = [partner(after(value, lse), 1, rows) for value in near]
        blocks = near[:2] + other[:2] + near[2:] + other[2:]
    else:
        blocks = spread_rows(gathered, rows)
    weights = assemble(place_of, group_of, blocks, splits)
    leaving = result.astype(bf16).reshape(rows, HD, cols, sub).transpose(0, 2, 1, 3)
    arrived = lax.all_to_all(leaving.reshape(rows * cols, HD, sub), ("row", "col"), 0, 0, tiled=True)

    out_grad_t = out_grad.T.astype(bf16)

    def quarter(values, shift):
        at = lax.rem(here + shift, cols) * sub
        return lax.dynamic_slice_in_dim(values, at, sub, 1)

    grad_pieces = ring_swap([quarter(out_grad_t, shift) for shift in range(cols)], cols)
    own_inverse = quarter(inverse_one, 0)
    own_at = lax.rem(here, cols // 2) * sub
    own_normed = jnp.where(
        here < cols // 2,
        lax.dynamic_slice_in_dim(normed_parts[0], own_at, sub, 1),
        lax.dynamic_slice_in_dim(normed_parts[1], own_at, sub, 1),
    )
    change, (
        back_two,
        gain_two_part,
        leaving,
        grad_mlp,
        attended,
        normed_two,
        activated,
        grad_up,
        grad_branch,
    ) = feed_forward(
        here_of, arrived, grad_pieces, own_normed, own_inverse, gains, weights, rows, cols, heads, twins
    )

    arrived = lax.all_to_all(leaving, ("row", "col"), 0, 0, tiled=True)
    go = arrived.reshape(rows, cols, HD, sub).transpose(0, 2, 1, 3).reshape(rows, HD, count)

    change = ring_swap([after(piece, go) for piece in change], cols)

    wide = (share, 3 * width)
    operands = (grad_branch, attended, normed_two, grad_up, grad_mlp, activated)
    if rows == 4:
        kept, sent = weight_grads(
            place_of,
            *operands,
            ((cols, 2) + wide,) * 2,
            ((0, 0), (1, 0), (0, 1), (1, 1)),
        )
        arrived = after(partner(sent, 1, rows), go)
        mine = add(kept, arrived).astype(bf16).reshape(cols, 2 * share, 3 * width)
        go = after(go, mine)
    else:
        (mine,) = weight_grads(
            jnp.zeros((1,), jnp.int32),
            *operands,
            ((cols, rows) + wide,),
            tuple((0, row) for row in range(rows)),
        )
        mine = lax.psum_scatter(mine, "row", scatter_dimension=1, tiled=False)

    pieces, dim_part = attend_back(
        starts, place_of, scale, qkv_heads, go, result, lse, tile, half
    )
    mine = lax.psum_scatter(mine, "col", scatter_dimension=0, tiled=False)
    if rows == 4:
        mine = mine.reshape((2,) + wide)
        mine = add(mine[0], partner(mine[1], 2, rows)).astype(bf16)
    shard = sum_groups(mine.reshape(wide), groups)

    arrived = []
    for at in range(2):
        leaving = [after(piece, *change) for piece in pieces[at * rows : (at + 1) * rows]]
        arrived.append(swapped(leaving, rows))
    blocks, pairs = [], []
    for at in range(2):
        own, right, left, grads = project_back(
            here_of,
            place_of,
            whole,
            normed_parts[at],
            back_two,
            arrived[at],
            rows,
            cols,
            heads,
            at * (cols // 2),
        )
        blocks.append(LineScatter(own, right, left, cols))
        pairs += [normed_parts[at], grads]

    first, second = blocks
    mark = first.step()
    second.step()
    pairs[1] = after(pairs[1], mark)
    own_head = (place % twins == 0).astype(f32)
    if rows == 4:
        kept, sent, gain_one_part = projection_grads(
            place_of, whole, pairs, ((2,) + wide,) * 2, ((0, 0), (1, 0), (0, 1), (1, 1))
        )
        arrived = partner(sent, 1, rows)
    else:
        mine, gain_one_part = projection_grads(
            jnp.zeros((1,), jnp.int32),
            whole,
            pairs,
            ((rows,) + wide,),
            tuple((0, row) for row in range(rows)),
        )
        arrived = lax.psum_scatter(mine, "row", scatter_dimension=0, tiled=False)
    small = jnp.concatenate([gain_one_part, gain_two_part, dim_part * own_head])[:, 0]
    first.step()
    second.step(arrived)
    if rows == 4:
        far = partner(add(kept[1], arrived[1]).astype(bf16), 2, rows)
        mine = (add(kept[0], arrived[0]) + far.astype(f32)).astype(bf16)
    else:
        far = mine = arrived
    small = total(small, (("row", rows), ("dp", groups)))
    small = small + partner(small, 1, cols, "col")
    first.step(far)
    second.step(far)
    qkv_grad = sum_groups(mine, groups)
    qkv_grad = qkv_grad.reshape(share, heads, 3, HD).transpose(0, 2, 1, 3).reshape(share, 3, width)
    small = small + partner(small, 2, cols, "col")
    gain_one_grad = lax.dynamic_slice_in_dim(small[:D], here * width, width) / norm1_gain
    gain_two_grad = lax.dynamic_slice_in_dim(small[D : 2 * D], here * width, width)
    scale_grad = small[2 * D :] / scale * (scale_base / math.sqrt(HD)) * jax.nn.sigmoid(per_dim)

    output = jnp.zeros_like(residual_in)
    for shift, piece in enumerate(change):
        at = lax.rem(here + cols - shift, cols) * sub
        piece = lax.dynamic_slice_in_dim(residual_in, at, sub, 0) + after(piece, mark).astype(f32).T
        output = lax.dynamic_update_slice_in_dim(output, piece, at, 0)

    summed = jnp.concatenate([first.total, second.total], axis=1)
    grad_one, along_one = summed[:width], summed[width : width + 1]
    back_one = inverse_one * norm1_gain[:, None] * grad_one - residual * inverse_one**2 * (
        along_one / D
    )
    input_grad = out_grad + back_one.T
    return (
        output,
        input_grad,
        gain_one_grad,
        qkv_grad,
        scale_grad,
        shard[:, :width].T,
        gain_two_grad,
        shard[:, width : 2 * width],
        shard[:, 2 * width :].T,
    )


def solution(mesh):
    in_specs = (
        P(("dp", "row"), "col"),
        P("dp"),
        P("col"),
        P("row", None, "col"),
        P(),
        P("col", "row"),
        P("col"),
        P("row", "col"),
        P("col", "row"),
        P(("dp", "row"), "col"),
    )
    out_specs = (
        P(("dp", "row"), "col"),
        P(("dp", "row"), "col"),
        P("col"),
        P("row", None, "col"),
        P(),
        P("col", "row"),
        P("col"),
        P("row", "col"),
        P("col", "row"),
    )
    return jax.shard_map(
        functools.partial(on_device, mesh.shape["dp"], mesh.shape["row"], mesh.shape["col"]),
        mesh=mesh,
        in_specs=in_specs,
        out_specs=out_specs,
        check_vma=False,
    )
```

```python
import functools
import math

import jax
import jax.numpy as jnp
from jax import lax
from jax.experimental import pallas as pl
from jax.experimental.pallas import tpu as pltpu
from jax.sharding import PartitionSpec as P

D = 1280
HD = 80
BLK = 256
LANES = 128

epsilon = 1e-06
scale_base = 1.442695041
excluded = -1e30

bf16 = jnp.bfloat16
f32 = jnp.float32


def dot(left, right):
    return jnp.dot(left, right, preferred_element_type=f32)


def product(form, left, right):
    return jnp.einsum(form, left, right, preferred_element_type=f32)


def three_terms(values):
    high = values.astype(bf16)
    rest = values - high.astype(f32)
    middle = rest.astype(bf16)
    return [high, middle, (rest - middle.astype(f32)).astype(bf16)]


def block_bias(starts_ref, first_block, width, block_count):
    shape = (block_count, width)
    block = lax.broadcasted_iota(jnp.int32, shape, 0)
    own = lax.broadcasted_iota(jnp.int32, shape, 1) // BLK
    start = jnp.zeros(shape, jnp.int32)
    for number in range(width // BLK):
        start = jnp.where(own == number, starts_ref[first_block + number], start)
    return jnp.where((block >= start) & (block <= first_block + own), 0.0, excluded).astype(bf16)


def extended(top, width, block_count, first_block, extra):
    row = lax.broadcasted_iota(jnp.int32, (LANES - HD, width), 0)
    block = first_block + lax.broadcasted_iota(jnp.int32, (LANES - HD, width), 1) // BLK
    marks = (row >= block_count) & (row < block_count + extra)
    if block_count:
        marks = marks | (row == block)
    return jnp.concatenate([top, jnp.where(marks, 1.0, 0.0).astype(bf16)], axis=0).T


def padded(parts, width):
    used = sum(part.shape[0] for part in parts)
    return jnp.concatenate(list(parts) + [jnp.zeros((LANES - used, width), bf16)], axis=0)


def store_pieces(ref, value, source, number, part):
    width, tile = ref.shape[2], value.shape[1]
    if width >= tile:
        ref[source * (part // width), :, pl.ds(pl.multiple_of(number * tile, tile), tile)] = value
        return
    first = source * (part // width) + number * (tile // width)
    for at in range(tile // width):
        ref[first + at] = value[:, at * width : (at + 1) * width]


def load_pieces(ref, source, number, part, tile):
    width = ref.shape[2]
    if width >= tile:
        return ref[source * (part // width), :, pl.ds(pl.multiple_of(number * tile, tile), tile)]
    first = source * (part // width) + number * (tile // width)
    return jnp.concatenate([ref[first + at] for at in range(tile // width)], axis=1)


def forward_kernel(starts_ref, place_ref, *refs, tokens, part, tile, rows):
    pieces = refs[: -5]
    out_ref, lse_ref, qkv_ref, leave_ref, key_scr = refs[-5:]
    half = pieces[0].shape[1]
    for number, piece in enumerate(pieces):
        flip, at = number % rows, number // rows
        qkv_ref[jnp.bitwise_xor(place_ref[0], flip), :, at * half : (at + 1) * half] = piece[...]
    block_count = tokens // BLK
    per_part = part // tile
    per_tile = tile // BLK
    for number in range(tokens // tile):
        source, at = divmod(number, per_part)
        key_scr[number * tile : (number + 1) * tile, :] = extended(
            qkv_ref[source, HD : 2 * HD, at * tile : (at + 1) * tile],
            tile,
            block_count,
            number * per_tile,
            0,
        )

    def query_tile(number, carried):
        source = number // per_part
        at = pl.multiple_of((number % per_part) * tile, tile)
        bias = block_bias(starts_ref, number * per_tile, tile, block_count)
        query = padded([qkv_ref[source, 0:HD, pl.ds(at, tile)], bias], tile)

        def key_tile(key_number, state):
            largest, total, result = state
            keys = key_scr[pl.ds(pl.multiple_of(key_number * tile, tile), tile), :]
            scores = dot(keys, query)
            key_at = pl.multiple_of((key_number % per_part) * tile, tile)
            values = qkv_ref[key_number // per_part, 2 * HD : 3 * HD, pl.ds(key_at, tile)]
            newest = jnp.maximum(largest, jnp.max(scores, axis=0, keepdims=True))
            factor = jnp.exp(largest - newest)
            weights = jnp.exp(scores - newest)
            total = total * factor + jnp.sum(weights, axis=0, keepdims=True)
            result = result * factor + dot(values, weights.astype(bf16))
            return newest, total, result

        largest, total, result = lax.fori_loop(
            starts_ref[number * per_tile] // per_tile,
            number + 1,
            key_tile,
            (
                jnp.full((1, tile), -jnp.inf, f32),
                jnp.zeros((1, tile), f32),
                jnp.zeros((HD, tile), f32),
            ),
        )
        result = result / total
        out_ref[source, :, pl.ds(at, tile)] = result
        store_pieces(leave_ref, result.astype(bf16), source, number % per_part, part)
        lse_ref[source, :, pl.ds(at, tile)] = largest + jnp.log(total)
        return carried

    lax.fori_loop(0, tokens // tile, query_tile, 0)


def backward_kernel(
    starts_ref,
    place_ref,
    scale_ref,
    qkv_ref,
    go_ref,
    out_ref,
    lse_ref,
    *refs,
    tokens,
    part,
    tile,
    rows,
):
    pieces = refs[: -6]
    dim_ref, grad_ref, key_scr, value_scr, key_grad, value_grad = refs[-6:]
    block_count = tokens // BLK
    per_part = part // tile
    per_tile = tile // BLK
    for number in range(tokens // tile):
        source, at = divmod(number, per_part)
        columns = slice(at * tile, (at + 1) * tile)
        band = slice(number * tile, (number + 1) * tile)
        key_scr[band, :] = extended(
            qkv_ref[source, HD : 2 * HD, columns], tile, block_count, number * per_tile, 3
        )
        value_scr[band, :] = extended(qkv_ref[source, 2 * HD : 3 * HD, columns], tile, 0, 0, 3)
    key_grad[...] = jnp.zeros_like(key_grad)
    value_grad[...] = jnp.zeros_like(value_grad)

    def query_tile(number, dim_total):
        source = number // per_part
        at = pl.multiple_of((number % per_part) * tile, tile)
        query_t = qkv_ref[source, 0:HD, pl.ds(at, tile)]
        go_t = load_pieces(go_ref, source, number % per_part, part, tile)
        delta = jnp.sum(
            go_t.astype(f32) * out_ref[source, :, pl.ds(at, tile)], axis=0, keepdims=True
        )
        lse = lse_ref[source, :, pl.ds(at, tile)]
        bias = block_bias(starts_ref, number * per_tile, tile, block_count)
        query_ext = padded([query_t, bias] + three_terms(-lse), tile)
        go_ext = padded([go_t] + three_terms(-delta), tile)
        query = padded([query_t], tile).T
        go = padded([go_t], tile).T

        def key_tile(key_number, total):
            band = pl.ds(pl.multiple_of(key_number * tile, tile), tile)
            key_at = pl.multiple_of((key_number % per_part) * tile, tile)
            keys_t = qkv_ref[key_number // per_part, HD : 2 * HD, pl.ds(key_at, tile)]
            weights = jnp.exp(dot(key_scr[band, :], query_ext))
            slopes = (weights * dot(value_scr[band, :], go_ext)).astype(bf16)
            value_grad[band, :] += dot(weights.astype(bf16), go)
            key_grad[band, :] += dot(slopes, query)
            return total + dot(keys_t, slopes)

        grad = lax.fori_loop(
            starts_ref[number * per_tile] // per_tile,
            number + 1,
            key_tile,
            jnp.zeros((HD, tile), f32),
        )
        grad_ref[source, 0:HD, pl.ds(at, tile)] = (grad * scale_ref[...]).astype(bf16)
        return dim_total + jnp.sum(grad * query_t.astype(f32), axis=1, keepdims=True)

    dim_ref[...] = lax.fori_loop(0, tokens // tile, query_tile, jnp.zeros((HD, 1), f32))
    for number in range(tokens // tile):
        source, at = divmod(number, per_part)
        columns = slice(at * tile, (at + 1) * tile)
        band = slice(number * tile, (number + 1) * tile)
        grad_ref[source, HD : 2 * HD, columns] = key_grad[band, :].T[:HD].astype(bf16)
        grad_ref[source, 2 * HD : 3 * HD, columns] = value_grad[band, :].T[:HD].astype(bf16)
    half = pieces[0].shape[1]
    for number, piece in enumerate(pieces):
        flip, at = number % rows, number // rows
        piece[...] = grad_ref[
            jnp.bitwise_xor(place_ref[0], flip), :, at * half : (at + 1) * half
        ]


in_vmem = pl.BlockSpec(memory_space=pltpu.VMEM)
in_smem = pl.BlockSpec(memory_space=pltpu.SMEM)


def attend(starts, place, pieces, rows, part, tile, width):
    tokens = rows * part
    return pl.pallas_call(
        functools.partial(forward_kernel, tokens=tokens, part=part, tile=tile, rows=rows),
        out_shape=(
            jax.ShapeDtypeStruct((rows, HD, part), f32),
            jax.ShapeDtypeStruct((rows, 1, part), f32),
            jax.ShapeDtypeStruct((rows, 3 * HD, part), bf16),
            jax.ShapeDtypeStruct((tokens // width, HD, width), bf16),
        ),
        in_specs=[in_smem] * 2 + [in_vmem] * len(pieces),
        out_specs=(in_vmem,) * 4,
        scratch_shapes=[pltpu.VMEM((tokens, LANES), bf16)],
        compiler_params=pltpu.CompilerParams(vmem_limit_bytes=60 << 20),
        cost_estimate=pl.CostEstimate(
            flops=3 * LANES * tokens * tokens,
            bytes_accessed=12 << 20,
            transcendentals=tokens * tokens // 3,
        ),
    )(starts, place, *pieces)


def attend_back(starts, place, scale, qkv, go, out, lse, tile, half):
    rows, _, part = qkv.shape
    tokens = rows * part
    count = rows * (part // half)
    results = pl.pallas_call(
        functools.partial(backward_kernel, tokens=tokens, part=part, tile=tile, rows=rows),
        out_shape=(jax.ShapeDtypeStruct((3 * HD, half), bf16),) * count
        + (jax.ShapeDtypeStruct((HD, 1), f32),),
        in_specs=[in_smem] * 2 + [in_vmem] * 5,
        out_specs=(in_vmem,) * (count + 1),
        scratch_shapes=[pltpu.VMEM((rows, 3 * HD, part), bf16)]
        + [pltpu.VMEM((tokens, LANES), bf16)] * 2
        + [pltpu.VMEM((tokens, LANES), f32)] * 2,
        compiler_params=pltpu.CompilerParams(vmem_limit_bytes=60 << 20),
        cost_estimate=pl.CostEstimate(
            flops=8 * LANES * tokens * tokens,
            bytes_accessed=16 << 20,
            transcendentals=tokens * tokens // 3,
        ),
    )(starts, place, scale.reshape(HD, 1), qkv, go, out, lse)
    return results[:-1], results[-1]


def assemble_kernel(here_ref, place_ref, group_ref, *refs, cols, splits):
    blocks, out_ref = refs[:-1], refs[-1]
    part = out_ref.shape[1] // len(blocks)
    width = out_ref.shape[2] // cols
    for number, block in enumerate(blocks):
        row = jnp.bitwise_xor(place_ref[0], number // splits)
        piece = jnp.bitwise_xor(group_ref[0], number % splits)
        band = pl.ds(pl.multiple_of((row * splits + piece) * part, 16), part)
        for col in range(cols):
            value = block[lax.rem(here_ref[0] + cols - col, cols), 0:part, :]
            for matrix in range(3):
                out_ref[matrix, band, col * width : (col + 1) * width] = value[
                    :, matrix * width : (matrix + 1) * width
                ]


def feed_kernel(
    here_ref,
    place_ref,
    att_ref,
    normed_ref,
    inverse_ref,
    gains_ref,
    w_hbm,
    *refs,
    rows,
    cols,
    heads,
    twins,
    order,
):
    go_pieces, change_pieces = refs[:cols], refs[cols : 2 * cols]
    back_ref, gain_ref, leave_ref, rhs_ref = refs[2 * cols : 2 * cols + 4]
    lhs_refs = refs[2 * cols + 4 : -12]
    (
        w_ref,
        attended,
        normed_two,
        branch_grad,
        go_ref,
        branch,
        middle,
        grad_two,
        flipped,
        flipped_go,
        grad_att,
        done,
    ) = refs[-12:]
    width, sub = go_pieces[0].shape
    copies = [
        pltpu.make_async_copy(w_hbm.at[number], w_ref.at[number], done.at[number])
        for number in range(3)
    ]
    for copy in copies:
        copy.start()

    def ring(shift):
        return pl.ds(pl.multiple_of(lax.rem(here_ref[0] + shift, cols) * width, 16), width)

    for number, piece in enumerate(go_pieces):
        go_ref[ring(cols - number), :] = piece[...]
    step = 256
    for col in range(cols):
        for head in range(heads):
            at = (col * heads + head) * HD
            attended[at : at + HD, :] = att_ref[head * twins * cols + col]
    inverse = inverse_ref[...]
    copies[0].wait()

    def part(number):
        return pl.ds(pl.multiple_of(number * step, step), step)

    def first(number, total):
        at = part(number)
        here = dot(w_ref[0, at, :], attended[...])
        branch[at, :] = here
        mid = normed_ref[at, :].astype(f32) / (inverse * gains_ref[at, 0:1]) + here
        middle[at, :] = mid
        flipped_go[:, at] = go_ref[at, :].T
        rhs_ref[0, :, at] = attended[at, :].T
        return total + jnp.sum(mid * mid, axis=0, keepdims=True)

    steps = D // step
    total = lax.fori_loop(0, steps, first, jnp.zeros((1, sub), f32))
    inverse_two = lax.rsqrt(total / D + epsilon)
    copies[1].wait()
    copies[2].wait()

    def second(number, carried):
        at = part(number)
        value = (middle[at, :] * inverse_two * gains_ref[at, 1:2]).astype(bf16)
        normed_two[at, :] = value
        flipped[:, at] = value.T
        return carried

    lax.fori_loop(0, steps, second, 0)

    def third(number, carried):
        at = part(number)
        up_proj = dot(flipped[...], w_ref[1, :, at])
        sigmoid_up = jax.nn.sigmoid(up_proj)
        rhs_ref[2, :, at] = (up_proj * sigmoid_up).astype(bf16)
        grad_act = dot(flipped_go[...], w_ref[2, :, at])
        rhs_ref[1, :, at] = (
            grad_act * sigmoid_up * (1.0 + up_proj * (1.0 - sigmoid_up))
        ).astype(bf16)
        return carried

    lax.fori_loop(0, steps, third, 0)

    def fourth(number, along):
        at = part(number)
        branch[at, :] += dot_last(w_ref[2, at, :], rhs_ref[2])
        grad = dot_last(w_ref[1, at, :], rhs_ref[1])
        grad_two[at, :] = grad
        return along + jnp.sum(gains_ref[at, 1:2] * grad * middle[at, :], axis=0, keepdims=True)

    along = lax.fori_loop(0, steps, fourth, jnp.zeros((1, sub), f32))
    shrink = inverse_two * inverse_two * inverse_two * along / D

    def fifth(number, carried):
        at = part(number)
        grad = grad_two[at, :]
        mid = middle[at, :]
        back = inverse_two * gains_ref[at, 1:2] * grad - mid * shrink
        back_ref[at, :] = (back / (inverse * gains_ref[at, 0:1])).astype(bf16)
        gain_ref[at, :] = jnp.sum(grad * mid * inverse_two, axis=1, keepdims=True)
        value = (go_ref[at, :].astype(f32) + back).astype(bf16)
        branch_grad[at, :] = value
        flipped[:, at] = value.T
        return carried

    lax.fori_loop(0, steps, fifth, 0)

    def sixth(number, carried):
        at = part(number)
        grad_att[at, :] = dot(flipped[...], w_ref[0, :, at]).T.astype(bf16)
        return carried

    lax.fori_loop(0, steps, sixth, 0)
    for number, piece in enumerate(change_pieces):
        piece[...] = branch[ring(number), :].astype(bf16)
    share = D // rows
    for slot, (out, at) in enumerate(order):
        row = jnp.bitwise_xor(place_ref[0], slot) if len(lhs_refs) > 1 else slot
        band = pl.ds(pl.multiple_of(row * share, 16), share)
        for number, value in enumerate((branch_grad, normed_two, go_ref)):
            lhs_refs[out][at, number] = value[band, :]
    for row in range(rows):
        for col in range(cols):
            at = (col * heads + row // twins) * HD
            leave_ref[row * cols + col] = grad_att[at : at + HD, :]


def dot_last(left, right):
    return lax.dot_general(left, right, (((1,), (1,)), ((), ())), preferred_element_type=f32)


def weights_kernel(here_ref, group_ref, *refs, count, splits):
    operands, outs = refs[:count], refs[count:]
    cols, part, wide = outs[0].shape
    width = wide // 3
    for index, out in enumerate(outs):
        slot = index // splits
        piece = jnp.bitwise_xor(group_ref[0], index % splits)
        band = pl.ds(pl.multiple_of(piece * part, 16), part)
        for number in range(3):
            value = sum(
                dot(operands[at][slot, number, band, :], operands[at + 1][number])
                for at in range(0, count, 2)
            ).astype(bf16)
            for col in range(cols):
                place = lax.rem(col + cols - here_ref[0], cols)
                out[place, :, number * width : (number + 1) * width] = value[
                    :, col * width : (col + 1) * width
                ]


def assemble(here, place, group, blocks, splits):
    cols = blocks[0].shape[0]
    return pl.pallas_call(
        functools.partial(assemble_kernel, cols=cols, splits=splits),
        out_shape=jax.ShapeDtypeStruct((3, D, D), bf16),
        in_specs=[in_smem] * 3 + [in_vmem] * len(blocks),
        out_specs=in_vmem,
        compiler_params=pltpu.CompilerParams(vmem_limit_bytes=60 << 20),
        cost_estimate=pl.CostEstimate(flops=0, bytes_accessed=20 << 20, transcendentals=0),
    )(here, place, group, *blocks)


def feed_forward(
    here, place, attended, pieces, normed, inverse, gains, weights, rows, cols, heads, twins, shapes, order
):
    width, sub = pieces[0].shape
    results = pl.pallas_call(
        functools.partial(
            feed_kernel, rows=rows, cols=cols, heads=heads, twins=twins, order=order
        ),
        out_shape=(jax.ShapeDtypeStruct((width, sub), bf16),) * cols
        + (
            jax.ShapeDtypeStruct((D, sub), bf16),
            jax.ShapeDtypeStruct((D, 1), f32),
            jax.ShapeDtypeStruct((rows * cols, HD, sub), bf16),
            jax.ShapeDtypeStruct((3, sub, D), bf16),
        )
        + tuple(jax.ShapeDtypeStruct(shape, bf16) for shape in shapes),
        in_specs=[in_smem] * 2
        + [in_vmem] * 4
        + [pl.BlockSpec(memory_space=pl.ANY)]
        + [in_vmem] * cols,
        out_specs=(in_vmem,) * (cols + 4 + len(shapes)),
        scratch_shapes=[pltpu.VMEM((3, D, D), bf16)]
        + [pltpu.VMEM((D, sub), bf16)] * 4
        + [pltpu.VMEM((D, sub), f32)] * 3
        + [pltpu.VMEM((sub, D), bf16)] * 2
        + [pltpu.VMEM((D, sub), bf16), pltpu.SemaphoreType.DMA((3,))],
        compiler_params=pltpu.CompilerParams(vmem_limit_bytes=60 << 20),
        cost_estimate=pl.CostEstimate(
            flops=12 * D * D * sub, bytes_accessed=20 << 20, transcendentals=D * sub
        ),
    )(here, place, attended, normed, inverse, gains, weights, *pieces)
    return results[:cols], results[cols : cols + 4], results[cols + 4 :]


def weight_grads(here, group, pairs, cols, splits):
    slots, _, share, sub = pairs[0].shape
    count = slots * splits
    return pl.pallas_call(
        functools.partial(weights_kernel, count=len(pairs), splits=splits),
        out_shape=(jax.ShapeDtypeStruct((cols, share // splits, 3 * D // cols), bf16),) * count,
        in_specs=[in_smem] * 2 + [in_vmem] * len(pairs),
        out_specs=(in_vmem,) * count,
        compiler_params=pltpu.CompilerParams(vmem_limit_bytes=60 << 20),
        cost_estimate=pl.CostEstimate(
            flops=6 * D * D * sub, bytes_accessed=16 << 20, transcendentals=0
        ),
    )(here, group, *pairs)


def copies_kernel(place_ref, *refs):
    blocks, (whole, turned) = refs[:-2], refs[-2:]
    share = blocks[0].shape[0]
    for flip, block in enumerate(blocks):
        row = jnp.bitwise_xor(place_ref[0], flip)
        whole[pl.ds(pl.multiple_of(row * share, 16), share), :] = block[...]
    for number in range(D // LANES):
        at = slice(number * LANES, (number + 1) * LANES)
        turned[:, at] = whole[at, :].T


def projection_copies(place, blocks):
    share, wide = blocks[0].shape
    return pl.pallas_call(
        copies_kernel,
        out_shape=(
            jax.ShapeDtypeStruct((D, wide), bf16),
            jax.ShapeDtypeStruct((wide, D), bf16),
        ),
        in_specs=[in_smem] + [in_vmem] * len(blocks),
        out_specs=(in_vmem,) * 2,
        compiler_params=pltpu.CompilerParams(vmem_limit_bytes=60 << 20),
        cost_estimate=pl.CostEstimate(flops=0, bytes_accessed=8 << 20, transcendentals=0),
    )(place, *blocks)


def project_kernel(place_ref, turned_ref, factor_ref, normed_ref, *refs, rows, heads):
    outs, result = refs[:-1], refs[-1]
    for head in range(heads):
        at = slice(head * 3 * HD, (head + 1) * 3 * HD)
        value = dot(turned_ref[at, :], normed_ref[...]) * factor_ref[at, :]
        result[head] = value.astype(bf16)
    for flip, out in enumerate(outs):
        out[...] = result[jnp.bitwise_xor(place_ref[0], flip) // (rows // heads)]


def project(place, turned, factors, normed, rows, heads):
    half = normed.shape[1]
    return pl.pallas_call(
        functools.partial(project_kernel, rows=rows, heads=heads),
        out_shape=(jax.ShapeDtypeStruct((3 * HD, half), bf16),) * rows,
        in_specs=[in_smem] + [in_vmem] * 3,
        out_specs=(in_vmem,) * rows,
        scratch_shapes=[pltpu.VMEM((heads, 3 * HD, half), bf16)],
        compiler_params=pltpu.CompilerParams(vmem_limit_bytes=60 << 20),
        cost_estimate=pl.CostEstimate(
            flops=2 * D * turned.shape[0] * half, bytes_accessed=10 << 20, transcendentals=0
        ),
    )(place, turned, factors, normed)


def back_kernel(here_ref, place_ref, whole_ref, *refs, rows, cols, heads):
    normed, back_ref, pieces, (payload, grads) = refs[:2], refs[2], refs[3:-2], refs[-2:]
    half = normed[0].shape[1]
    width = D // cols
    sub = back_ref.shape[1]
    here = here_ref[0]
    gather_heads(place_ref, pieces, grads, heads)
    for number in range(2):
        along = jnp.zeros((1, half), f32)
        tokens = slice(number * half, (number + 1) * half)
        for col in range(cols):
            at = slice(col * width, (col + 1) * width)
            value = dot(whole_ref[at, :], grads[:, tokens])
            along += jnp.sum(value * normed[number][at, :].astype(f32), axis=0, keepdims=True)
            for quarter in range(half // sub):
                columns = slice(quarter * sub, (quarter + 1) * sub)
                into = slice(number * half + quarter * sub, number * half + (quarter + 1) * sub)
                mine = jnp.where(here == number * (half // sub) + quarter, 1.0, 0.0)
                payload[col, 0:width, into] = (
                    value[:, columns] + back_ref[at, :].astype(f32) * mine
                ).astype(bf16)
        tail = jnp.concatenate([along, jnp.zeros((15, half), f32)], axis=0).astype(bf16)
        for col in range(cols):
            payload[col, width : width + 16, tokens] = tail


def gather_heads(place_ref, pieces, grads, heads):
    for flip, piece in enumerate(pieces):
        head = jnp.bitwise_xor(place_ref[0], flip) // (len(pieces) // heads)
        grads[pl.ds(pl.multiple_of(head * 3 * HD, 16), 3 * HD), :] = piece[...]


def project_back(here, place, whole, normed, back, pieces, rows, cols, heads):
    count = 2 * normed[0].shape[1]
    width = D // cols
    return pl.pallas_call(
        functools.partial(back_kernel, rows=rows, cols=cols, heads=heads),
        out_shape=jax.ShapeDtypeStruct((cols, width + 16, count), bf16),
        in_specs=[in_smem] * 2 + [in_vmem] * (4 + rows),
        out_specs=in_vmem,
        scratch_shapes=[pltpu.VMEM((3 * width, count), bf16)],
        compiler_params=pltpu.CompilerParams(vmem_limit_bytes=60 << 20),
        cost_estimate=pl.CostEstimate(
            flops=2 * D * 3 * width * count, bytes_accessed=16 << 20, transcendentals=0
        ),
    )(here, place, whole, *normed, back, *pieces)


def projection_grads_kernel(place_ref, whole_ref, *refs, order, heads):
    outs, (gain_ref, grads) = refs[-2 - (1 + max(out for out, _ in order)) : -2], refs[-2:]
    normed, pieces = refs[:2], refs[2 : -2 - len(outs)]
    half = normed[0].shape[1]
    gather_heads(place_ref, pieces, grads, heads)
    share = outs[0].shape[1]
    for slot, (out, at) in enumerate(order):
        row = jnp.bitwise_xor(place_ref[0], slot) if len(outs) > 1 else slot
        band = pl.ds(pl.multiple_of(row * share, 16), share)
        value = dot_last(normed[0][band, :], grads[:, :half]) + dot_last(
            normed[1][band, :], grads[:, half:]
        )
        gain_ref[band, :] = jnp.sum(value * whole_ref[band, :].astype(f32), axis=1, keepdims=True)
        outs[out][at] = value.astype(bf16)


def projection_grads(place, whole, normed, pieces, heads, shapes, order):
    half = normed[0].shape[1]
    return pl.pallas_call(
        functools.partial(projection_grads_kernel, order=order, heads=heads),
        out_shape=tuple(jax.ShapeDtypeStruct(shape, bf16) for shape in shapes)
        + (jax.ShapeDtypeStruct((D, 1), f32),),
        in_specs=[in_smem] + [in_vmem] * (3 + len(pieces)),
        out_specs=(in_vmem,) * (len(shapes) + 1),
        scratch_shapes=[pltpu.VMEM((whole.shape[1], 2 * half), bf16)],
        compiler_params=pltpu.CompilerParams(vmem_limit_bytes=60 << 20),
        cost_estimate=pl.CostEstimate(
            flops=4 * D * whole.shape[1] * half, bytes_accessed=12 << 20, transcendentals=0
        ),
    )(place, whole, *normed, *pieces)


def after(values, *others):
    return lax.optimization_barrier((values,) + others)[0]


def partner(values, flip, size, axis="row"):
    return lax.ppermute(values, axis, [(at, at ^ flip) for at in range(size)])


def plane(values, splits):
    result = [values[0]]
    for index in range(1, len(values)):
        flip, other = index // splits * 2, index % splits
        result.append(
            lax.ppermute(
                values[index],
                ("dp", "row"),
                [(at, at ^ (other * 4 + flip)) for at in range(splits * 4)],
            )
            if splits == 2
            else partner(values[index], flip, 4)
        )
    return result


def swapped(pieces, rows):
    return [pieces[0]] + [partner(pieces[flip], flip, rows) for flip in range(1, rows)]


def spread_rows(values, rows):
    if rows != 4:
        return swapped([values] * rows, rows)
    far = partner(values, 2, rows)
    return [values, partner(values, 1, rows), far, partner(far, 1, rows)]


def add(left, right):
    return left.astype(f32) + right.astype(f32)


def total(values, axes):
    for axis, size in axes:
        flip = 1
        while flip < size:
            values = values + partner(values, flip, size, axis)
            flip *= 2
    return values


def sum_groups(values, groups):
    if groups == 2:
        return add(values, partner(values, 1, 2, "dp"))
    return lax.psum(values, "dp").astype(f32)


def ring_swap(pieces, cols):
    return [pieces[0]] + [
        lax.ppermute(pieces[shift], "col", [(at, (at + shift) % cols) for at in range(cols)])
        for shift in range(1, cols)
    ]


def on_device(
    groups, rows, cols, residual_in, seq_ids, norm1_gain, w_qkv, per_dim, w_out, norm2_gain, w_up, w_down, out_grad
):
    count, width = residual_in.shape
    heads = width // HD
    twins = rows // heads
    sub = count // cols
    half = count // 2
    share = w_qkv.shape[0]
    tile = 768 if count % 768 == 0 else BLK
    here = lax.axis_index("col")
    place = lax.axis_index("row")
    here_of, place_of = here[None].astype(jnp.int32), place[None].astype(jnp.int32)

    block_seq = seq_ids[::BLK]
    starts = jnp.sum((block_seq[None, :] < block_seq[:, None]).astype(jnp.int32), axis=1)

    residual = residual_in.T
    squares = jnp.sum(residual * residual, axis=0)
    squares = squares + partner(squares, 1, cols, "col")
    inverse_one = lax.rsqrt((squares + partner(squares, 2, cols, "col")) / D + epsilon)[None, :]
    normed = (residual * inverse_one * norm1_gain[:, None]).astype(bf16)
    qkv_local = w_qkv.astype(bf16).reshape(share, 3, heads, HD).transpose(0, 2, 1, 3)
    qkv_local = qkv_local.reshape(share, heads * 3 * HD)
    whole, turned = projection_copies(place_of, spread_rows(qkv_local, rows))
    scale = jax.nn.softplus(per_dim) * scale_base / math.sqrt(HD)
    factors = jnp.tile(jnp.concatenate([scale, jnp.ones((2 * HD,), f32)]), heads)[:, None]
    stacked = jnp.concatenate(
        [w_out.T, w_up, w_down.T], axis=1
    ).astype(bf16)
    gains = [jnp.concatenate(three_terms(gain))[None] for gain in (norm1_gain, norm2_gain)]
    splits = 2 if groups == 2 and rows == 4 else 1
    part = share // splits
    group_of = jnp.zeros((1,), jnp.int32)
    if splits == 2:
        group = lax.axis_index("dp")
        group_of = group[None].astype(jnp.int32)
        stacked = lax.dynamic_slice_in_dim(stacked, group * part, part, 0)
    stacked = jnp.concatenate([stacked] + gains + [jnp.zeros((14, 3 * width), bf16)], axis=0)
    gathered = jnp.stack(ring_swap([after(stacked, turned)] * cols, cols))
    gains = gathered[:, part : part + 2].astype(f32).reshape(cols, 2, 3, width).sum(axis=2)
    gains = jnp.concatenate(
        [
            lax.dynamic_index_in_dim(gains, lax.rem(here + cols - col, cols), 0, keepdims=False)
            for col in range(cols)
        ],
        axis=1,
    ).T
    near = [gathered]
    if rows == 4:
        if splits == 2:
            near.append(partner(gathered, 1, 2, "dp"))
        near.append(partner(gathered, 2, rows))
        if splits == 2:
            near.append(partner(after(near[2], near[1]), 1, 2, "dp"))

    pieces, normed_parts = [], []
    for at in range(2):
        part = normed[:, at * half : (at + 1) * half]
        if at:
            part = after(part, turned)
        normed_parts.append(lax.all_gather(part, "col", axis=0, tiled=True))
        outs = project(place_of, turned, factors, normed_parts[at], rows, heads)
        pieces += swapped(outs, rows)

    tidy = sub % LANES == 0
    if rows == 4:
        pieces[0] = after(pieces[0], *near[1:])
    result, lse, qkv_heads, leaving = attend(
        starts, place_of, pieces, rows, count, tile, sub if tidy else count
    )
    if rows == 4:
        near = [after(value, lse) for value in near]
        other = [partner(value, 1, rows) for value in near]
        blocks = near[:splits] + other[:splits] + near[splits:] + other[splits:]
    else:
        blocks = spread_rows(gathered, rows)
    weights = assemble(here_of, place_of, group_of, blocks, splits)
    out_grad_t = out_grad.T.astype(bf16)

    def quarter(values, shift):
        at = lax.rem(here + shift, cols) * sub
        return lax.dynamic_slice_in_dim(values, at, sub, 1)

    grad_pieces = ring_swap([quarter(out_grad_t, shift) for shift in range(cols)], cols)

    if not tidy:
        leaving = leaving.reshape(rows, HD, cols, sub).transpose(0, 2, 1, 3)
        leaving = leaving.reshape(rows * cols, HD, sub)
    leaving = after(leaving, *grad_pieces)
    arrived = lax.all_to_all(leaving, ("row", "col"), 0, 0, tiled=True)

    own_inverse = quarter(inverse_one, 0)
    own_at = lax.rem(here, cols // 2) * sub
    own_normed = jnp.where(
        here < cols // 2,
        lax.dynamic_slice_in_dim(normed_parts[0], own_at, sub, 1),
        lax.dynamic_slice_in_dim(normed_parts[1], own_at, sub, 1),
    )
    wide = (share, 3 * width)
    pairwise = ((0, 0), (1, 0), (0, 1), (1, 1))
    natural = tuple((0, row) for row in range(rows))
    order, slots = (pairwise, 2) if rows == 4 else (natural, rows)
    change, (back_two, gain_two_part, leaving, rhs), lhs = feed_forward(
        here_of,
        place_of,
        arrived,
        grad_pieces,
        own_normed,
        own_inverse,
        gains,
        weights,
        rows,
        cols,
        heads,
        twins,
        ((slots, 3, share, sub),) * (rows // slots),
        order,
    )

    go = lax.all_to_all(leaving, ("row", "col"), 0, 0, tiled=True)
    if not tidy:
        go = go.reshape(rows, cols, HD, sub).transpose(0, 2, 1, 3).reshape(rows, HD, count)

    if rows == 4:
        pairs = [lhs[0], rhs, partner(lhs[1], 1, rows), partner(rhs, 1, rows)]
        mine = weight_grads(here_of, group_of, pairs, cols, splits)
        go = after(go, *mine)
        mine = plane(mine, splits)
    else:
        mine = jnp.stack(weight_grads(here_of, group_of, [lhs[0], rhs], cols, 1))
        mine = lax.psum_scatter(mine, "row", scatter_dimension=0, tiled=False)

    pieces, dim_part = attend_back(
        starts, place_of, scale, qkv_heads, go, result, lse, tile, count
    )
    arrived = swapped(pieces, rows)

    if rows == 4:
        mine = sum(after(value, arrived[1]).astype(f32) for value in mine).astype(bf16)
    mine = ring_swap([mine[shift] for shift in range(cols)], cols)
    mine = sum(value.astype(f32) for value in mine).astype(bf16)
    if splits == 2:
        mine = jnp.stack([mine, partner(mine, 1, 2, "dp")])
        shard = jnp.where(group == 0, mine, mine[::-1]).reshape(wide).astype(f32)
    else:
        shard = sum_groups(mine, groups)

    arrived[0] = after(arrived[0], mine)
    payload = project_back(
        here_of, place_of, whole, normed_parts, back_two, arrived, rows, cols, heads
    )
    summed = lax.psum_scatter(payload, "col", scatter_dimension=0, tiled=False).astype(f32)

    own_head = (place % twins == 0).astype(f32)
    *parts, gain_one_part = projection_grads(
        place_of,
        after(whole, payload),
        normed_parts,
        arrived,
        heads,
        ((slots,) + wide,) * (rows // slots),
        order,
    )
    small = jnp.concatenate([gain_one_part, gain_two_part, dim_part * own_head])[:, 0]
    if rows == 4:
        kept, sent = parts
        arrived = partner(sent, 1, rows)
        far = partner(add(kept[1], arrived[1]).astype(bf16), 2, rows)
        mine = (add(kept[0], arrived[0]) + far.astype(f32)).astype(bf16)
    else:
        mine = lax.psum_scatter(parts[0], "row", scatter_dimension=0, tiled=False)
    qkv_grad = sum_groups(mine, groups)
    qkv_grad = qkv_grad.reshape(share, heads, 3, HD).transpose(0, 2, 1, 3).reshape(share, 3, width)
    small = total(small, (("row", rows), ("dp", groups), ("col", cols)))
    gain_one_grad = lax.dynamic_slice_in_dim(small[:D], here * width, width) / norm1_gain
    gain_two_grad = lax.dynamic_slice_in_dim(small[D : 2 * D], here * width, width)
    scale_grad = small[2 * D :] / scale * (scale_base / math.sqrt(HD)) * jax.nn.sigmoid(per_dim)

    change = ring_swap(
        [after(piece, go if at % 2 else payload) for at, piece in enumerate(change)], cols
    )
    output = jnp.zeros_like(residual_in)
    for shift, piece in enumerate(change):
        at = lax.rem(here + cols - shift, cols) * sub
        piece = lax.dynamic_slice_in_dim(residual_in, at, sub, 0) + piece.astype(f32).T
        output = lax.dynamic_update_slice_in_dim(output, piece, at, 0)

    grad_one, along_one = summed[:width], summed[width : width + 1]
    back_one = inverse_one * norm1_gain[:, None] * grad_one - residual * inverse_one**2 * (
        along_one / D
    )
    input_grad = out_grad + back_one.T
    return (
        output,
        input_grad,
        gain_one_grad,
        qkv_grad,
        scale_grad,
        shard[:, :width].T,
        gain_two_grad,
        shard[:, width : 2 * width],
        shard[:, 2 * width :].T,
    )


def solution(mesh):
    in_specs = (
        P(("dp", "row"), "col"),
        P("dp"),
        P("col"),
        P("row", None, "col"),
        P(),
        P("col", "row"),
        P("col"),
        P("row", "col"),
        P("col", "row"),
        P(("dp", "row"), "col"),
    )
    out_specs = (
        P(("dp", "row"), "col"),
        P(("dp", "row"), "col"),
        P("col"),
        P("row", None, "col"),
        P(),
        P("col", "row"),
        P("col"),
        P("row", "col"),
        P("col", "row"),
    )
    return jax.shard_map(
        functools.partial(on_device, mesh.shape["dp"], mesh.shape["row"], mesh.shape["col"]),
        mesh=mesh,
        in_specs=in_specs,
        out_specs=out_specs,
        check_vma=False,
    )
```

```python
import functools
import math

import jax
import jax.numpy as jnp
from jax import lax
from jax.experimental import pallas as pl
from jax.experimental.pallas import tpu as pltpu
from jax.sharding import PartitionSpec as P

D = 1280
HD = 80
BLK = 256
LANES = 128

epsilon = 1e-06
scale_base = 1.442695041
excluded = -1e30

bf16 = jnp.bfloat16
f32 = jnp.float32


def dot(left, right):
    return jnp.dot(left, right, preferred_element_type=f32)


def product(form, left, right):
    return jnp.einsum(form, left, right, preferred_element_type=f32)


def three_terms(values):
    high = values.astype(bf16)
    rest = values - high.astype(f32)
    middle = rest.astype(bf16)
    return [high, middle, (rest - middle.astype(f32)).astype(bf16)]


def block_bias(starts_ref, first_block, width, block_count):
    shape = (block_count, width)
    block = lax.broadcasted_iota(jnp.int32, shape, 0)
    own = lax.broadcasted_iota(jnp.int32, shape, 1) // BLK
    start = jnp.zeros(shape, jnp.int32)
    for number in range(width // BLK):
        start = jnp.where(own == number, starts_ref[first_block + number], start)
    return jnp.where((block >= start) & (block <= first_block + own), 0.0, excluded).astype(bf16)


def extended(top, width, block_count, first_block, extra):
    row = lax.broadcasted_iota(jnp.int32, (LANES - HD, width), 0)
    block = first_block + lax.broadcasted_iota(jnp.int32, (LANES - HD, width), 1) // BLK
    marks = (row >= block_count) & (row < block_count + extra)
    if block_count:
        marks = marks | (row == block)
    return jnp.concatenate([top, jnp.where(marks, 1.0, 0.0).astype(bf16)], axis=0).T


def padded(parts, width):
    used = sum(part.shape[0] for part in parts)
    return jnp.concatenate(list(parts) + [jnp.zeros((LANES - used, width), bf16)], axis=0)


def store_pieces(ref, value, source, number, part):
    width, tile = ref.shape[2], value.shape[1]
    if width >= tile:
        ref[source * (part // width), :, pl.ds(pl.multiple_of(number * tile, tile), tile)] = value
        return
    first = source * (part // width) + number * (tile // width)
    for at in range(tile // width):
        ref[first + at] = value[:, at * width : (at + 1) * width]


def load_pieces(ref, source, number, part, tile):
    width = ref.shape[2]
    if width >= tile:
        return ref[source * (part // width), :, pl.ds(pl.multiple_of(number * tile, tile), tile)]
    grain = math.gcd(width, tile)
    chunks = []
    for at in range(tile // grain):
        start = number * tile + at * grain
        column = pl.multiple_of(lax.rem(start, width), grain)
        chunks.append(ref[source * (part // width) + start // width, :, pl.ds(column, grain)])
    return jnp.concatenate(chunks, axis=1)


def forward_kernel(starts_ref, place_ref, *refs, tokens, part, tile, rows):
    pieces = refs[: -5]
    out_ref, lse_ref, qkv_ref, leave_ref, key_scr = refs[-5:]
    half = pieces[0].shape[1]
    for number, piece in enumerate(pieces):
        flip, at = number % rows, number // rows
        qkv_ref[jnp.bitwise_xor(place_ref[0], flip), :, at * half : (at + 1) * half] = piece[...]
    block_count = tokens // BLK
    per_part = part // tile
    per_tile = tile // BLK
    for number in range(tokens // tile):
        source, at = divmod(number, per_part)
        key_scr[number * tile : (number + 1) * tile, :] = extended(
            qkv_ref[source, HD : 2 * HD, at * tile : (at + 1) * tile],
            tile,
            block_count,
            number * per_tile,
            0,
        )

    def query_tile(number, carried):
        source = number // per_part
        at = pl.multiple_of((number % per_part) * tile, tile)
        bias = block_bias(starts_ref, number * per_tile, tile, block_count)
        query = padded([qkv_ref[source, 0:HD, pl.ds(at, tile)], bias], tile)

        def key_tile(key_number, state):
            largest, total, result = state
            keys = key_scr[pl.ds(pl.multiple_of(key_number * tile, tile), tile), :]
            scores = dot(keys, query)
            key_at = pl.multiple_of((key_number % per_part) * tile, tile)
            values = qkv_ref[key_number // per_part, 2 * HD : 3 * HD, pl.ds(key_at, tile)]
            newest = jnp.maximum(largest, jnp.max(scores, axis=0, keepdims=True))
            factor = jnp.exp(largest - newest)
            weights = jnp.exp(scores - newest)
            total = total * factor + jnp.sum(weights, axis=0, keepdims=True)
            result = result * factor + dot(values, weights.astype(bf16))
            return newest, total, result

        largest, total, result = lax.fori_loop(
            starts_ref[number * per_tile] // per_tile,
            number + 1,
            key_tile,
            (
                jnp.full((1, tile), -jnp.inf, f32),
                jnp.zeros((1, tile), f32),
                jnp.zeros((HD, tile), f32),
            ),
        )
        result = result / total
        out_ref[source, :, pl.ds(at, tile)] = result
        store_pieces(leave_ref, result.astype(bf16), source, number % per_part, part)
        lse_ref[source, :, pl.ds(at, tile)] = largest + jnp.log(total)
        return carried

    lax.fori_loop(0, tokens // tile, query_tile, 0)


def backward_kernel(
    starts_ref,
    place_ref,
    scale_ref,
    qkv_ref,
    go_ref,
    out_ref,
    lse_ref,
    *refs,
    tokens,
    part,
    tile,
    rows,
):
    pieces = refs[: -6]
    dim_ref, grad_ref, key_scr, value_scr, key_grad, value_grad = refs[-6:]
    block_count = tokens // BLK
    per_part = part // tile
    per_tile = tile // BLK
    for number in range(tokens // tile):
        source, at = divmod(number, per_part)
        columns = slice(at * tile, (at + 1) * tile)
        band = slice(number * tile, (number + 1) * tile)
        key_scr[band, :] = extended(
            qkv_ref[source, HD : 2 * HD, columns], tile, block_count, number * per_tile, 3
        )
        value_scr[band, :] = extended(qkv_ref[source, 2 * HD : 3 * HD, columns], tile, 0, 0, 3)
    key_grad[...] = jnp.zeros_like(key_grad)
    value_grad[...] = jnp.zeros_like(value_grad)

    def query_tile(number, dim_total):
        source = number // per_part
        at = pl.multiple_of((number % per_part) * tile, tile)
        query_t = qkv_ref[source, 0:HD, pl.ds(at, tile)]
        go_t = load_pieces(go_ref, source, number % per_part, part, tile)
        delta = jnp.sum(
            go_t.astype(f32) * out_ref[source, :, pl.ds(at, tile)], axis=0, keepdims=True
        )
        lse = lse_ref[source, :, pl.ds(at, tile)]
        bias = block_bias(starts_ref, number * per_tile, tile, block_count)
        query_ext = padded([query_t, bias] + three_terms(-lse), tile)
        go_ext = padded([go_t] + three_terms(-delta), tile)
        query = padded([query_t], tile).T
        go = padded([go_t], tile).T

        def key_tile(key_number, total):
            band = pl.ds(pl.multiple_of(key_number * tile, tile), tile)
            key_at = pl.multiple_of((key_number % per_part) * tile, tile)
            keys_t = qkv_ref[key_number // per_part, HD : 2 * HD, pl.ds(key_at, tile)]
            weights = jnp.exp(dot(key_scr[band, :], query_ext))
            slopes = (weights * dot(value_scr[band, :], go_ext)).astype(bf16)
            value_grad[band, :] += dot(weights.astype(bf16), go)
            key_grad[band, :] += dot(slopes, query)
            return total + dot(keys_t, slopes)

        grad = lax.fori_loop(
            starts_ref[number * per_tile] // per_tile,
            number + 1,
            key_tile,
            jnp.zeros((HD, tile), f32),
        )
        grad_ref[source, 0:HD, pl.ds(at, tile)] = (grad * scale_ref[...]).astype(bf16)
        return dim_total + jnp.sum(grad * query_t.astype(f32), axis=1, keepdims=True)

    dim_ref[...] = lax.fori_loop(0, tokens // tile, query_tile, jnp.zeros((HD, 1), f32))
    for number in range(tokens // tile):
        source, at = divmod(number, per_part)
        columns = slice(at * tile, (at + 1) * tile)
        band = slice(number * tile, (number + 1) * tile)
        grad_ref[source, HD : 2 * HD, columns] = key_grad[band, :].T[:HD].astype(bf16)
        grad_ref[source, 2 * HD : 3 * HD, columns] = value_grad[band, :].T[:HD].astype(bf16)
    half = pieces[0].shape[1]
    for number, piece in enumerate(pieces):
        flip, at = number % rows, number // rows
        piece[...] = grad_ref[
            jnp.bitwise_xor(place_ref[0], flip), :, at * half : (at + 1) * half
        ]


in_vmem = pl.BlockSpec(memory_space=pltpu.VMEM)
in_smem = pl.BlockSpec(memory_space=pltpu.SMEM)


def attend(starts, place, pieces, rows, part, tile, width):
    tokens = rows * part
    return pl.pallas_call(
        functools.partial(forward_kernel, tokens=tokens, part=part, tile=tile, rows=rows),
        out_shape=(
            jax.ShapeDtypeStruct((rows, HD, part), f32),
            jax.ShapeDtypeStruct((rows, 1, part), f32),
            jax.ShapeDtypeStruct((rows, 3 * HD, part), bf16),
            jax.ShapeDtypeStruct((tokens // width, HD, width), bf16),
        ),
        in_specs=[in_smem] * 2 + [in_vmem] * len(pieces),
        out_specs=(in_vmem,) * 4,
        scratch_shapes=[pltpu.VMEM((tokens, LANES), bf16)],
        compiler_params=pltpu.CompilerParams(vmem_limit_bytes=60 << 20),
        cost_estimate=pl.CostEstimate(
            flops=3 * LANES * tokens * tokens,
            bytes_accessed=12 << 20,
            transcendentals=tokens * tokens // 3,
        ),
    )(starts, place, *pieces)


def attend_back(starts, place, scale, qkv, go, out, lse, tile, half):
    rows, _, part = qkv.shape
    tokens = rows * part
    count = rows * (part // half)
    results = pl.pallas_call(
        functools.partial(backward_kernel, tokens=tokens, part=part, tile=tile, rows=rows),
        out_shape=(jax.ShapeDtypeStruct((3 * HD, half), bf16),) * count
        + (jax.ShapeDtypeStruct((HD, 1), f32),),
        in_specs=[in_smem] * 2 + [in_vmem] * 5,
        out_specs=(in_vmem,) * (count + 1),
        scratch_shapes=[pltpu.VMEM((rows, 3 * HD, part), bf16)]
        + [pltpu.VMEM((tokens, LANES), bf16)] * 2
        + [pltpu.VMEM((tokens, LANES), f32)] * 2,
        compiler_params=pltpu.CompilerParams(vmem_limit_bytes=60 << 20),
        cost_estimate=pl.CostEstimate(
            flops=8 * LANES * tokens * tokens,
            bytes_accessed=16 << 20,
            transcendentals=tokens * tokens // 3,
        ),
    )(starts, place, scale.reshape(HD, 1), qkv, go, out, lse)
    return results[:-1], results[-1]


def assemble_kernel(here_ref, place_ref, group_ref, *refs, cols, splits):
    blocks, out_ref = refs[:-1], refs[-1]
    part = out_ref.shape[1] // len(blocks)
    width = out_ref.shape[2] // cols
    for number, block in enumerate(blocks):
        row = jnp.bitwise_xor(place_ref[0], number // splits)
        piece = jnp.bitwise_xor(group_ref[0], number % splits)
        band = pl.ds(pl.multiple_of((row * splits + piece) * part, 16), part)
        for col in range(cols):
            value = block[lax.rem(here_ref[0] + cols - col, cols), 0:part, :]
            for matrix in range(3):
                out_ref[matrix, band, col * width : (col + 1) * width] = value[
                    :, matrix * width : (matrix + 1) * width
                ]


def unrolled(count, body, value):
    for number in range(count):
        value = body(number, value)
    return value


def feed_kernel(
    here_ref,
    place_ref,
    att_ref,
    normed_ref,
    inverse_ref,
    gains_ref,
    w_hbm,
    *refs,
    rows,
    cols,
    heads,
    twins,
    order,
):
    go_pieces, change_pieces = refs[:cols], refs[cols : 2 * cols]
    back_ref, gain_ref, leave_ref, rhs_ref = refs[2 * cols : 2 * cols + 4]
    lhs_refs = refs[2 * cols + 4 : -12]
    (
        w_ref,
        attended,
        normed_two,
        branch_grad,
        go_ref,
        branch,
        middle,
        grad_two,
        flipped,
        flipped_go,
        grad_att,
        done,
    ) = refs[-12:]
    width, sub = go_pieces[0].shape
    copies = [
        pltpu.make_async_copy(w_hbm.at[number], w_ref.at[number], done.at[number])
        for number in range(3)
    ]
    for copy in copies:
        copy.start()

    def ring(shift):
        return pl.ds(pl.multiple_of(lax.rem(here_ref[0] + shift, cols) * width, 16), width)

    for number, piece in enumerate(go_pieces):
        go_ref[ring(cols - number), :] = piece[...]
    step = 256
    for col in range(cols):
        for head in range(heads):
            at = (col * heads + head) * HD
            attended[at : at + HD, :] = att_ref[head * twins * cols + col]
    inverse = inverse_ref[...]
    copies[0].wait()

    def part(number):
        return pl.ds(number * step, step)

    def first(number, total):
        at = part(number)
        here = dot(w_ref[0, at, :], attended[...])
        branch[at, :] = here
        mid = normed_ref[at, :].astype(f32) / (inverse * gains_ref[at, 0:1]) + here
        middle[at, :] = mid
        flipped_go[:, at] = go_ref[at, :].T
        rhs_ref[0, :, at] = attended[at, :].T
        return total + jnp.sum(mid * mid, axis=0, keepdims=True)

    steps = D // step
    total = unrolled(steps, first, jnp.zeros((1, sub), f32))
    inverse_two = lax.rsqrt(total / D + epsilon)
    copies[1].wait()
    copies[2].wait()

    def second(number, carried):
        at = part(number)
        value = (middle[at, :] * inverse_two * gains_ref[at, 1:2]).astype(bf16)
        normed_two[at, :] = value
        flipped[:, at] = value.T
        return carried

    unrolled(steps, second, 0)

    def third(number, carried):
        at = part(number)
        up_proj = dot(flipped[...], w_ref[1, :, at])
        sigmoid_up = jax.nn.sigmoid(up_proj)
        rhs_ref[2, :, at] = (up_proj * sigmoid_up).astype(bf16)
        grad_act = dot(flipped_go[...], w_ref[2, :, at])
        rhs_ref[1, :, at] = (
            grad_act * sigmoid_up * (1.0 + up_proj * (1.0 - sigmoid_up))
        ).astype(bf16)
        return carried

    unrolled(steps, third, 0)

    def fourth(number, along):
        at = part(number)
        branch[at, :] += dot_last(w_ref[2, at, :], rhs_ref[2])
        grad = dot_last(w_ref[1, at, :], rhs_ref[1])
        grad_two[at, :] = grad
        return along + jnp.sum(gains_ref[at, 1:2] * grad * middle[at, :], axis=0, keepdims=True)

    along = unrolled(steps, fourth, jnp.zeros((1, sub), f32))
    shrink = inverse_two * inverse_two * inverse_two * along / D

    def fifth(number, carried):
        at = part(number)
        grad = grad_two[at, :]
        mid = middle[at, :]
        back = inverse_two * gains_ref[at, 1:2] * grad - mid * shrink
        back_ref[at, :] = (back / (inverse * gains_ref[at, 0:1])).astype(bf16)
        gain_ref[at, :] = jnp.sum(grad * mid * inverse_two, axis=1, keepdims=True)
        value = (go_ref[at, :].astype(f32) + back).astype(bf16)
        branch_grad[at, :] = value
        flipped[:, at] = value.T
        return carried

    unrolled(steps, fifth, 0)

    def sixth(number, carried):
        at = part(number)
        grad_att[at, :] = dot(flipped[...], w_ref[0, :, at]).T.astype(bf16)
        return carried

    unrolled(steps, sixth, 0)
    for number, piece in enumerate(change_pieces):
        piece[...] = branch[ring(number), :].astype(bf16)
    share = D // rows
    for slot, (out, at) in enumerate(order):
        row = jnp.bitwise_xor(place_ref[0], slot) if len(lhs_refs) > 1 else slot
        band = pl.ds(pl.multiple_of(row * share, 16), share)
        for number, value in enumerate((branch_grad, normed_two, go_ref)):
            lhs_refs[out][at, number] = value[band, :]
    for row in range(rows):
        for col in range(cols):
            at = (col * heads + row // twins) * HD
            leave_ref[row * cols + col] = grad_att[at : at + HD, :]


def dot_last(left, right):
    return lax.dot_general(left, right, (((1,), (1,)), ((), ())), preferred_element_type=f32)


def weights_kernel(here_ref, group_ref, *refs, count, splits):
    operands, outs = refs[:count], refs[count:]
    cols, part, wide = outs[0].shape
    width = wide // 3
    for index, out in enumerate(outs):
        slot = index // splits
        piece = jnp.bitwise_xor(group_ref[0], index % splits)
        band = pl.ds(pl.multiple_of(piece * part, 16), part)
        for number in range(3):
            value = sum(
                dot(operands[at][slot, number, band, :], operands[at + 1][number])
                for at in range(0, count, 2)
            ).astype(bf16)
            for col in range(cols):
                place = lax.rem(col + cols - here_ref[0], cols)
                out[place, :, number * width : (number + 1) * width] = value[
                    :, col * width : (col + 1) * width
                ]


def assemble(here, place, group, blocks, splits):
    cols = blocks[0].shape[0]
    return pl.pallas_call(
        functools.partial(assemble_kernel, cols=cols, splits=splits),
        out_shape=jax.ShapeDtypeStruct((3, D, D), bf16),
        in_specs=[in_smem] * 3 + [in_vmem] * len(blocks),
        out_specs=in_vmem,
        compiler_params=pltpu.CompilerParams(vmem_limit_bytes=60 << 20),
        cost_estimate=pl.CostEstimate(flops=0, bytes_accessed=20 << 20, transcendentals=0),
    )(here, place, group, *blocks)


def feed_forward(
    here, place, attended, pieces, normed, inverse, gains, weights, rows, cols, heads, twins, shapes, order
):
    width, sub = pieces[0].shape
    results = pl.pallas_call(
        functools.partial(
            feed_kernel, rows=rows, cols=cols, heads=heads, twins=twins, order=order
        ),
        out_shape=(jax.ShapeDtypeStruct((width, sub), bf16),) * cols
        + (
            jax.ShapeDtypeStruct((D, sub), bf16),
            jax.ShapeDtypeStruct((D, 1), f32),
            jax.ShapeDtypeStruct((rows * cols, HD, sub), bf16),
            jax.ShapeDtypeStruct((3, sub, D), bf16),
        )
        + tuple(jax.ShapeDtypeStruct(shape, bf16) for shape in shapes),
        in_specs=[in_smem] * 2
        + [in_vmem] * 4
        + [pl.BlockSpec(memory_space=pl.ANY)]
        + [in_vmem] * cols,
        out_specs=(in_vmem,) * (cols + 4 + len(shapes)),
        scratch_shapes=[pltpu.VMEM((3, D, D), bf16)]
        + [pltpu.VMEM((D, sub), bf16)] * 4
        + [pltpu.VMEM((D, sub), f32)] * 3
        + [pltpu.VMEM((sub, D), bf16)] * 2
        + [pltpu.VMEM((D, sub), bf16), pltpu.SemaphoreType.DMA((3,))],
        compiler_params=pltpu.CompilerParams(vmem_limit_bytes=60 << 20),
        cost_estimate=pl.CostEstimate(
            flops=12 * D * D * sub, bytes_accessed=20 << 20, transcendentals=D * sub
        ),
    )(here, place, attended, normed, inverse, gains, weights, *pieces)
    return results[:cols], results[cols : cols + 4], results[cols + 4 :]


def weight_grads(here, group, pairs, cols, splits):
    slots, _, share, sub = pairs[0].shape
    count = slots * splits
    return pl.pallas_call(
        functools.partial(weights_kernel, count=len(pairs), splits=splits),
        out_shape=(jax.ShapeDtypeStruct((cols, share // splits, 3 * D // cols), bf16),) * count,
        in_specs=[in_smem] * 2 + [in_vmem] * len(pairs),
        out_specs=(in_vmem,) * count,
        compiler_params=pltpu.CompilerParams(vmem_limit_bytes=60 << 20),
        cost_estimate=pl.CostEstimate(
            flops=6 * D * D * sub, bytes_accessed=16 << 20, transcendentals=0
        ),
    )(here, group, *pairs)


def copies_kernel(place_ref, *refs):
    blocks, (whole, turned) = refs[:-2], refs[-2:]
    share = blocks[0].shape[0]
    for flip, block in enumerate(blocks):
        row = jnp.bitwise_xor(place_ref[0], flip)
        whole[pl.ds(pl.multiple_of(row * share, 16), share), :] = block[...]
    for number in range(D // LANES):
        at = slice(number * LANES, (number + 1) * LANES)
        turned[:, at] = whole[at, :].T


def projection_copies(place, blocks):
    share, wide = blocks[0].shape
    return pl.pallas_call(
        copies_kernel,
        out_shape=(
            jax.ShapeDtypeStruct((D, wide), bf16),
            jax.ShapeDtypeStruct((wide, D), bf16),
        ),
        in_specs=[in_smem] + [in_vmem] * len(blocks),
        out_specs=(in_vmem,) * 2,
        compiler_params=pltpu.CompilerParams(vmem_limit_bytes=60 << 20),
        cost_estimate=pl.CostEstimate(flops=0, bytes_accessed=8 << 20, transcendentals=0),
    )(place, *blocks)


def project_kernel(place_ref, turned_ref, factor_ref, normed_ref, *refs, rows, heads):
    outs, result = refs[:-1], refs[-1]
    for head in range(heads):
        at = slice(head * 3 * HD, (head + 1) * 3 * HD)
        value = dot(turned_ref[at, :], normed_ref[...]) * factor_ref[at, :]
        result[head] = value.astype(bf16)
    for flip, out in enumerate(outs):
        out[...] = result[jnp.bitwise_xor(place_ref[0], flip) // (rows // heads)]


def project(place, turned, factors, normed, rows, heads):
    half = normed.shape[1]
    return pl.pallas_call(
        functools.partial(project_kernel, rows=rows, heads=heads),
        out_shape=(jax.ShapeDtypeStruct((3 * HD, half), bf16),) * rows,
        in_specs=[in_smem] + [in_vmem] * 3,
        out_specs=(in_vmem,) * rows,
        scratch_shapes=[pltpu.VMEM((heads, 3 * HD, half), bf16)],
        compiler_params=pltpu.CompilerParams(vmem_limit_bytes=60 << 20),
        cost_estimate=pl.CostEstimate(
            flops=2 * D * turned.shape[0] * half, bytes_accessed=10 << 20, transcendentals=0
        ),
    )(place, turned, factors, normed)


def back_kernel(here_ref, place_ref, whole_ref, *refs, rows, cols, heads):
    normed, back_ref, pieces, (payload, grads) = refs[:2], refs[2], refs[3:-2], refs[-2:]
    half = normed[0].shape[1]
    width = D // cols
    sub = back_ref.shape[1]
    here = here_ref[0]
    gather_heads(place_ref, pieces, grads, heads)
    for number in range(2):
        along = jnp.zeros((1, half), f32)
        tokens = slice(number * half, (number + 1) * half)
        for col in range(cols):
            at = slice(col * width, (col + 1) * width)
            value = dot(whole_ref[at, :], grads[:, tokens])
            along += jnp.sum(value * normed[number][at, :].astype(f32), axis=0, keepdims=True)
            for quarter in range(half // sub):
                columns = slice(quarter * sub, (quarter + 1) * sub)
                into = slice(number * half + quarter * sub, number * half + (quarter + 1) * sub)
                mine = jnp.where(here == number * (half // sub) + quarter, 1.0, 0.0)
                payload[col, 0:width, into] = (
                    value[:, columns] + back_ref[at, :].astype(f32) * mine
                ).astype(bf16)
        tail = jnp.concatenate([along, jnp.zeros((15, half), f32)], axis=0).astype(bf16)
        for col in range(cols):
            payload[col, width : width + 16, tokens] = tail


def gather_heads(place_ref, pieces, grads, heads):
    for flip, piece in enumerate(pieces):
        head = jnp.bitwise_xor(place_ref[0], flip) // (len(pieces) // heads)
        grads[pl.ds(pl.multiple_of(head * 3 * HD, 16), 3 * HD), :] = piece[...]


def project_back(here, place, whole, normed, back, pieces, rows, cols, heads):
    count = 2 * normed[0].shape[1]
    width = D // cols
    return pl.pallas_call(
        functools.partial(back_kernel, rows=rows, cols=cols, heads=heads),
        out_shape=jax.ShapeDtypeStruct((cols, width + 16, count), bf16),
        in_specs=[in_smem] * 2 + [in_vmem] * (4 + rows),
        out_specs=in_vmem,
        scratch_shapes=[pltpu.VMEM((3 * width, count), bf16)],
        compiler_params=pltpu.CompilerParams(vmem_limit_bytes=60 << 20),
        cost_estimate=pl.CostEstimate(
            flops=2 * D * 3 * width * count, bytes_accessed=16 << 20, transcendentals=0
        ),
    )(here, place, whole, *normed, back, *pieces)


def projection_grads_kernel(place_ref, whole_ref, *refs, order, heads):
    outs, (gain_ref, grads) = refs[-2 - (1 + max(out for out, _ in order)) : -2], refs[-2:]
    normed, pieces = refs[:2], refs[2 : -2 - len(outs)]
    half = normed[0].shape[1]
    gather_heads(place_ref, pieces, grads, heads)
    share = outs[0].shape[1]
    for slot, (out, at) in enumerate(order):
        row = jnp.bitwise_xor(place_ref[0], slot) if len(outs) > 1 else slot
        band = pl.ds(pl.multiple_of(row * share, 16), share)
        value = dot_last(normed[0][band, :], grads[:, :half]) + dot_last(
            normed[1][band, :], grads[:, half:]
        )
        gain_ref[band, :] = jnp.sum(value * whole_ref[band, :].astype(f32), axis=1, keepdims=True)
        outs[out][at] = value.astype(bf16)


def projection_grads(place, whole, normed, pieces, heads, shapes, order):
    half = normed[0].shape[1]
    return pl.pallas_call(
        functools.partial(projection_grads_kernel, order=order, heads=heads),
        out_shape=tuple(jax.ShapeDtypeStruct(shape, bf16) for shape in shapes)
        + (jax.ShapeDtypeStruct((D, 1), f32),),
        in_specs=[in_smem] + [in_vmem] * (3 + len(pieces)),
        out_specs=(in_vmem,) * (len(shapes) + 1),
        scratch_shapes=[pltpu.VMEM((whole.shape[1], 2 * half), bf16)],
        compiler_params=pltpu.CompilerParams(vmem_limit_bytes=60 << 20),
        cost_estimate=pl.CostEstimate(
            flops=4 * D * whole.shape[1] * half, bytes_accessed=12 << 20, transcendentals=0
        ),
    )(place, whole, *normed, *pieces)


def after(values, *others):
    return lax.optimization_barrier((values,) + others)[0]


def partner(values, flip, size, axis="row"):
    return lax.ppermute(values, axis, [(at, at ^ flip) for at in range(size)])


def plane(values, splits):
    result = [values[0]]
    for index in range(1, len(values)):
        flip, other = index // splits * 2, index % splits
        result.append(
            lax.ppermute(
                values[index],
                ("dp", "row"),
                [(at, at ^ (other * 4 + flip)) for at in range(splits * 4)],
            )
            if splits == 2
            else partner(values[index], flip, 4)
        )
    return result


def swapped(pieces, rows):
    return [pieces[0]] + [partner(pieces[flip], flip, rows) for flip in range(1, rows)]


def spread_rows(values, rows):
    if rows != 4:
        return swapped([values] * rows, rows)
    far = partner(values, 2, rows)
    return [values, partner(values, 1, rows), far, partner(far, 1, rows)]


def add(left, right):
    return left.astype(f32) + right.astype(f32)


def total(values, axes):
    for axis, size in axes:
        flip = 1
        while flip < size:
            values = values + partner(values, flip, size, axis)
            flip *= 2
    return values


def sum_groups(values, groups):
    if groups == 2:
        return add(values, partner(values, 1, 2, "dp"))
    return lax.psum(values, "dp").astype(f32)


def ring_swap(pieces, cols):
    return [pieces[0]] + [
        lax.ppermute(pieces[shift], "col", [(at, (at + shift) % cols) for at in range(cols)])
        for shift in range(1, cols)
    ]


def on_device(
    groups, rows, cols, residual_in, seq_ids, norm1_gain, w_qkv, per_dim, w_out, norm2_gain, w_up, w_down, out_grad
):
    count, width = residual_in.shape
    heads = width // HD
    twins = rows // heads
    sub = count // cols
    half = count // 2
    share = w_qkv.shape[0]
    tile = 768 if count % 768 == 0 else BLK
    back_tile = 512 if count % 512 == 0 else tile
    here = lax.axis_index("col")
    place = lax.axis_index("row")
    here_of, place_of = here[None].astype(jnp.int32), place[None].astype(jnp.int32)

    block_seq = seq_ids[::BLK]
    starts = jnp.sum((block_seq[None, :] < block_seq[:, None]).astype(jnp.int32), axis=1)

    residual = residual_in.T
    squares = jnp.sum(residual * residual, axis=0)
    squares = squares + partner(squares, 1, cols, "col")
    inverse_one = lax.rsqrt((squares + partner(squares, 2, cols, "col")) / D + epsilon)[None, :]
    normed = (residual * inverse_one * norm1_gain[:, None]).astype(bf16)
    qkv_local = w_qkv.astype(bf16).reshape(share, 3, heads, HD).transpose(0, 2, 1, 3)
    qkv_local = qkv_local.reshape(share, heads * 3 * HD)
    whole, turned = projection_copies(place_of, spread_rows(qkv_local, rows))
    scale = jax.nn.softplus(per_dim) * scale_base / math.sqrt(HD)
    factors = jnp.tile(jnp.concatenate([scale, jnp.ones((2 * HD,), f32)]), heads)[:, None]
    stacked = jnp.concatenate(
        [w_out.T, w_up, w_down.T], axis=1
    ).astype(bf16)
    gains = [jnp.concatenate(three_terms(gain))[None] for gain in (norm1_gain, norm2_gain)]
    splits = 2 if groups == 2 and rows == 4 else 1
    part = share // splits
    group_of = jnp.zeros((1,), jnp.int32)
    if splits == 2:
        group = lax.axis_index("dp")
        group_of = group[None].astype(jnp.int32)
        stacked = lax.dynamic_slice_in_dim(stacked, group * part, part, 0)
    stacked = jnp.concatenate([stacked] + gains + [jnp.zeros((14, 3 * width), bf16)], axis=0)
    gathered = jnp.stack(ring_swap([after(stacked, turned)] * cols, cols))
    gains = gathered[:, part : part + 2].astype(f32).reshape(cols, 2, 3, width).sum(axis=2)
    gains = jnp.concatenate(
        [
            lax.dynamic_index_in_dim(gains, lax.rem(here + cols - col, cols), 0, keepdims=False)
            for col in range(cols)
        ],
        axis=1,
    ).T
    near = [gathered]
    if rows == 4:
        if splits == 2:
            near.append(partner(gathered, 1, 2, "dp"))
        near.append(partner(gathered, 2, rows))
        if splits == 2:
            near.append(partner(after(near[2], near[1]), 1, 2, "dp"))

    out_grad_t = out_grad.T.astype(bf16)

    def quarter(values, shift):
        at = lax.rem(here + shift, cols) * sub
        return lax.dynamic_slice_in_dim(values, at, sub, 1)

    grad_pieces = [quarter(out_grad_t, shift) for shift in range(cols)]

    pieces, normed_parts = [], []
    for at in range(2):
        part = normed[:, at * half : (at + 1) * half]
        if at:
            part = after(part, turned, *grad_pieces)
        normed_parts.append(lax.all_gather(part, "col", axis=0, tiled=True))
        outs = project(place_of, turned, factors, normed_parts[at], rows, heads)
        pieces += swapped(outs, rows)

    tidy = sub % LANES == 0
    if rows == 4:
        pieces[0] = after(pieces[0], *near[1:3])
    result, lse, qkv_heads, leaving = attend(
        starts, place_of, pieces, rows, count, tile, sub if tidy else count
    )
    if rows == 4:
        near = [after(value, lse) for value in near]
        other = [partner(value, 1, rows) for value in near]
        blocks = near[:splits] + other[:splits] + near[splits:] + other[splits:]
    else:
        blocks = spread_rows(gathered, rows)
    weights = assemble(here_of, place_of, group_of, blocks, splits)
    grad_pieces = ring_swap(grad_pieces, cols)

    if not tidy:
        leaving = leaving.reshape(rows, HD, cols, sub).transpose(0, 2, 1, 3)
        leaving = leaving.reshape(rows * cols, HD, sub)
    leaving = after(leaving, *grad_pieces)
    arrived = lax.all_to_all(leaving, ("row", "col"), 0, 0, tiled=True)

    own_inverse = quarter(inverse_one, 0)
    own_at = lax.rem(here, cols // 2) * sub
    own_normed = jnp.where(
        here < cols // 2,
        lax.dynamic_slice_in_dim(normed_parts[0], own_at, sub, 1),
        lax.dynamic_slice_in_dim(normed_parts[1], own_at, sub, 1),
    )
    wide = (share, 3 * width)
    pairwise = ((0, 0), (1, 0), (0, 1), (1, 1))
    natural = tuple((0, row) for row in range(rows))
    order, slots = (pairwise, 2) if rows == 4 else (natural, rows)
    change, (back_two, gain_two_part, leaving, rhs), lhs = feed_forward(
        here_of,
        place_of,
        arrived,
        grad_pieces,
        own_normed,
        own_inverse,
        gains,
        weights,
        rows,
        cols,
        heads,
        twins,
        ((slots, 3, share, sub),) * (rows // slots),
        order,
    )

    go = lax.all_to_all(leaving, ("row", "col"), 0, 0, tiled=True)
    if not tidy:
        go = go.reshape(rows, cols, HD, sub).transpose(0, 2, 1, 3).reshape(rows, HD, count)

    if rows == 4:
        pairs = [lhs[0], rhs, partner(lhs[1], 1, rows), partner(rhs, 1, rows)]
        mine = weight_grads(here_of, group_of, pairs, cols, splits)
        go = after(go, *mine)
        mine = plane(mine, splits)
    else:
        mine = jnp.stack(weight_grads(here_of, group_of, [lhs[0], rhs], cols, 1))
        mine = lax.psum_scatter(mine, "row", scatter_dimension=0, tiled=False)

    pieces, dim_part = attend_back(
        starts, place_of, scale, qkv_heads, go, result, lse, back_tile, count
    )
    arrived = swapped(pieces, rows)

    if rows == 4:
        mine = sum(after(value, arrived[1]).astype(f32) for value in mine).astype(bf16)
    mine = ring_swap([mine[shift] for shift in range(cols)], cols)
    mine = sum(value.astype(f32) for value in mine).astype(bf16)
    if splits == 2:
        mine = jnp.stack([mine, partner(mine, 1, 2, "dp")])
        shard = jnp.where(group == 0, mine, mine[::-1]).reshape(wide).astype(f32)
    else:
        shard = sum_groups(mine, groups)

    arrived[0] = after(arrived[0], mine)
    payload = project_back(
        here_of, place_of, whole, normed_parts, back_two, arrived, rows, cols, heads
    )
    summed = lax.psum_scatter(payload, "col", scatter_dimension=0, tiled=False).astype(f32)

    own_head = (place % twins == 0).astype(f32)
    *parts, gain_one_part = projection_grads(
        place_of,
        after(whole, payload),
        normed_parts,
        arrived,
        heads,
        ((slots,) + wide,) * (rows // slots),
        order,
    )
    small = jnp.concatenate([gain_one_part, gain_two_part, dim_part * own_head])[:, 0]
    if rows == 4:
        kept, sent = parts
        arrived = partner(sent, 1, rows)
        far = partner(add(kept[1], arrived[1]).astype(bf16), 2, rows)
        mine = (add(kept[0], arrived[0]) + far.astype(f32)).astype(bf16)
    else:
        mine = lax.psum_scatter(parts[0], "row", scatter_dimension=0, tiled=False)
    qkv_grad = sum_groups(mine, groups)
    qkv_grad = qkv_grad.reshape(share, heads, 3, HD).transpose(0, 2, 1, 3).reshape(share, 3, width)
    small = total(small, (("row", rows), ("dp", groups), ("col", cols)))
    gain_one_grad = lax.dynamic_slice_in_dim(small[:D], here * width, width) / norm1_gain
    gain_two_grad = lax.dynamic_slice_in_dim(small[D : 2 * D], here * width, width)
    scale_grad = small[2 * D :] / scale * (scale_base / math.sqrt(HD)) * jax.nn.sigmoid(per_dim)

    change = ring_swap(
        [after(piece, go if at % 2 else payload) for at, piece in enumerate(change)], cols
    )
    output = jnp.zeros_like(residual_in)
    for shift, piece in enumerate(change):
        at = lax.rem(here + cols - shift, cols) * sub
        piece = lax.dynamic_slice_in_dim(residual_in, at, sub, 0) + piece.astype(f32).T
        output = lax.dynamic_update_slice_in_dim(output, piece, at, 0)

    grad_one, along_one = summed[:width], summed[width : width + 1]
    back_one = inverse_one * norm1_gain[:, None] * grad_one - residual * inverse_one**2 * (
        along_one / D
    )
    input_grad = out_grad + back_one.T
    return (
        output,
        input_grad,
        gain_one_grad,
        qkv_grad,
        scale_grad,
        shard[:, :width].T,
        gain_two_grad,
        shard[:, width : 2 * width],
        shard[:, 2 * width :].T,
    )


def solution(mesh):
    in_specs = (
        P(("dp", "row"), "col"),
        P("dp"),
        P("col"),
        P("row", None, "col"),
        P(),
        P("col", "row"),
        P("col"),
        P("row", "col"),
        P("col", "row"),
        P(("dp", "row"), "col"),
    )
    out_specs = (
        P(("dp", "row"), "col"),
        P(("dp", "row"), "col"),
        P("col"),
        P("row", None, "col"),
        P(),
        P("col", "row"),
        P("col"),
        P("row", "col"),
        P("col", "row"),
    )
    return jax.shard_map(
        functools.partial(on_device, mesh.shape["dp"], mesh.shape["row"], mesh.shape["col"]),
        mesh=mesh,
        in_specs=in_specs,
        out_specs=out_specs,
        check_vma=False,
    )
```

```python
import functools
import math

import jax
import jax.numpy as jnp
from jax import lax
from jax.experimental import pallas as pl
from jax.experimental.pallas import tpu as pltpu
from jax.sharding import PartitionSpec as P

D = 1280
HD = 80
BLK = 256
LANES = 128

epsilon = 1e-06
scale_base = 1.442695041
excluded = -1e30

bf16 = jnp.bfloat16
f32 = jnp.float32


def dot(left, right):
    return jnp.dot(left, right, preferred_element_type=f32)


def product(form, left, right):
    return jnp.einsum(form, left, right, preferred_element_type=f32)


def three_terms(values):
    high = values.astype(bf16)
    rest = values - high.astype(f32)
    middle = rest.astype(bf16)
    return [high, middle, (rest - middle.astype(f32)).astype(bf16)]


def block_bias(starts_ref, first_block, width, block_count):
    shape = (block_count, width)
    block = lax.broadcasted_iota(jnp.int32, shape, 0)
    own = lax.broadcasted_iota(jnp.int32, shape, 1) // BLK
    start = jnp.zeros(shape, jnp.int32)
    for number in range(width // BLK):
        start = jnp.where(own == number, starts_ref[first_block + number], start)
    return jnp.where((block >= start) & (block <= first_block + own), 0.0, excluded).astype(bf16)


def extended(top, width, block_count, first_block, extra):
    row = lax.broadcasted_iota(jnp.int32, (LANES - HD, width), 0)
    block = first_block + lax.broadcasted_iota(jnp.int32, (LANES - HD, width), 1) // BLK
    marks = (row >= block_count) & (row < block_count + extra)
    if block_count:
        marks = marks | (row == block)
    return jnp.concatenate([top, jnp.where(marks, 1.0, 0.0).astype(bf16)], axis=0).T


def padded(parts, width):
    used = sum(part.shape[0] for part in parts)
    return jnp.concatenate(list(parts) + [jnp.zeros((LANES - used, width), bf16)], axis=0)


def store_pieces(ref, value, source, number, part):
    width, tile = ref.shape[2], value.shape[1]
    if width >= tile:
        ref[source * (part // width), :, pl.ds(pl.multiple_of(number * tile, tile), tile)] = value
        return
    first = source * (part // width) + number * (tile // width)
    for at in range(tile // width):
        ref[first + at] = value[:, at * width : (at + 1) * width]


def load_pieces(ref, source, number, part, tile):
    width = ref.shape[2]
    if width >= tile:
        return ref[source * (part // width), :, pl.ds(pl.multiple_of(number * tile, tile), tile)]
    grain = math.gcd(width, tile)
    chunks = []
    for at in range(tile // grain):
        start = number * tile + at * grain
        column = pl.multiple_of(lax.rem(start, width), grain)
        chunks.append(ref[source * (part // width) + start // width, :, pl.ds(column, grain)])
    return jnp.concatenate(chunks, axis=1)


def forward_kernel(starts_ref, place_ref, *refs, tokens, part, tile, rows):
    pieces = refs[: -5]
    out_ref, lse_ref, qkv_ref, leave_ref, key_scr = refs[-5:]
    half = pieces[0].shape[1]
    for number, piece in enumerate(pieces):
        flip, at = number % rows, number // rows
        qkv_ref[jnp.bitwise_xor(place_ref[0], flip), :, at * half : (at + 1) * half] = piece[...]
    block_count = tokens // BLK
    per_part = part // tile
    per_tile = tile // BLK
    for number in range(tokens // tile):
        source, at = divmod(number, per_part)
        key_scr[number * tile : (number + 1) * tile, :] = extended(
            qkv_ref[source, HD : 2 * HD, at * tile : (at + 1) * tile],
            tile,
            block_count,
            number * per_tile,
            0,
        )

    def query_tile(number, carried):
        source = number // per_part
        at = pl.multiple_of((number % per_part) * tile, tile)
        bias = block_bias(starts_ref, number * per_tile, tile, block_count)
        query = padded([qkv_ref[source, 0:HD, pl.ds(at, tile)], bias], tile)

        def key_tile(key_number, state):
            largest, total, result = state
            keys = key_scr[pl.ds(pl.multiple_of(key_number * tile, tile), tile), :]
            scores = dot(keys, query)
            key_at = pl.multiple_of((key_number % per_part) * tile, tile)
            values = qkv_ref[key_number // per_part, 2 * HD : 3 * HD, pl.ds(key_at, tile)]
            newest = jnp.maximum(largest, jnp.max(scores, axis=0, keepdims=True))
            factor = jnp.exp(largest - newest)
            weights = jnp.exp(scores - newest)
            total = total * factor + jnp.sum(weights, axis=0, keepdims=True)
            result = result * factor + dot(values, weights.astype(bf16))
            return newest, total, result

        largest, total, result = lax.fori_loop(
            starts_ref[number * per_tile] // per_tile,
            number + 1,
            key_tile,
            (
                jnp.full((1, tile), -jnp.inf, f32),
                jnp.zeros((1, tile), f32),
                jnp.zeros((HD, tile), f32),
            ),
        )
        result = result / total
        out_ref[source, :, pl.ds(at, tile)] = result
        store_pieces(leave_ref, result.astype(bf16), source, number % per_part, part)
        lse_ref[source, :, pl.ds(at, tile)] = largest + jnp.log(total)
        return carried

    lax.fori_loop(0, tokens // tile, query_tile, 0)


def backward_kernel(
    starts_ref,
    place_ref,
    scale_ref,
    qkv_ref,
    go_ref,
    out_ref,
    lse_ref,
    *refs,
    tokens,
    part,
    tile,
    rows,
):
    pieces = refs[: -6]
    dim_ref, grad_ref, key_scr, value_scr, key_grad, value_grad = refs[-6:]
    block_count = tokens // BLK
    per_part = part // tile
    per_tile = tile // BLK
    for number in range(tokens // tile):
        source, at = divmod(number, per_part)
        columns = slice(at * tile, (at + 1) * tile)
        band = slice(number * tile, (number + 1) * tile)
        key_scr[band, :] = extended(
            qkv_ref[source, HD : 2 * HD, columns], tile, block_count, number * per_tile, 3
        )
        value_scr[band, :] = extended(qkv_ref[source, 2 * HD : 3 * HD, columns], tile, 0, 0, 3)
    key_grad[...] = jnp.zeros_like(key_grad)
    value_grad[...] = jnp.zeros_like(value_grad)

    def query_tile(number, dim_total):
        source = number // per_part
        at = pl.multiple_of((number % per_part) * tile, tile)
        query_t = qkv_ref[source, 0:HD, pl.ds(at, tile)]
        go_t = load_pieces(go_ref, source, number % per_part, part, tile)
        delta = jnp.sum(
            go_t.astype(f32) * out_ref[source, :, pl.ds(at, tile)], axis=0, keepdims=True
        )
        lse = lse_ref[source, :, pl.ds(at, tile)]
        bias = block_bias(starts_ref, number * per_tile, tile, block_count)
        query_ext = padded([query_t, bias] + three_terms(-lse), tile)
        go_ext = padded([go_t] + three_terms(-delta), tile)
        query = padded([query_t], tile).T
        go = padded([go_t], tile).T

        def key_tile(key_number, total):
            band = pl.ds(pl.multiple_of(key_number * tile, tile), tile)
            key_at = pl.multiple_of((key_number % per_part) * tile, tile)
            keys_t = qkv_ref[key_number // per_part, HD : 2 * HD, pl.ds(key_at, tile)]
            weights = jnp.exp(dot(key_scr[band, :], query_ext))
            slopes = (weights * dot(value_scr[band, :], go_ext)).astype(bf16)
            value_grad[band, :] += dot(weights.astype(bf16), go)
            key_grad[band, :] += dot(slopes, query)
            return total + dot(keys_t, slopes)

        grad = lax.fori_loop(
            starts_ref[number * per_tile] // per_tile,
            number + 1,
            key_tile,
            jnp.zeros((HD, tile), f32),
        )
        grad_ref[source, 0:HD, pl.ds(at, tile)] = (grad * scale_ref[...]).astype(bf16)
        return dim_total + jnp.sum(grad * query_t.astype(f32), axis=1, keepdims=True)

    dim_ref[...] = lax.fori_loop(0, tokens // tile, query_tile, jnp.zeros((HD, 1), f32))
    for number in range(tokens // tile):
        source, at = divmod(number, per_part)
        columns = slice(at * tile, (at + 1) * tile)
        band = slice(number * tile, (number + 1) * tile)
        grad_ref[source, HD : 2 * HD, columns] = key_grad[band, :].T[:HD].astype(bf16)
        grad_ref[source, 2 * HD : 3 * HD, columns] = value_grad[band, :].T[:HD].astype(bf16)
    half = pieces[0].shape[1]
    for number, piece in enumerate(pieces):
        flip, at = number % rows, number // rows
        piece[...] = grad_ref[
            jnp.bitwise_xor(place_ref[0], flip), :, at * half : (at + 1) * half
        ]


in_vmem = pl.BlockSpec(memory_space=pltpu.VMEM)
in_smem = pl.BlockSpec(memory_space=pltpu.SMEM)


def attend(starts, place, pieces, rows, part, tile, width):
    tokens = rows * part
    return pl.pallas_call(
        functools.partial(forward_kernel, tokens=tokens, part=part, tile=tile, rows=rows),
        out_shape=(
            jax.ShapeDtypeStruct((rows, HD, part), f32),
            jax.ShapeDtypeStruct((rows, 1, part), f32),
            jax.ShapeDtypeStruct((rows, 3 * HD, part), bf16),
            jax.ShapeDtypeStruct((tokens // width, HD, width), bf16),
        ),
        in_specs=[in_smem] * 2 + [in_vmem] * len(pieces),
        out_specs=(in_vmem,) * 4,
        scratch_shapes=[pltpu.VMEM((tokens, LANES), bf16)],
        compiler_params=pltpu.CompilerParams(vmem_limit_bytes=60 << 20),
        cost_estimate=pl.CostEstimate(
            flops=3 * LANES * tokens * tokens,
            bytes_accessed=12 << 20,
            transcendentals=tokens * tokens // 3,
        ),
    )(starts, place, *pieces)


def attend_back(starts, place, scale, qkv, go, out, lse, tile, half):
    rows, _, part = qkv.shape
    tokens = rows * part
    count = rows * (part // half)
    results = pl.pallas_call(
        functools.partial(backward_kernel, tokens=tokens, part=part, tile=tile, rows=rows),
        out_shape=(jax.ShapeDtypeStruct((3 * HD, half), bf16),) * count
        + (jax.ShapeDtypeStruct((HD, 1), f32),),
        in_specs=[in_smem] * 2 + [in_vmem] * 5,
        out_specs=(in_vmem,) * (count + 1),
        scratch_shapes=[pltpu.VMEM((rows, 3 * HD, part), bf16)]
        + [pltpu.VMEM((tokens, LANES), bf16)] * 2
        + [pltpu.VMEM((tokens, LANES), f32)] * 2,
        compiler_params=pltpu.CompilerParams(vmem_limit_bytes=60 << 20),
        cost_estimate=pl.CostEstimate(
            flops=8 * LANES * tokens * tokens,
            bytes_accessed=16 << 20,
            transcendentals=tokens * tokens // 3,
        ),
    )(starts, place, scale.reshape(HD, 1), qkv, go, out, lse)
    return results[:-1], results[-1]


def assemble_kernel(here_ref, place_ref, group_ref, *refs, cols, splits):
    blocks, out_ref = refs[:-1], refs[-1]
    part = out_ref.shape[1] // len(blocks)
    width = out_ref.shape[2] // cols
    for number, block in enumerate(blocks):
        row = jnp.bitwise_xor(place_ref[0], number // splits)
        piece = jnp.bitwise_xor(group_ref[0], number % splits)
        band = pl.ds(pl.multiple_of((row * splits + piece) * part, 16), part)
        for col in range(cols):
            value = block[lax.rem(here_ref[0] + cols - col, cols), 0:part, :]
            for matrix in range(3):
                out_ref[matrix, band, col * width : (col + 1) * width] = value[
                    :, matrix * width : (matrix + 1) * width
                ]


def unrolled(count, body, value):
    for number in range(count):
        value = body(number, value)
    return value


def feed_kernel(
    here_ref,
    place_ref,
    att_ref,
    normed_ref,
    inverse_ref,
    gains_ref,
    w_hbm,
    *refs,
    rows,
    cols,
    heads,
    twins,
    order,
):
    go_pieces, change_pieces = refs[:cols], refs[cols : 2 * cols]
    back_ref, gain_ref, leave_ref, rhs_ref = refs[2 * cols : 2 * cols + 4]
    lhs_refs = refs[2 * cols + 4 : -12]
    (
        w_ref,
        attended,
        normed_two,
        branch_grad,
        go_ref,
        branch,
        middle,
        grad_two,
        flipped,
        flipped_go,
        grad_att,
        done,
    ) = refs[-12:]
    width, sub = go_pieces[0].shape
    copies = [
        pltpu.make_async_copy(w_hbm.at[number], w_ref.at[number], done.at[number])
        for number in range(3)
    ]
    for copy in copies:
        copy.start()

    def ring(shift):
        return pl.ds(pl.multiple_of(lax.rem(here_ref[0] + shift, cols) * width, 16), width)

    for number, piece in enumerate(go_pieces):
        go_ref[ring(cols - number), :] = piece[...]
    step = 256
    for col in range(cols):
        for head in range(heads):
            at = (col * heads + head) * HD
            attended[at : at + HD, :] = att_ref[head * twins * cols + col]
    inverse = inverse_ref[...]
    copies[0].wait()

    def part(number):
        return pl.ds(number * step, step)

    def first(number, total):
        at = part(number)
        here = dot(w_ref[0, at, :], attended[...])
        branch[at, :] = here
        mid = normed_ref[at, :].astype(f32) / (inverse * gains_ref[at, 0:1]) + here
        middle[at, :] = mid
        flipped_go[:, at] = go_ref[at, :].T
        rhs_ref[0, :, at] = attended[at, :].T
        return total + jnp.sum(mid * mid, axis=0, keepdims=True)

    steps = D // step
    total = unrolled(steps, first, jnp.zeros((1, sub), f32))
    inverse_two = lax.rsqrt(total / D + epsilon)
    copies[1].wait()
    copies[2].wait()

    def second(number, carried):
        at = part(number)
        value = (middle[at, :] * inverse_two * gains_ref[at, 1:2]).astype(bf16)
        normed_two[at, :] = value
        flipped[:, at] = value.T
        return carried

    unrolled(steps, second, 0)

    def third(number, carried):
        at = part(number)
        up_proj = dot(flipped[...], w_ref[1, :, at])
        sigmoid_up = jax.nn.sigmoid(up_proj)
        rhs_ref[2, :, at] = (up_proj * sigmoid_up).astype(bf16)
        grad_act = dot(flipped_go[...], w_ref[2, :, at])
        rhs_ref[1, :, at] = (
            grad_act * sigmoid_up * (1.0 + up_proj * (1.0 - sigmoid_up))
        ).astype(bf16)
        return carried

    unrolled(steps, third, 0)

    def fourth(number, along):
        at = part(number)
        branch[at, :] += dot_last(w_ref[2, at, :], rhs_ref[2])
        grad = dot_last(w_ref[1, at, :], rhs_ref[1])
        grad_two[at, :] = grad
        return along + jnp.sum(gains_ref[at, 1:2] * grad * middle[at, :], axis=0, keepdims=True)

    along = unrolled(steps, fourth, jnp.zeros((1, sub), f32))
    shrink = inverse_two * inverse_two * inverse_two * along / D

    def fifth(number, carried):
        at = part(number)
        grad = grad_two[at, :]
        mid = middle[at, :]
        back = inverse_two * gains_ref[at, 1:2] * grad - mid * shrink
        back_ref[at, :] = (back / (inverse * gains_ref[at, 0:1])).astype(bf16)
        gain_ref[at, :] = jnp.sum(grad * mid * inverse_two, axis=1, keepdims=True)
        value = (go_ref[at, :].astype(f32) + back).astype(bf16)
        branch_grad[at, :] = value
        flipped[:, at] = value.T
        return carried

    unrolled(steps, fifth, 0)

    def sixth(number, carried):
        at = part(number)
        grad_att[at, :] = dot(flipped[...], w_ref[0, :, at]).T.astype(bf16)
        return carried

    unrolled(steps, sixth, 0)
    for number, piece in enumerate(change_pieces):
        piece[...] = branch[ring(number), :].astype(bf16)
    share = D // rows
    for slot, (out, at) in enumerate(order):
        row = jnp.bitwise_xor(place_ref[0], slot) if len(lhs_refs) > 1 else slot
        band = pl.ds(pl.multiple_of(row * share, 16), share)
        for number, value in enumerate((branch_grad, normed_two, go_ref)):
            lhs_refs[out][at, number] = value[band, :]
    for row in range(rows):
        for col in range(cols):
            at = (col * heads + row // twins) * HD
            leave_ref[row * cols + col] = grad_att[at : at + HD, :]


def dot_last(left, right):
    return lax.dot_general(left, right, (((1,), (1,)), ((), ())), preferred_element_type=f32)


def weights_kernel(here_ref, group_ref, *refs, count, splits):
    operands, outs = refs[:count], refs[count:]
    cols, part, wide = outs[0].shape
    width = wide // 3
    for index, out in enumerate(outs):
        slot = index // splits
        piece = jnp.bitwise_xor(group_ref[0], index % splits)
        band = pl.ds(pl.multiple_of(piece * part, 16), part)
        for number in range(3):
            value = sum(
                dot(operands[at][slot, number, band, :], operands[at + 1][number])
                for at in range(0, count, 2)
            ).astype(bf16)
            for col in range(cols):
                place = lax.rem(col + cols - here_ref[0], cols)
                out[place, :, number * width : (number + 1) * width] = value[
                    :, col * width : (col + 1) * width
                ]


def assemble(here, place, group, blocks, splits):
    cols = blocks[0].shape[0]
    return pl.pallas_call(
        functools.partial(assemble_kernel, cols=cols, splits=splits),
        out_shape=jax.ShapeDtypeStruct((3, D, D), bf16),
        in_specs=[in_smem] * 3 + [in_vmem] * len(blocks),
        out_specs=in_vmem,
        compiler_params=pltpu.CompilerParams(vmem_limit_bytes=60 << 20),
        cost_estimate=pl.CostEstimate(flops=0, bytes_accessed=20 << 20, transcendentals=0),
    )(here, place, group, *blocks)


def feed_forward(
    here, place, attended, pieces, normed, inverse, gains, weights, rows, cols, heads, twins, shapes, order
):
    width, sub = pieces[0].shape
    results = pl.pallas_call(
        functools.partial(
            feed_kernel, rows=rows, cols=cols, heads=heads, twins=twins, order=order
        ),
        out_shape=(jax.ShapeDtypeStruct((width, sub), bf16),) * cols
        + (
            jax.ShapeDtypeStruct((D, sub), bf16),
            jax.ShapeDtypeStruct((D, 1), f32),
            jax.ShapeDtypeStruct((rows * cols, HD, sub), bf16),
            jax.ShapeDtypeStruct((3, sub, D), bf16),
        )
        + tuple(jax.ShapeDtypeStruct(shape, bf16) for shape in shapes),
        in_specs=[in_smem] * 2
        + [in_vmem] * 4
        + [pl.BlockSpec(memory_space=pl.ANY)]
        + [in_vmem] * cols,
        out_specs=(in_vmem,) * (cols + 4 + len(shapes)),
        scratch_shapes=[pltpu.VMEM((3, D, D), bf16)]
        + [pltpu.VMEM((D, sub), bf16)] * 4
        + [pltpu.VMEM((D, sub), f32)] * 3
        + [pltpu.VMEM((sub, D), bf16)] * 2
        + [pltpu.VMEM((D, sub), bf16), pltpu.SemaphoreType.DMA((3,))],
        compiler_params=pltpu.CompilerParams(vmem_limit_bytes=60 << 20),
        cost_estimate=pl.CostEstimate(
            flops=12 * D * D * sub, bytes_accessed=20 << 20, transcendentals=D * sub
        ),
    )(here, place, attended, normed, inverse, gains, weights, *pieces)
    return results[:cols], results[cols : cols + 4], results[cols + 4 :]


def weight_grads(here, group, pairs, cols, splits):
    slots, _, share, sub = pairs[0].shape
    count = slots * splits
    return pl.pallas_call(
        functools.partial(weights_kernel, count=len(pairs), splits=splits),
        out_shape=(jax.ShapeDtypeStruct((cols, share // splits, 3 * D // cols), bf16),) * count,
        in_specs=[in_smem] * 2 + [in_vmem] * len(pairs),
        out_specs=(in_vmem,) * count,
        compiler_params=pltpu.CompilerParams(vmem_limit_bytes=60 << 20),
        cost_estimate=pl.CostEstimate(
            flops=6 * D * D * sub, bytes_accessed=16 << 20, transcendentals=0
        ),
    )(here, group, *pairs)


def copies_kernel(place_ref, *refs):
    blocks, (whole, turned) = refs[:-2], refs[-2:]
    share = blocks[0].shape[0]
    for flip, block in enumerate(blocks):
        row = jnp.bitwise_xor(place_ref[0], flip)
        whole[pl.ds(pl.multiple_of(row * share, 16), share), :] = block[...]
    for number in range(D // LANES):
        at = slice(number * LANES, (number + 1) * LANES)
        turned[:, at] = whole[at, :].T


def projection_copies(place, blocks):
    share, wide = blocks[0].shape
    return pl.pallas_call(
        copies_kernel,
        out_shape=(
            jax.ShapeDtypeStruct((D, wide), bf16),
            jax.ShapeDtypeStruct((wide, D), bf16),
        ),
        in_specs=[in_smem] + [in_vmem] * len(blocks),
        out_specs=(in_vmem,) * 2,
        compiler_params=pltpu.CompilerParams(vmem_limit_bytes=60 << 20),
        cost_estimate=pl.CostEstimate(flops=0, bytes_accessed=8 << 20, transcendentals=0),
    )(place, *blocks)


def project_kernel(place_ref, turned_ref, factor_ref, normed_ref, *refs, rows, heads):
    outs, result = refs[:-1], refs[-1]
    for head in range(heads):
        at = slice(head * 3 * HD, (head + 1) * 3 * HD)
        value = dot(turned_ref[at, :], normed_ref[...]) * factor_ref[at, :]
        result[head] = value.astype(bf16)
    for flip, out in enumerate(outs):
        out[...] = result[jnp.bitwise_xor(place_ref[0], flip) // (rows // heads)]


def project(place, turned, factors, normed, rows, heads):
    half = normed.shape[1]
    return pl.pallas_call(
        functools.partial(project_kernel, rows=rows, heads=heads),
        out_shape=(jax.ShapeDtypeStruct((3 * HD, half), bf16),) * rows,
        in_specs=[in_smem] + [in_vmem] * 3,
        out_specs=(in_vmem,) * rows,
        scratch_shapes=[pltpu.VMEM((heads, 3 * HD, half), bf16)],
        compiler_params=pltpu.CompilerParams(vmem_limit_bytes=60 << 20),
        cost_estimate=pl.CostEstimate(
            flops=2 * D * turned.shape[0] * half, bytes_accessed=10 << 20, transcendentals=0
        ),
    )(place, turned, factors, normed)


def back_kernel(here_ref, place_ref, whole_ref, *refs, rows, cols, heads):
    normed, back_ref, pieces, (payload, grads) = refs[:2], refs[2], refs[3:-2], refs[-2:]
    half = normed[0].shape[1]
    width = D // cols
    sub = back_ref.shape[1]
    here = here_ref[0]
    gather_heads(place_ref, pieces, grads, heads)
    for number in range(2):
        along = jnp.zeros((1, half), f32)
        tokens = slice(number * half, (number + 1) * half)
        for col in range(cols):
            at = slice(col * width, (col + 1) * width)
            value = dot(whole_ref[at, :], grads[:, tokens])
            along += jnp.sum(value * normed[number][at, :].astype(f32), axis=0, keepdims=True)
            for quarter in range(half // sub):
                columns = slice(quarter * sub, (quarter + 1) * sub)
                into = slice(number * half + quarter * sub, number * half + (quarter + 1) * sub)
                mine = jnp.where(here == number * (half // sub) + quarter, 1.0, 0.0)
                payload[col, 0:width, into] = (
                    value[:, columns] + back_ref[at, :].astype(f32) * mine
                ).astype(bf16)
        tail = jnp.concatenate([along, jnp.zeros((15, half), f32)], axis=0).astype(bf16)
        for col in range(cols):
            payload[col, width : width + 16, tokens] = tail


def gather_heads(place_ref, pieces, grads, heads):
    for flip, piece in enumerate(pieces):
        head = jnp.bitwise_xor(place_ref[0], flip) // (len(pieces) // heads)
        grads[pl.ds(pl.multiple_of(head * 3 * HD, 16), 3 * HD), :] = piece[...]


def project_back(here, place, whole, normed, back, pieces, rows, cols, heads):
    count = 2 * normed[0].shape[1]
    width = D // cols
    return pl.pallas_call(
        functools.partial(back_kernel, rows=rows, cols=cols, heads=heads),
        out_shape=jax.ShapeDtypeStruct((cols, width + 16, count), bf16),
        in_specs=[in_smem] * 2 + [in_vmem] * (4 + rows),
        out_specs=in_vmem,
        scratch_shapes=[pltpu.VMEM((3 * width, count), bf16)],
        compiler_params=pltpu.CompilerParams(vmem_limit_bytes=60 << 20),
        cost_estimate=pl.CostEstimate(
            flops=2 * D * 3 * width * count, bytes_accessed=16 << 20, transcendentals=0
        ),
    )(here, place, whole, *normed, back, *pieces)


def projection_grads_kernel(place_ref, whole_ref, *refs, order, heads):
    outs, (gain_ref, grads) = refs[-2 - (1 + max(out for out, _ in order)) : -2], refs[-2:]
    normed, pieces = refs[:2], refs[2 : -2 - len(outs)]
    half = normed[0].shape[1]
    gather_heads(place_ref, pieces, grads, heads)
    share = outs[0].shape[1]
    for slot, (out, at) in enumerate(order):
        row = jnp.bitwise_xor(place_ref[0], slot) if len(outs) > 1 else slot
        band = pl.ds(pl.multiple_of(row * share, 16), share)
        value = dot_last(normed[0][band, :], grads[:, :half]) + dot_last(
            normed[1][band, :], grads[:, half:]
        )
        gain_ref[band, :] = jnp.sum(value * whole_ref[band, :].astype(f32), axis=1, keepdims=True)
        outs[out][at] = value.astype(bf16)


def projection_grads(place, whole, normed, pieces, heads, shapes, order):
    half = normed[0].shape[1]
    return pl.pallas_call(
        functools.partial(projection_grads_kernel, order=order, heads=heads),
        out_shape=tuple(jax.ShapeDtypeStruct(shape, bf16) for shape in shapes)
        + (jax.ShapeDtypeStruct((D, 1), f32),),
        in_specs=[in_smem] + [in_vmem] * (3 + len(pieces)),
        out_specs=(in_vmem,) * (len(shapes) + 1),
        scratch_shapes=[pltpu.VMEM((whole.shape[1], 2 * half), bf16)],
        compiler_params=pltpu.CompilerParams(vmem_limit_bytes=60 << 20),
        cost_estimate=pl.CostEstimate(
            flops=4 * D * whole.shape[1] * half, bytes_accessed=12 << 20, transcendentals=0
        ),
    )(place, whole, *normed, *pieces)


def after(values, *others):
    return lax.optimization_barrier((values,) + others)[0]


def partner(values, flip, size, axis="row"):
    return lax.ppermute(values, axis, [(at, at ^ flip) for at in range(size)])


def plane(values, splits):
    result = [values[0]]
    for index in range(1, len(values)):
        flip, other = index // splits * 2, index % splits
        result.append(
            lax.ppermute(
                values[index],
                ("dp", "row"),
                [(at, at ^ (other * 4 + flip)) for at in range(splits * 4)],
            )
            if splits == 2
            else partner(values[index], flip, 4)
        )
    return result


def swapped(pieces, rows):
    return [pieces[0]] + [partner(pieces[flip], flip, rows) for flip in range(1, rows)]


def spread_rows(values, rows):
    if rows != 4:
        return swapped([values] * rows, rows)
    far = partner(values, 2, rows)
    return [values, partner(values, 1, rows), far, partner(far, 1, rows)]


def add(left, right):
    return left.astype(f32) + right.astype(f32)


def total(values, axes):
    for axis, size in axes:
        flip = 1
        while flip < size:
            values = values + partner(values, flip, size, axis)
            flip *= 2
    return values


def sum_groups(values, groups):
    if groups == 2:
        return add(values, partner(values, 1, 2, "dp"))
    return lax.psum(values, "dp").astype(f32)


def ring_swap(pieces, cols):
    return [pieces[0]] + [
        lax.ppermute(pieces[shift], "col", [(at, (at + shift) % cols) for at in range(cols)])
        for shift in range(1, cols)
    ]


def on_device(
    groups, rows, cols, residual_in, seq_ids, norm1_gain, w_qkv, per_dim, w_out, norm2_gain, w_up, w_down, out_grad
):
    count, width = residual_in.shape
    heads = width // HD
    twins = rows // heads
    sub = count // cols
    half = count // 2
    share = w_qkv.shape[0]
    tile = 768 if count % 768 == 0 else BLK
    back_tile = 512 if count % 512 == 0 else tile
    here = lax.axis_index("col")
    place = lax.axis_index("row")
    here_of, place_of = here[None].astype(jnp.int32), place[None].astype(jnp.int32)

    block_seq = seq_ids[::BLK]
    starts = jnp.sum((block_seq[None, :] < block_seq[:, None]).astype(jnp.int32), axis=1)

    residual = residual_in.T
    squares = jnp.sum(residual * residual, axis=0)
    squares = squares + partner(squares, 1, cols, "col")
    inverse_one = lax.rsqrt((squares + partner(squares, 2, cols, "col")) / D + epsilon)[None, :]
    normed = (residual * inverse_one * norm1_gain[:, None]).astype(bf16)
    qkv_local = w_qkv.astype(bf16).reshape(share, 3, heads, HD).transpose(0, 2, 1, 3)
    qkv_local = qkv_local.reshape(share, heads * 3 * HD)
    whole, turned = projection_copies(place_of, spread_rows(qkv_local, rows))
    scale = jax.nn.softplus(per_dim) * scale_base / math.sqrt(HD)
    factors = jnp.tile(jnp.concatenate([scale, jnp.ones((2 * HD,), f32)]), heads)[:, None]
    stacked = jnp.concatenate(
        [w_out.T, w_up, w_down.T], axis=1
    ).astype(bf16)
    gains = [jnp.concatenate(three_terms(gain))[None] for gain in (norm1_gain, norm2_gain)]
    splits = 2 if groups == 2 and rows == 4 else 1
    part = share // splits
    group_of = jnp.zeros((1,), jnp.int32)
    if splits == 2:
        group = lax.axis_index("dp")
        group_of = group[None].astype(jnp.int32)
        stacked = lax.dynamic_slice_in_dim(stacked, group * part, part, 0)
    stacked = jnp.concatenate([stacked] + gains + [jnp.zeros((14, 3 * width), bf16)], axis=0)
    gathered = jnp.stack(ring_swap([after(stacked, turned)] * cols, cols))
    gains = gathered[:, part : part + 2].astype(f32).reshape(cols, 2, 3, width).sum(axis=2)
    gains = jnp.concatenate(
        [
            lax.dynamic_index_in_dim(gains, lax.rem(here + cols - col, cols), 0, keepdims=False)
            for col in range(cols)
        ],
        axis=1,
    ).T
    near = [gathered]
    if rows == 4:
        if splits == 2:
            near.append(partner(gathered, 1, 2, "dp"))
        near.append(partner(gathered, 2, rows))
        if splits == 2:
            near.append(partner(after(near[2], near[1]), 1, 2, "dp"))

    out_grad_t = out_grad.T.astype(bf16)

    def quarter(values, shift):
        at = lax.rem(here + shift, cols) * sub
        return lax.dynamic_slice_in_dim(values, at, sub, 1)

    grad_pieces = [quarter(out_grad_t, shift) for shift in range(cols)]

    pieces, normed_parts = [], []
    for at in range(2):
        part = normed[:, at * half : (at + 1) * half]
        if at:
            part = after(part, turned, *grad_pieces)
        normed_parts.append(lax.all_gather(part, "col", axis=0, tiled=True))
        outs = project(place_of, turned, factors, normed_parts[at], rows, heads)
        pieces += swapped(outs, rows)

    tidy = sub % LANES == 0
    if rows == 4:
        pieces[0] = after(pieces[0], *near[1:3])
    result, lse, qkv_heads, leaving = attend(
        starts, place_of, pieces, rows, count, tile, sub if tidy else count
    )
    if rows == 4:
        near = [after(value, lse) for value in near]
        other = [partner(value, 1, rows) for value in near]
        blocks = near[:splits] + other[:splits] + near[splits:] + other[splits:]
    else:
        blocks = spread_rows(gathered, rows)
    weights = assemble(here_of, place_of, group_of, blocks, splits)
    grad_pieces = ring_swap(grad_pieces, cols)

    if not tidy:
        leaving = leaving.reshape(rows, HD, cols, sub).transpose(0, 2, 1, 3)
        leaving = leaving.reshape(rows * cols, HD, sub)
    leaving = after(leaving, *grad_pieces)
    arrived = lax.all_to_all(leaving, ("row", "col"), 0, 0, tiled=True)

    own_inverse = quarter(inverse_one, 0)
    own_at = lax.rem(here, cols // 2) * sub
    own_normed = jnp.where(
        here < cols // 2,
        lax.dynamic_slice_in_dim(normed_parts[0], own_at, sub, 1),
        lax.dynamic_slice_in_dim(normed_parts[1], own_at, sub, 1),
    )
    wide = (share, 3 * width)
    pairwise = ((0, 0), (1, 0), (0, 1), (1, 1))
    natural = tuple((0, row) for row in range(rows))
    order, slots = (pairwise, 2) if rows == 4 else (natural, rows)
    change, (back_two, gain_two_part, leaving, rhs), lhs = feed_forward(
        here_of,
        place_of,
        arrived,
        grad_pieces,
        own_normed,
        own_inverse,
        gains,
        weights,
        rows,
        cols,
        heads,
        twins,
        ((slots, 3, share, sub),) * (rows // slots),
        order,
    )

    go = lax.all_to_all(leaving, ("row", "col"), 0, 0, tiled=True)
    if not tidy:
        go = go.reshape(rows, cols, HD, sub).transpose(0, 2, 1, 3).reshape(rows, HD, count)

    if rows == 4:
        pairs = [lhs[0], rhs, partner(lhs[1], 1, rows), partner(rhs, 1, rows)]
        mine = weight_grads(here_of, group_of, pairs, cols, splits)
        go = after(go, *mine)
        mine = plane(mine, splits)
    else:
        mine = jnp.stack(weight_grads(here_of, group_of, [lhs[0], rhs], cols, 1))
        mine = lax.psum_scatter(mine, "row", scatter_dimension=0, tiled=False)

    pieces, dim_part = attend_back(
        starts, place_of, scale, qkv_heads, go, result, lse, back_tile, count
    )
    arrived = swapped(pieces, rows)

    if rows == 4:
        mine = sum(after(value, arrived[1]).astype(f32) for value in mine).astype(bf16)
    mine = ring_swap([mine[shift] for shift in range(cols)], cols)
    mine = sum(value.astype(f32) for value in mine).astype(bf16)
    if splits == 2:
        mine = jnp.stack([mine, partner(mine, 1, 2, "dp")])
        shard = jnp.where(group == 0, mine, mine[::-1]).reshape(wide).astype(f32)
    else:
        shard = sum_groups(mine, groups)

    change = ring_swap([after(piece, go) for piece in change], cols)
    arrived[0] = after(arrived[0], mine, *change)
    payload = project_back(
        here_of, place_of, whole, normed_parts, back_two, arrived, rows, cols, heads
    )
    summed = lax.psum_scatter(payload, "col", scatter_dimension=0, tiled=False).astype(f32)

    own_head = (place % twins == 0).astype(f32)
    *parts, gain_one_part = projection_grads(
        place_of,
        after(whole, payload),
        normed_parts,
        arrived,
        heads,
        ((slots,) + wide,) * (rows // slots),
        order,
    )
    small = jnp.concatenate([gain_one_part, gain_two_part, dim_part * own_head])[:, 0]
    if rows == 4:
        kept, sent = parts
        arrived = partner(sent, 1, rows)
        far = partner(add(kept[1], arrived[1]).astype(bf16), 2, rows)
        mine = (add(kept[0], arrived[0]) + far.astype(f32)).astype(bf16)
    else:
        mine = lax.psum_scatter(parts[0], "row", scatter_dimension=0, tiled=False)
    qkv_grad = sum_groups(mine, groups)
    qkv_grad = qkv_grad.reshape(share, heads, 3, HD).transpose(0, 2, 1, 3).reshape(share, 3, width)
    small = total(small, (("row", rows), ("dp", groups), ("col", cols)))
    gain_one_grad = lax.dynamic_slice_in_dim(small[:D], here * width, width) / norm1_gain
    gain_two_grad = lax.dynamic_slice_in_dim(small[D : 2 * D], here * width, width)
    scale_grad = small[2 * D :] / scale * (scale_base / math.sqrt(HD)) * jax.nn.sigmoid(per_dim)

    output = jnp.zeros_like(residual_in)
    for shift, piece in enumerate(change):
        at = lax.rem(here + cols - shift, cols) * sub
        piece = lax.dynamic_slice_in_dim(residual_in, at, sub, 0) + piece.astype(f32).T
        output = lax.dynamic_update_slice_in_dim(output, piece, at, 0)

    grad_one, along_one = summed[:width], summed[width : width + 1]
    back_one = inverse_one * norm1_gain[:, None] * grad_one - residual * inverse_one**2 * (
        along_one / D
    )
    input_grad = out_grad + back_one.T
    return (
        output,
        input_grad,
        gain_one_grad,
        qkv_grad,
        scale_grad,
        shard[:, :width].T,
        gain_two_grad,
        shard[:, width : 2 * width],
        shard[:, 2 * width :].T,
    )


def solution(mesh):
    in_specs = (
        P(("dp", "row"), "col"),
        P("dp"),
        P("col"),
        P("row", None, "col"),
        P(),
        P("col", "row"),
        P("col"),
        P("row", "col"),
        P("col", "row"),
        P(("dp", "row"), "col"),
    )
    out_specs = (
        P(("dp", "row"), "col"),
        P(("dp", "row"), "col"),
        P("col"),
        P("row", None, "col"),
        P(),
        P("col", "row"),
        P("col"),
        P("row", "col"),
        P("col", "row"),
    )
    return jax.shard_map(
        functools.partial(on_device, mesh.shape["dp"], mesh.shape["row"], mesh.shape["col"]),
        mesh=mesh,
        in_specs=in_specs,
        out_specs=out_specs,
        check_vma=False,
    )
```

```python
import functools
import math

import jax
import jax.numpy as jnp
from jax import lax
from jax.experimental import pallas as pl
from jax.experimental.pallas import tpu as pltpu
from jax.sharding import PartitionSpec as P

D = 1280
HD = 80
BLK = 256
LANES = 128

epsilon = 1e-06
scale_base = 1.442695041
excluded = -1e30

bf16 = jnp.bfloat16
f32 = jnp.float32


def dot(left, right):
    return jnp.dot(left, right, preferred_element_type=f32)


def product(form, left, right):
    return jnp.einsum(form, left, right, preferred_element_type=f32)


def three_terms(values):
    high = values.astype(bf16)
    rest = values - high.astype(f32)
    middle = rest.astype(bf16)
    return [high, middle, (rest - middle.astype(f32)).astype(bf16)]


def block_bias(starts_ref, first_block, width, block_count):
    shape = (block_count, width)
    block = lax.broadcasted_iota(jnp.int32, shape, 0)
    own = lax.broadcasted_iota(jnp.int32, shape, 1) // BLK
    start = jnp.zeros(shape, jnp.int32)
    for number in range(width // BLK):
        start = jnp.where(own == number, starts_ref[first_block + number], start)
    return jnp.where((block >= start) & (block <= first_block + own), 0.0, excluded).astype(bf16)


def extended(top, width, block_count, first_block, extra):
    row = lax.broadcasted_iota(jnp.int32, (LANES - HD, width), 0)
    block = first_block + lax.broadcasted_iota(jnp.int32, (LANES - HD, width), 1) // BLK
    marks = (row >= block_count) & (row < block_count + extra)
    if block_count:
        marks = marks | (row == block)
    return jnp.concatenate([top, jnp.where(marks, 1.0, 0.0).astype(bf16)], axis=0).T


def padded(parts, width):
    used = sum(part.shape[0] for part in parts)
    return jnp.concatenate(list(parts) + [jnp.zeros((LANES - used, width), bf16)], axis=0)


def store_pieces(ref, value, source, number, part):
    width, tile = ref.shape[2], value.shape[1]
    if width >= tile:
        ref[source * (part // width), :, pl.ds(pl.multiple_of(number * tile, tile), tile)] = value
        return
    first = source * (part // width) + number * (tile // width)
    for at in range(tile // width):
        ref[first + at] = value[:, at * width : (at + 1) * width]


def load_pieces(ref, source, number, part, tile):
    width = ref.shape[2]
    if width >= tile:
        return ref[source * (part // width), :, pl.ds(pl.multiple_of(number * tile, tile), tile)]
    grain = math.gcd(width, tile)
    chunks = []
    for at in range(tile // grain):
        start = number * tile + at * grain
        column = pl.multiple_of(lax.rem(start, width), grain)
        chunks.append(ref[source * (part // width) + start // width, :, pl.ds(column, grain)])
    return jnp.concatenate(chunks, axis=1)


def forward_kernel(starts_ref, place_ref, *refs, tokens, part, tile, rows):
    pieces = refs[: -5]
    out_ref, lse_ref, qkv_ref, leave_ref, key_scr = refs[-5:]
    half = pieces[0].shape[1]
    for number, piece in enumerate(pieces):
        flip, at = number % rows, number // rows
        qkv_ref[jnp.bitwise_xor(place_ref[0], flip), :, at * half : (at + 1) * half] = piece[...]
    block_count = tokens // BLK
    per_part = part // tile
    per_tile = tile // BLK
    for number in range(tokens // tile):
        source, at = divmod(number, per_part)
        key_scr[number * tile : (number + 1) * tile, :] = extended(
            qkv_ref[source, HD : 2 * HD, at * tile : (at + 1) * tile],
            tile,
            block_count,
            number * per_tile,
            0,
        )

    def query_tile(number, carried):
        source = number // per_part
        at = pl.multiple_of((number % per_part) * tile, tile)
        bias = block_bias(starts_ref, number * per_tile, tile, block_count)
        query = padded([qkv_ref[source, 0:HD, pl.ds(at, tile)], bias], tile)

        def key_tile(key_number, state):
            largest, result = state
            keys = key_scr[pl.ds(pl.multiple_of(key_number * tile, tile), tile), :]
            scores = dot(keys, query)
            key_at = pl.multiple_of((key_number % per_part) * tile, tile)
            values = qkv_ref[key_number // per_part, 2 * HD : 3 * HD, pl.ds(key_at, tile)]
            values = jnp.concatenate([values, jnp.ones((16, tile), bf16)], axis=0)
            newest = jnp.maximum(largest, jnp.max(scores, axis=0, keepdims=True))
            factor = jnp.exp(largest - newest)
            weights = jnp.exp(scores - newest)
            result = result * factor + dot(values, weights.astype(bf16))
            return newest, result

        largest, result = lax.fori_loop(
            starts_ref[number * per_tile] // per_tile,
            number + 1,
            key_tile,
            (jnp.full((1, tile), -jnp.inf, f32), jnp.zeros((HD + 16, tile), f32)),
        )
        total = result[HD : HD + 1]
        result = result[:HD] / total
        out_ref[source, :, pl.ds(at, tile)] = result
        store_pieces(leave_ref, result.astype(bf16), source, number % per_part, part)
        lse_ref[source, :, pl.ds(at, tile)] = largest + jnp.log(total)
        return carried

    lax.fori_loop(0, tokens // tile, query_tile, 0)


def backward_kernel(
    starts_ref,
    place_ref,
    scale_ref,
    qkv_ref,
    go_ref,
    out_ref,
    lse_ref,
    *refs,
    tokens,
    part,
    tile,
    rows,
):
    pieces = refs[: -6]
    dim_ref, grad_ref, key_scr, value_scr, key_grad, value_grad = refs[-6:]
    block_count = tokens // BLK
    per_part = part // tile
    per_tile = tile // BLK
    for number in range(tokens // tile):
        source, at = divmod(number, per_part)
        columns = slice(at * tile, (at + 1) * tile)
        band = slice(number * tile, (number + 1) * tile)
        key_scr[band, :] = extended(
            qkv_ref[source, HD : 2 * HD, columns], tile, block_count, number * per_tile, 3
        )
        value_scr[band, :] = extended(qkv_ref[source, 2 * HD : 3 * HD, columns], tile, 0, 0, 3)
    key_grad[...] = jnp.zeros_like(key_grad)
    value_grad[...] = jnp.zeros_like(value_grad)

    def query_tile(number, dim_total):
        source = number // per_part
        at = pl.multiple_of((number % per_part) * tile, tile)
        query_t = qkv_ref[source, 0:HD, pl.ds(at, tile)]
        go_t = load_pieces(go_ref, source, number % per_part, part, tile)
        delta = jnp.sum(
            go_t.astype(f32) * out_ref[source, :, pl.ds(at, tile)], axis=0, keepdims=True
        )
        lse = lse_ref[source, :, pl.ds(at, tile)]
        bias = block_bias(starts_ref, number * per_tile, tile, block_count)
        query_ext = padded([query_t, bias] + three_terms(-lse), tile)
        go_ext = padded([go_t] + three_terms(-delta), tile)
        query = padded([query_t], tile).T
        go = padded([go_t], tile).T

        def key_tile(key_number, total):
            band = pl.ds(pl.multiple_of(key_number * tile, tile), tile)
            key_at = pl.multiple_of((key_number % per_part) * tile, tile)
            keys_t = qkv_ref[key_number // per_part, HD : 2 * HD, pl.ds(key_at, tile)]
            weights = jnp.exp(dot(key_scr[band, :], query_ext))
            slopes = (weights * dot(value_scr[band, :], go_ext)).astype(bf16)
            value_grad[band, :] += dot(weights.astype(bf16), go)
            key_grad[band, :] += dot(slopes, query)
            return total + dot(keys_t, slopes)

        grad = lax.fori_loop(
            starts_ref[number * per_tile] // per_tile,
            number + 1,
            key_tile,
            jnp.zeros((HD, tile), f32),
        )
        grad_ref[source, 0:HD, pl.ds(at, tile)] = (grad * scale_ref[...]).astype(bf16)
        return dim_total + jnp.sum(grad * query_t.astype(f32), axis=1, keepdims=True)

    dim_ref[...] = lax.fori_loop(0, tokens // tile, query_tile, jnp.zeros((HD, 1), f32))
    for number in range(tokens // tile):
        source, at = divmod(number, per_part)
        columns = slice(at * tile, (at + 1) * tile)
        band = slice(number * tile, (number + 1) * tile)
        grad_ref[source, HD : 2 * HD, columns] = key_grad[band, :].T[:HD].astype(bf16)
        grad_ref[source, 2 * HD : 3 * HD, columns] = value_grad[band, :].T[:HD].astype(bf16)
    half = pieces[0].shape[1]
    for number, piece in enumerate(pieces):
        flip, at = number % rows, number // rows
        piece[...] = grad_ref[
            jnp.bitwise_xor(place_ref[0], flip), :, at * half : (at + 1) * half
        ]


in_vmem = pl.BlockSpec(memory_space=pltpu.VMEM)
in_smem = pl.BlockSpec(memory_space=pltpu.SMEM)


def attend(starts, place, pieces, rows, part, tile, width):
    tokens = rows * part
    return pl.pallas_call(
        functools.partial(forward_kernel, tokens=tokens, part=part, tile=tile, rows=rows),
        out_shape=(
            jax.ShapeDtypeStruct((rows, HD, part), f32),
            jax.ShapeDtypeStruct((rows, 1, part), f32),
            jax.ShapeDtypeStruct((rows, 3 * HD, part), bf16),
            jax.ShapeDtypeStruct((tokens // width, HD, width), bf16),
        ),
        in_specs=[in_smem] * 2 + [in_vmem] * len(pieces),
        out_specs=(in_vmem,) * 4,
        scratch_shapes=[pltpu.VMEM((tokens, LANES), bf16)],
        compiler_params=pltpu.CompilerParams(vmem_limit_bytes=60 << 20),
        cost_estimate=pl.CostEstimate(
            flops=3 * LANES * tokens * tokens,
            bytes_accessed=12 << 20,
            transcendentals=tokens * tokens // 3,
        ),
    )(starts, place, *pieces)


def attend_back(starts, place, scale, qkv, go, out, lse, tile, half):
    rows, _, part = qkv.shape
    tokens = rows * part
    count = rows * (part // half)
    results = pl.pallas_call(
        functools.partial(backward_kernel, tokens=tokens, part=part, tile=tile, rows=rows),
        out_shape=(jax.ShapeDtypeStruct((3 * HD, half), bf16),) * count
        + (jax.ShapeDtypeStruct((HD, 1), f32),),
        in_specs=[in_smem] * 2 + [in_vmem] * 5,
        out_specs=(in_vmem,) * (count + 1),
        scratch_shapes=[pltpu.VMEM((rows, 3 * HD, part), bf16)]
        + [pltpu.VMEM((tokens, LANES), bf16)] * 2
        + [pltpu.VMEM((tokens, LANES), f32)] * 2,
        compiler_params=pltpu.CompilerParams(vmem_limit_bytes=60 << 20),
        cost_estimate=pl.CostEstimate(
            flops=8 * LANES * tokens * tokens,
            bytes_accessed=16 << 20,
            transcendentals=tokens * tokens // 3,
        ),
    )(starts, place, scale.reshape(HD, 1), qkv, go, out, lse)
    return results[:-1], results[-1]


def assemble_kernel(here_ref, place_ref, group_ref, *refs, cols, splits):
    blocks, out_ref = refs[:-1], refs[-1]
    part = out_ref.shape[1] // len(blocks)
    width = out_ref.shape[2] // cols
    for number, block in enumerate(blocks):
        row = jnp.bitwise_xor(place_ref[0], number // splits)
        piece = jnp.bitwise_xor(group_ref[0], number % splits)
        band = pl.ds(pl.multiple_of((row * splits + piece) * part, 16), part)
        for col in range(cols):
            value = block[lax.rem(here_ref[0] + cols - col, cols), 0:part, :]
            for matrix in range(3):
                out_ref[matrix, band, col * width : (col + 1) * width] = value[
                    :, matrix * width : (matrix + 1) * width
                ]


def unrolled(count, body, value):
    for number in range(count):
        value = body(number, value)
    return value


def feed_kernel(
    here_ref,
    place_ref,
    att_ref,
    normed_ref,
    inverse_ref,
    gains_ref,
    w_hbm,
    *refs,
    rows,
    cols,
    heads,
    twins,
    order,
):
    go_pieces, change_pieces = refs[:cols], refs[cols : 2 * cols]
    back_ref, gain_ref, leave_ref, rhs_ref = refs[2 * cols : 2 * cols + 4]
    lhs_refs = refs[2 * cols + 4 : -12]
    (
        w_ref,
        attended,
        normed_two,
        branch_grad,
        go_ref,
        branch,
        middle,
        grad_two,
        flipped,
        flipped_go,
        grad_att,
        done,
    ) = refs[-12:]
    width, sub = go_pieces[0].shape
    copies = [
        pltpu.make_async_copy(w_hbm.at[number], w_ref.at[number], done.at[number])
        for number in range(3)
    ]
    for copy in copies:
        copy.start()

    def ring(shift):
        return pl.ds(pl.multiple_of(lax.rem(here_ref[0] + shift, cols) * width, 16), width)

    for number, piece in enumerate(go_pieces):
        go_ref[ring(cols - number), :] = piece[...]
    step = 256
    for col in range(cols):
        for head in range(heads):
            at = (col * heads + head) * HD
            attended[at : at + HD, :] = att_ref[head * twins * cols + col]
    inverse = inverse_ref[...]
    copies[0].wait()

    def part(number):
        return pl.ds(number * step, step)

    def first(number, total):
        at = part(number)
        here = dot(w_ref[0, at, :], attended[...])
        branch[at, :] = here
        mid = normed_ref[at, :].astype(f32) / (inverse * gains_ref[at, 0:1]) + here
        middle[at, :] = mid
        flipped_go[:, at] = go_ref[at, :].T
        rhs_ref[0, :, at] = attended[at, :].T
        return total + jnp.sum(mid * mid, axis=0, keepdims=True)

    steps = D // step
    total = unrolled(steps, first, jnp.zeros((1, sub), f32))
    inverse_two = lax.rsqrt(total / D + epsilon)
    copies[1].wait()
    copies[2].wait()

    def second(number, carried):
        at = part(number)
        value = (middle[at, :] * inverse_two * gains_ref[at, 1:2]).astype(bf16)
        normed_two[at, :] = value
        flipped[:, at] = value.T
        return carried

    unrolled(steps, second, 0)

    def third(number, carried):
        at = part(number)
        up_proj = dot(flipped[...], w_ref[1, :, at])
        sigmoid_up = jax.nn.sigmoid(up_proj)
        rhs_ref[2, :, at] = (up_proj * sigmoid_up).astype(bf16)
        grad_act = dot(flipped_go[...], w_ref[2, :, at])
        rhs_ref[1, :, at] = (
            grad_act * sigmoid_up * (1.0 + up_proj * (1.0 - sigmoid_up))
        ).astype(bf16)
        return carried

    unrolled(steps, third, 0)

    def fourth(number, along):
        at = part(number)
        branch[at, :] += dot_last(w_ref[2, at, :], rhs_ref[2])
        grad = dot_last(w_ref[1, at, :], rhs_ref[1])
        grad_two[at, :] = grad
        return along + jnp.sum(gains_ref[at, 1:2] * grad * middle[at, :], axis=0, keepdims=True)

    along = unrolled(steps, fourth, jnp.zeros((1, sub), f32))
    shrink = inverse_two * inverse_two * inverse_two * along / D

    def fifth(number, carried):
        at = part(number)
        grad = grad_two[at, :]
        mid = middle[at, :]
        back = inverse_two * gains_ref[at, 1:2] * grad - mid * shrink
        back_ref[at, :] = (back / (inverse * gains_ref[at, 0:1])).astype(bf16)
        gain_ref[at, :] = jnp.sum(grad * mid * inverse_two, axis=1, keepdims=True)
        value = (go_ref[at, :].astype(f32) + back).astype(bf16)
        branch_grad[at, :] = value
        flipped[:, at] = value.T
        return carried

    unrolled(steps, fifth, 0)

    def sixth(number, carried):
        at = part(number)
        grad_att[at, :] = dot(flipped[...], w_ref[0, :, at]).T.astype(bf16)
        return carried

    unrolled(steps, sixth, 0)
    for number, piece in enumerate(change_pieces):
        piece[...] = branch[ring(number), :].astype(bf16)
    share = D // rows
    for slot, (out, at) in enumerate(order):
        row = jnp.bitwise_xor(place_ref[0], slot) if len(lhs_refs) > 1 else slot
        band = pl.ds(pl.multiple_of(row * share, 16), share)
        for number, value in enumerate((branch_grad, normed_two, go_ref)):
            lhs_refs[out][at, number] = value[band, :]
    for row in range(rows):
        for col in range(cols):
            at = (col * heads + row // twins) * HD
            leave_ref[row * cols + col] = grad_att[at : at + HD, :]


def dot_last(left, right):
    return lax.dot_general(left, right, (((1,), (1,)), ((), ())), preferred_element_type=f32)


def weights_kernel(here_ref, group_ref, *refs, count, splits):
    operands, outs = refs[:count], refs[count:]
    cols, part, wide = outs[0].shape
    width = wide // 3
    for index, out in enumerate(outs):
        slot = index // splits
        piece = jnp.bitwise_xor(group_ref[0], index % splits)
        band = pl.ds(pl.multiple_of(piece * part, 16), part)
        for number in range(3):
            value = sum(
                dot(operands[at][slot, number, band, :], operands[at + 1][number])
                for at in range(0, count, 2)
            ).astype(bf16)
            for col in range(cols):
                place = lax.rem(col + cols - here_ref[0], cols)
                out[place, :, number * width : (number + 1) * width] = value[
                    :, col * width : (col + 1) * width
                ]


def assemble(here, place, group, blocks, splits):
    cols = blocks[0].shape[0]
    return pl.pallas_call(
        functools.partial(assemble_kernel, cols=cols, splits=splits),
        out_shape=jax.ShapeDtypeStruct((3, D, D), bf16),
        in_specs=[in_smem] * 3 + [in_vmem] * len(blocks),
        out_specs=in_vmem,
        compiler_params=pltpu.CompilerParams(vmem_limit_bytes=60 << 20),
        cost_estimate=pl.CostEstimate(flops=0, bytes_accessed=20 << 20, transcendentals=0),
    )(here, place, group, *blocks)


def feed_forward(
    here, place, attended, pieces, normed, inverse, gains, weights, rows, cols, heads, twins, shapes, order
):
    width, sub = pieces[0].shape
    results = pl.pallas_call(
        functools.partial(
            feed_kernel, rows=rows, cols=cols, heads=heads, twins=twins, order=order
        ),
        out_shape=(jax.ShapeDtypeStruct((width, sub), bf16),) * cols
        + (
            jax.ShapeDtypeStruct((D, sub), bf16),
            jax.ShapeDtypeStruct((D, 1), f32),
            jax.ShapeDtypeStruct((rows * cols, HD, sub), bf16),
            jax.ShapeDtypeStruct((3, sub, D), bf16),
        )
        + tuple(jax.ShapeDtypeStruct(shape, bf16) for shape in shapes),
        in_specs=[in_smem] * 2
        + [in_vmem] * 4
        + [pl.BlockSpec(memory_space=pl.ANY)]
        + [in_vmem] * cols,
        out_specs=(in_vmem,) * (cols + 4 + len(shapes)),
        scratch_shapes=[pltpu.VMEM((3, D, D), bf16)]
        + [pltpu.VMEM((D, sub), bf16)] * 4
        + [pltpu.VMEM((D, sub), f32)] * 3
        + [pltpu.VMEM((sub, D), bf16)] * 2
        + [pltpu.VMEM((D, sub), bf16), pltpu.SemaphoreType.DMA((3,))],
        compiler_params=pltpu.CompilerParams(vmem_limit_bytes=60 << 20),
        cost_estimate=pl.CostEstimate(
            flops=12 * D * D * sub, bytes_accessed=20 << 20, transcendentals=D * sub
        ),
    )(here, place, attended, normed, inverse, gains, weights, *pieces)
    return results[:cols], results[cols : cols + 4], results[cols + 4 :]


def weight_grads(here, group, pairs, cols, splits):
    slots, _, share, sub = pairs[0].shape
    count = slots * splits
    return pl.pallas_call(
        functools.partial(weights_kernel, count=len(pairs), splits=splits),
        out_shape=(jax.ShapeDtypeStruct((cols, share // splits, 3 * D // cols), bf16),) * count,
        in_specs=[in_smem] * 2 + [in_vmem] * len(pairs),
        out_specs=(in_vmem,) * count,
        compiler_params=pltpu.CompilerParams(vmem_limit_bytes=60 << 20),
        cost_estimate=pl.CostEstimate(
            flops=6 * D * D * sub, bytes_accessed=16 << 20, transcendentals=0
        ),
    )(here, group, *pairs)


def copies_kernel(place_ref, *refs):
    blocks, (whole, turned) = refs[:-2], refs[-2:]
    share = blocks[0].shape[0]
    for flip, block in enumerate(blocks):
        row = jnp.bitwise_xor(place_ref[0], flip)
        whole[pl.ds(pl.multiple_of(row * share, 16), share), :] = block[...]
    for number in range(D // LANES):
        at = slice(number * LANES, (number + 1) * LANES)
        turned[:, at] = whole[at, :].T


def projection_copies(place, blocks):
    share, wide = blocks[0].shape
    return pl.pallas_call(
        copies_kernel,
        out_shape=(
            jax.ShapeDtypeStruct((D, wide), bf16),
            jax.ShapeDtypeStruct((wide, D), bf16),
        ),
        in_specs=[in_smem] + [in_vmem] * len(blocks),
        out_specs=(in_vmem,) * 2,
        compiler_params=pltpu.CompilerParams(vmem_limit_bytes=60 << 20),
        cost_estimate=pl.CostEstimate(flops=0, bytes_accessed=8 << 20, transcendentals=0),
    )(place, *blocks)


def project_kernel(place_ref, turned_ref, factor_ref, normed_ref, *refs, rows, heads):
    outs, result = refs[:-1], refs[-1]
    for head in range(heads):
        at = slice(head * 3 * HD, (head + 1) * 3 * HD)
        value = dot(turned_ref[at, :], normed_ref[...]) * factor_ref[at, :]
        result[head] = value.astype(bf16)
    for flip, out in enumerate(outs):
        out[...] = result[jnp.bitwise_xor(place_ref[0], flip) // (rows // heads)]


def project(place, turned, factors, normed, rows, heads):
    half = normed.shape[1]
    return pl.pallas_call(
        functools.partial(project_kernel, rows=rows, heads=heads),
        out_shape=(jax.ShapeDtypeStruct((3 * HD, half), bf16),) * rows,
        in_specs=[in_smem] + [in_vmem] * 3,
        out_specs=(in_vmem,) * rows,
        scratch_shapes=[pltpu.VMEM((heads, 3 * HD, half), bf16)],
        compiler_params=pltpu.CompilerParams(vmem_limit_bytes=60 << 20),
        cost_estimate=pl.CostEstimate(
            flops=2 * D * turned.shape[0] * half, bytes_accessed=10 << 20, transcendentals=0
        ),
    )(place, turned, factors, normed)


def back_kernel(here_ref, place_ref, whole_ref, *refs, rows, cols, heads):
    normed, back_ref, pieces, (payload, grads) = refs[:2], refs[2], refs[3:-2], refs[-2:]
    half = normed[0].shape[1]
    width = D // cols
    sub = back_ref.shape[1]
    here = here_ref[0]
    gather_heads(place_ref, pieces, grads, heads)
    for number in range(2):
        along = jnp.zeros((1, half), f32)
        tokens = slice(number * half, (number + 1) * half)
        for col in range(cols):
            at = slice(col * width, (col + 1) * width)
            value = dot(whole_ref[at, :], grads[:, tokens])
            along += jnp.sum(value * normed[number][at, :].astype(f32), axis=0, keepdims=True)
            for quarter in range(half // sub):
                columns = slice(quarter * sub, (quarter + 1) * sub)
                into = slice(number * half + quarter * sub, number * half + (quarter + 1) * sub)
                mine = jnp.where(here == number * (half // sub) + quarter, 1.0, 0.0)
                payload[col, 0:width, into] = (
                    value[:, columns] + back_ref[at, :].astype(f32) * mine
                ).astype(bf16)
        tail = jnp.concatenate([along, jnp.zeros((15, half), f32)], axis=0).astype(bf16)
        for col in range(cols):
            payload[col, width : width + 16, tokens] = tail


def gather_heads(place_ref, pieces, grads, heads):
    for flip, piece in enumerate(pieces):
        head = jnp.bitwise_xor(place_ref[0], flip) // (len(pieces) // heads)
        grads[pl.ds(pl.multiple_of(head * 3 * HD, 16), 3 * HD), :] = piece[...]


def project_back(here, place, whole, normed, back, pieces, rows, cols, heads):
    count = 2 * normed[0].shape[1]
    width = D // cols
    return pl.pallas_call(
        functools.partial(back_kernel, rows=rows, cols=cols, heads=heads),
        out_shape=jax.ShapeDtypeStruct((cols, width + 16, count), bf16),
        in_specs=[in_smem] * 2 + [in_vmem] * (4 + rows),
        out_specs=in_vmem,
        scratch_shapes=[pltpu.VMEM((3 * width, count), bf16)],
        compiler_params=pltpu.CompilerParams(vmem_limit_bytes=60 << 20),
        cost_estimate=pl.CostEstimate(
            flops=2 * D * 3 * width * count, bytes_accessed=16 << 20, transcendentals=0
        ),
    )(here, place, whole, *normed, back, *pieces)


def projection_grads_kernel(place_ref, whole_ref, *refs, order, heads):
    outs, (gain_ref, grads) = refs[-2 - (1 + max(out for out, _ in order)) : -2], refs[-2:]
    normed, pieces = refs[:2], refs[2 : -2 - len(outs)]
    half = normed[0].shape[1]
    gather_heads(place_ref, pieces, grads, heads)
    share = outs[0].shape[1]
    for slot, (out, at) in enumerate(order):
        row = jnp.bitwise_xor(place_ref[0], slot) if len(outs) > 1 else slot
        band = pl.ds(pl.multiple_of(row * share, 16), share)
        value = dot_last(normed[0][band, :], grads[:, :half]) + dot_last(
            normed[1][band, :], grads[:, half:]
        )
        gain_ref[band, :] = jnp.sum(value * whole_ref[band, :].astype(f32), axis=1, keepdims=True)
        outs[out][at] = value.astype(bf16)


def projection_grads(place, whole, normed, pieces, heads, shapes, order):
    half = normed[0].shape[1]
    return pl.pallas_call(
        functools.partial(projection_grads_kernel, order=order, heads=heads),
        out_shape=tuple(jax.ShapeDtypeStruct(shape, bf16) for shape in shapes)
        + (jax.ShapeDtypeStruct((D, 1), f32),),
        in_specs=[in_smem] + [in_vmem] * (3 + len(pieces)),
        out_specs=(in_vmem,) * (len(shapes) + 1),
        scratch_shapes=[pltpu.VMEM((whole.shape[1], 2 * half), bf16)],
        compiler_params=pltpu.CompilerParams(vmem_limit_bytes=60 << 20),
        cost_estimate=pl.CostEstimate(
            flops=4 * D * whole.shape[1] * half, bytes_accessed=12 << 20, transcendentals=0
        ),
    )(place, whole, *normed, *pieces)


def after(values, *others):
    return lax.optimization_barrier((values,) + others)[0]


def partner(values, flip, size, axis="row"):
    return lax.ppermute(values, axis, [(at, at ^ flip) for at in range(size)])


def plane(values, splits):
    result = [values[0]]
    for index in range(1, len(values)):
        flip, other = index // splits * 2, index % splits
        result.append(
            lax.ppermute(
                values[index],
                ("dp", "row"),
                [(at, at ^ (other * 4 + flip)) for at in range(splits * 4)],
            )
            if splits == 2
            else partner(values[index], flip, 4)
        )
    return result


def swapped(pieces, rows):
    return [pieces[0]] + [partner(pieces[flip], flip, rows) for flip in range(1, rows)]


def spread_rows(values, rows):
    if rows != 4:
        return swapped([values] * rows, rows)
    far = partner(values, 2, rows)
    return [values, partner(values, 1, rows), far, partner(far, 1, rows)]


def add(left, right):
    return left.astype(f32) + right.astype(f32)


def total(values, axes):
    for axis, size in axes:
        flip = 1
        while flip < size:
            values = values + partner(values, flip, size, axis)
            flip *= 2
    return values


def sum_groups(values, groups):
    if groups == 2:
        return add(values, partner(values, 1, 2, "dp"))
    return lax.psum(values, "dp").astype(f32)


def ring_swap(pieces, cols):
    return [pieces[0]] + [
        lax.ppermute(pieces[shift], "col", [(at, (at + shift) % cols) for at in range(cols)])
        for shift in range(1, cols)
    ]


def on_device(
    groups, rows, cols, residual_in, seq_ids, norm1_gain, w_qkv, per_dim, w_out, norm2_gain, w_up, w_down, out_grad
):
    count, width = residual_in.shape
    heads = width // HD
    twins = rows // heads
    sub = count // cols
    half = count // 2
    share = w_qkv.shape[0]
    tile = 768 if count % 768 == 0 else BLK
    back_tile = 512 if count % 512 == 0 else tile
    here = lax.axis_index("col")
    place = lax.axis_index("row")
    here_of, place_of = here[None].astype(jnp.int32), place[None].astype(jnp.int32)

    block_seq = seq_ids[::BLK]
    starts = jnp.sum((block_seq[None, :] < block_seq[:, None]).astype(jnp.int32), axis=1)

    residual = residual_in.T
    squares = jnp.sum(residual * residual, axis=0)
    squares = squares + partner(squares, 1, cols, "col")
    inverse_one = lax.rsqrt((squares + partner(squares, 2, cols, "col")) / D + epsilon)[None, :]
    normed = (residual * inverse_one * norm1_gain[:, None]).astype(bf16)
    qkv_local = w_qkv.astype(bf16).reshape(share, 3, heads, HD).transpose(0, 2, 1, 3)
    qkv_local = qkv_local.reshape(share, heads * 3 * HD)
    whole, turned = projection_copies(place_of, spread_rows(qkv_local, rows))
    scale = jax.nn.softplus(per_dim) * scale_base / math.sqrt(HD)
    factors = jnp.tile(jnp.concatenate([scale, jnp.ones((2 * HD,), f32)]), heads)[:, None]
    stacked = jnp.concatenate(
        [w_out.T, w_up, w_down.T], axis=1
    ).astype(bf16)
    gains = [jnp.concatenate(three_terms(gain))[None] for gain in (norm1_gain, norm2_gain)]
    splits = 2 if groups == 2 and rows == 4 else 1
    part = share // splits
    group_of = jnp.zeros((1,), jnp.int32)
    if splits == 2:
        group = lax.axis_index("dp")
        group_of = group[None].astype(jnp.int32)
        stacked = lax.dynamic_slice_in_dim(stacked, group * part, part, 0)
    stacked = jnp.concatenate([stacked] + gains + [jnp.zeros((14, 3 * width), bf16)], axis=0)
    gathered = jnp.stack(ring_swap([after(stacked, turned)] * cols, cols))
    gains = gathered[:, part : part + 2].astype(f32).reshape(cols, 2, 3, width).sum(axis=2)
    gains = jnp.concatenate(
        [
            lax.dynamic_index_in_dim(gains, lax.rem(here + cols - col, cols), 0, keepdims=False)
            for col in range(cols)
        ],
        axis=1,
    ).T
    near = [gathered]
    if rows == 4:
        if splits == 2:
            near.append(partner(gathered, 1, 2, "dp"))
        near.append(partner(gathered, 2, rows))
        if splits == 2:
            near.append(partner(after(near[2], near[1]), 1, 2, "dp"))

    out_grad_t = out_grad.T.astype(bf16)

    def quarter(values, shift):
        at = lax.rem(here + shift, cols) * sub
        return lax.dynamic_slice_in_dim(values, at, sub, 1)

    grad_pieces = [quarter(out_grad_t, shift) for shift in range(cols)]

    pieces, normed_parts = [], []
    for at in range(2):
        part = normed[:, at * half : (at + 1) * half]
        if at:
            part = after(part, turned, *grad_pieces)
        normed_parts.append(lax.all_gather(part, "col", axis=0, tiled=True))
        outs = project(place_of, turned, factors, normed_parts[at], rows, heads)
        pieces += swapped(outs, rows)

    tidy = sub % LANES == 0
    if rows == 4:
        pieces[0] = after(pieces[0], *near[1:3])
    result, lse, qkv_heads, leaving = attend(
        starts, place_of, pieces, rows, count, tile, sub if tidy else count
    )
    if rows == 4:
        near = [after(value, lse) for value in near]
        other = [partner(value, 1, rows) for value in near]
        blocks = near[:splits] + other[:splits] + near[splits:] + other[splits:]
    else:
        blocks = spread_rows(gathered, rows)
    weights = assemble(here_of, place_of, group_of, blocks, splits)
    grad_pieces = ring_swap(grad_pieces, cols)

    if not tidy:
        leaving = leaving.reshape(rows, HD, cols, sub).transpose(0, 2, 1, 3)
        leaving = leaving.reshape(rows * cols, HD, sub)
    leaving = after(leaving, *grad_pieces)
    arrived = lax.all_to_all(leaving, ("row", "col"), 0, 0, tiled=True)

    own_inverse = quarter(inverse_one, 0)
    own_at = lax.rem(here, cols // 2) * sub
    own_normed = jnp.where(
        here < cols // 2,
        lax.dynamic_slice_in_dim(normed_parts[0], own_at, sub, 1),
        lax.dynamic_slice_in_dim(normed_parts[1], own_at, sub, 1),
    )
    wide = (share, 3 * width)
    pairwise = ((0, 0), (1, 0), (0, 1), (1, 1))
    natural = tuple((0, row) for row in range(rows))
    order, slots = (pairwise, 2) if rows == 4 else (natural, rows)
    change, (back_two, gain_two_part, leaving, rhs), lhs = feed_forward(
        here_of,
        place_of,
        arrived,
        grad_pieces,
        own_normed,
        own_inverse,
        gains,
        weights,
        rows,
        cols,
        heads,
        twins,
        ((slots, 3, share, sub),) * (rows // slots),
        order,
    )

    go = lax.all_to_all(leaving, ("row", "col"), 0, 0, tiled=True)
    if not tidy:
        go = go.reshape(rows, cols, HD, sub).transpose(0, 2, 1, 3).reshape(rows, HD, count)

    if rows == 4:
        pairs = [lhs[0], rhs, partner(lhs[1], 1, rows), partner(rhs, 1, rows)]
        mine = weight_grads(here_of, group_of, pairs, cols, splits)
        go = after(go, *mine)
        mine = plane(mine, splits)
    else:
        mine = jnp.stack(weight_grads(here_of, group_of, [lhs[0], rhs], cols, 1))
        mine = lax.psum_scatter(mine, "row", scatter_dimension=0, tiled=False)

    pieces, dim_part = attend_back(
        starts, place_of, scale, qkv_heads, go, result, lse, back_tile, count
    )
    arrived = swapped(pieces, rows)

    if rows == 4:
        mine = sum(after(value, arrived[1]).astype(f32) for value in mine).astype(bf16)
    mine = ring_swap([mine[shift] for shift in range(cols)], cols)
    mine = sum(value.astype(f32) for value in mine).astype(bf16)
    if splits == 2:
        mine = jnp.stack([mine, partner(mine, 1, 2, "dp")])
        shard = jnp.where(group == 0, mine, mine[::-1]).reshape(wide).astype(f32)
    else:
        shard = sum_groups(mine, groups)

    change = ring_swap([after(piece, go) for piece in change], cols)
    arrived[0] = after(arrived[0], mine, *change)
    payload = project_back(
        here_of, place_of, whole, normed_parts, back_two, arrived, rows, cols, heads
    )
    summed = lax.psum_scatter(payload, "col", scatter_dimension=0, tiled=False).astype(f32)

    own_head = (place % twins == 0).astype(f32)
    *parts, gain_one_part = projection_grads(
        place_of,
        after(whole, payload),
        normed_parts,
        arrived,
        heads,
        ((slots,) + wide,) * (rows // slots),
        order,
    )
    small = jnp.concatenate([gain_one_part, gain_two_part, dim_part * own_head])[:, 0]
    if rows == 4:
        kept, sent = parts
        arrived = partner(sent, 1, rows)
        far = partner(add(kept[1], arrived[1]).astype(bf16), 2, rows)
        mine = (add(kept[0], arrived[0]) + far.astype(f32)).astype(bf16)
    else:
        mine = lax.psum_scatter(parts[0], "row", scatter_dimension=0, tiled=False)
    qkv_grad = sum_groups(mine, groups)
    qkv_grad = qkv_grad.reshape(share, heads, 3, HD).transpose(0, 2, 1, 3).reshape(share, 3, width)
    small = total(small, (("row", rows), ("dp", groups), ("col", cols)))
    gain_one_grad = lax.dynamic_slice_in_dim(small[:D], here * width, width) / norm1_gain
    gain_two_grad = lax.dynamic_slice_in_dim(small[D : 2 * D], here * width, width)
    scale_grad = small[2 * D :] / scale * (scale_base / math.sqrt(HD)) * jax.nn.sigmoid(per_dim)

    output = jnp.zeros_like(residual_in)
    for shift, piece in enumerate(change):
        at = lax.rem(here + cols - shift, cols) * sub
        piece = lax.dynamic_slice_in_dim(residual_in, at, sub, 0) + piece.astype(f32).T
        output = lax.dynamic_update_slice_in_dim(output, piece, at, 0)

    grad_one, along_one = summed[:width], summed[width : width + 1]
    back_one = inverse_one * norm1_gain[:, None] * grad_one - residual * inverse_one**2 * (
        along_one / D
    )
    input_grad = out_grad + back_one.T
    return (
        output,
        input_grad,
        gain_one_grad,
        qkv_grad,
        scale_grad,
        shard[:, :width].T,
        gain_two_grad,
        shard[:, width : 2 * width],
        shard[:, 2 * width :].T,
    )


def solution(mesh):
    in_specs = (
        P(("dp", "row"), "col"),
        P("dp"),
        P("col"),
        P("row", None, "col"),
        P(),
        P("col", "row"),
        P("col"),
        P("row", "col"),
        P("col", "row"),
        P(("dp", "row"), "col"),
    )
    out_specs = (
        P(("dp", "row"), "col"),
        P(("dp", "row"), "col"),
        P("col"),
        P("row", None, "col"),
        P(),
        P("col", "row"),
        P("col"),
        P("row", "col"),
        P("col", "row"),
    )
    return jax.shard_map(
        functools.partial(on_device, mesh.shape["dp"], mesh.shape["row"], mesh.shape["col"]),
        mesh=mesh,
        in_specs=in_specs,
        out_specs=out_specs,
        check_vma=False,
    )
```
